256 devices in a mesh: segment: 32 (over y_hi, z, core), tensor: 8 (over x, y_lo).
Axes of the slice: x: 4, y: 4 (y_hi: 2, y_lo: 2; y = y_hi * 2 + y_lo), z: 8, core: 2. Of those that a mesh axis runs over, the one named last changes fastest.
Arguments:
- teacher_slabs: bfloat16 [96, 128, 16384], P('segment', None, 'tensor'), may hold values from -6 to 6
- proj_weight: bfloat16 [8, 2048, 8192], P(None, 'segment', 'tensor'), may hold values from -0.046875 to 0.046875
- child_hidden: bfloat16 [96, 128, 8192], P('segment', None, 'tensor'), may hold values from -6 to 6
- norm_gain: float32 [32, 8192], P('segment', 'tensor'), may hold values from 0.5 to 1.5
- key_weight: bfloat16 [32, 8192, 1024], P('segment', 'tensor'), may hold values from -0.0625 to 0.0625
- value_weight: bfloat16 [32, 8192, 1024], P('segment', 'tensor'), may hold values from -0.0625 to 0.0625
- key_cotangent: bfloat16 [32, 128, 1024], P('segment'), may hold values from -3 to 3
- value_cotangent: bfloat16 [32, 128, 1024], P('segment'), may hold values from -3 to 3
- layer_map: int32 [32], replicated, may hold values from 0 to 47, as said below
- layer_counts: int32 [16], replicated, may hold values from 1 to 3, 32 in all
Outputs:
- hidden_grad: bfloat16 [96, 128, 8192], P('segment', None, 'tensor')
- key_weight_grad: bfloat16 [32, 8192, 1024], P('segment', 'tensor')
- value_weight_grad: bfloat16 [32, 8192, 1024], P('segment', 'tensor')
- gain_grad: float32 [32, 8192], P('segment', 'tensor')
The draws below stay inside these ranges and needn't reach their ends.
Inputs may be any that keep to these rules, and one draw needn't show every extreme that they name: `layer_map`: strictly increasing. Teacher layer g is held by segment g // 3 in its slot g % 3. Child segment 16 + i owns layer_counts[i] consecutive child layers, in order; they sum to 32, and some segment owns 3.
All inputs are finite; a program needn't handle non-finite values.
Results may differ from the reference program's by a relative error of at most 0.023.
Values may be sent and summed in bfloat16 or wider, within the bound.
No kernel may reach another device: no remote copies, remote signals or barrier semaphores. Data moves between devices by JAX's collectives and lax.ppermute only.
A program may use at most 128 MiB of HBM per device.

```python
import math
import jax
import jax.numpy as jnp
import numpy as np
from jax import lax

D = 8192
DT = 16384
TOK = 128
TL_DEV = 3
MOST = 3
KV = 1024
N_HALF = 16
LAYERS = 32
TEACHER_LAYERS = 48
N_SEGMENT = 32
N_TENSOR = 8


def draw_layer_map(key, part):
    key = jax.random.fold_in(key, 7)
    order = jax.random.permutation(key, TEACHER_LAYERS)
    chosen = order[:LAYERS]
    return jnp.sort(chosen).astype(jnp.int32)


def shard_levels(key, dims, split, smallest, high):
    gain, own = 1.0, jax.random.fold_in(key, 6)
    for dim, shards_of in split:
        steps = jnp.exp(jax.random.uniform(jax.random.fold_in(own, dim), (shards_of,), jnp.float32, smallest / len(split), high / len(split)))
        gain = gain * jnp.repeat(steps, dims[dim] // shards_of).reshape([-1 if axis == dim else 1 for axis in range(len(dims))])
    return gain


def length_profile(number_of, total, most, slope):
    loads = [(1 << 20) // math.isqrt(grade ** slope) + 1 for grade in range(2, number_of + 1)]
    surplus, counts = total - most - (number_of - 1), [1] * (number_of - 1)
    while surplus > 0:
        candidates = [i for i in range(number_of - 1) if counts[i] < most]
        mass, budget = sum([loads[i] for i in candidates]), surplus
        for i in candidates:
            more = min(most - counts[i], max(1, budget * loads[i] // mass), surplus)
            counts[i] = counts[i] + more
            surplus = surplus - more
    return np.array([most] + counts)


def ragged(rng, amount, total, most, lean):
    if amount == 2:
        one = jax.random.randint(rng, (), max(1, total - most), min(most, total - 1) + 1)
        return jnp.stack([one, total - one])
    lengths = jnp.asarray(length_profile(amount, total, most, lean), jnp.int32)
    twos = (amount - 1) // 2
    giver, taker = lengths[1:1 + 2 * twos:2], lengths[2:2 + 2 * twos:2]
    room = jnp.minimum(giver - 1, most - taker)
    moved = jax.random.randint(jax.random.fold_in(rng, 1), (twos,), 0, 1 << 20) % (room + 1)
    lengths = lengths.at[1:1 + 2 * twos:2].set(giver - moved).at[2:2 + 2 * twos:2].set(taker + moved)
    return lengths[jax.random.permutation(jax.random.fold_in(rng, 2), amount)]


def bell_draw(key, dims, deviation, reach, shards=(), held_as=jnp.bfloat16):
    drawn = deviation * jax.random.normal(key, dims, jnp.float32)
    if shards:
        drawn = drawn * shard_levels(key, dims, shards, -0.22, 0.18)
    return jnp.clip(drawn, -reach, reach).astype(held_as)


def setup_inputs(seed: int = 0) -> dict:
    seeds = jax.random.split(jax.random.key(seed), 11)
    return {
        "teacher_slabs": bell_draw(seeds[0], (N_SEGMENT * TL_DEV, TOK, DT), 1.0, 6.0, ((0, 32), (2, 8))),
        "proj_weight": bell_draw(seeds[1], (N_TENSOR, DT // N_TENSOR, D), DT ** -0.5, 0.046875, ((1, 32), (2, 8))),
        "child_hidden": bell_draw(seeds[2], (N_SEGMENT * MOST, TOK, D), 1.0, 6.0, ((0, 32), (2, 8))),
        "norm_gain": jnp.clip(1.0 + 0.1 * jax.random.normal(seeds[3], (N_SEGMENT, D), jnp.float32), 0.5, 1.5),
        "key_weight": bell_draw(seeds[4], (N_SEGMENT, D, KV), D ** -0.5, 0.0625, ((0, 32), (1, 8))),
        "value_weight": bell_draw(seeds[5], (N_SEGMENT, D, KV), D ** -0.5, 0.0625, ((0, 32), (1, 8))),
        "key_cotangent": bell_draw(seeds[6], (N_SEGMENT, TOK, KV), 0.5, 3.0, ((0, 32),)),
        "value_cotangent": bell_draw(seeds[7], (N_SEGMENT, TOK, KV), 0.5, 3.0, ((0, 32),)),
        "layer_map": draw_layer_map(jax.random.fold_in(seeds[10], 71), 0),
        "layer_counts": ragged(seeds[9], N_HALF, LAYERS, MOST, 2).astype(jnp.int32),
    }


EPSILON = 1e-05

def layer_window(inputs):
    first_hidden, norm_scale, key_part, value_part, key_cot, value_cot = inputs
    hidden = first_hidden.astype(jnp.float32)
    delta_norm = jnp.dot(key_cot, key_part.T, preferred_element_type=jnp.float32) + jnp.dot(value_cot, value_part.T, preferred_element_type=jnp.float32)
    inverse_rms = lax.rsqrt(lax.optimization_barrier(jnp.mean(hidden * hidden, axis=-1, keepdims=True)) + EPSILON)
    normed = (hidden * inverse_rms * norm_scale).astype(jnp.bfloat16)
    key_grad = jnp.dot(normed.T, key_cot, preferred_element_type=jnp.float32).astype(jnp.bfloat16)
    value_grad = jnp.dot(normed.T, value_cot, preferred_element_type=jnp.float32).astype(jnp.bfloat16)
    gain_grad = lax.optimization_barrier(jnp.sum(hidden * inverse_rms * delta_norm, axis=0))
    inner_sum = lax.optimization_barrier(jnp.sum(hidden * norm_scale * delta_norm, axis=-1, keepdims=True))
    layer_grad = inverse_rms * norm_scale * delta_norm - hidden * inverse_rms ** 3 * inner_sum / D
    return (layer_grad, key_grad, value_grad, gain_grad)

def reference(teacher_slabs, proj_weight, child_hidden, norm_gain, key_weight, value_weight, key_cotangent, value_cotangent, layer_map, layer_counts):
    middle = N_SEGMENT // 2
    piece_width = DT // (N_TENSOR * N_SEGMENT)
    mapped = jnp.take(teacher_slabs, layer_map, axis=0)
    blocks = mapped.reshape(LAYERS, TOK, N_TENSOR, N_SEGMENT, piece_width)
    weight_blocks = proj_weight.reshape(N_TENSOR, N_SEGMENT, piece_width, D)

    def add_partial(running, index):
        slab_block = jnp.take(blocks, index, axis=3).astype(jnp.float32)
        weight_block = jnp.take(weight_blocks, index, axis=1).astype(jnp.float32)
        rounded = jnp.einsum('ckts,tsd->ckd', slab_block, weight_block).astype(jnp.bfloat16)
        return (running + rounded.astype(jnp.float32), None)
    projected, _ = lax.scan(add_partial, jnp.zeros((LAYERS, TOK, D), jnp.float32), jnp.arange(N_SEGMENT))
    prefix_end = jnp.cumsum(layer_counts)
    prefix_start = prefix_end - layer_counts
    segment_ids = jnp.arange(N_SEGMENT)
    child_index = segment_ids - middle
    child_slot = jnp.clip(child_index, 0, middle - 1)
    slot_ids = jnp.arange(MOST)
    own_count = jnp.where(child_index >= 0, layer_counts[child_slot], 0)
    owned = slot_ids[None, :] < own_count[:, None]
    layer_of = jnp.clip(prefix_start[child_slot][:, None] + slot_ids[None, :], 0, LAYERS - 1)
    hidden = child_hidden.reshape(N_SEGMENT, MOST, TOK, D)
    target = jnp.take(projected, layer_of.reshape(-1), axis=0).reshape(N_SEGMENT, MOST, TOK, D)
    regression = jnp.where(owned[:, :, None, None], hidden.astype(jnp.float32) - target, 0.0)
    layer_grad, key_grad, value_grad, gain_grad = lax.map(layer_window, (hidden[:, 0], norm_gain, key_weight, value_weight, key_cotangent, value_cotangent))
    is_child = segment_ids >= middle
    layer_grad = jnp.where(is_child[:, None, None], layer_grad, 0.0)
    regression = regression.at[:, 0].add(layer_grad)
    hidden_grad = regression.astype(jnp.bfloat16).reshape(N_SEGMENT * MOST, TOK, D)
    key_grad = jnp.where(is_child[:, None, None], key_grad, jnp.zeros_like(key_grad))
    value_grad = jnp.where(is_child[:, None, None], value_grad, jnp.zeros_like(value_grad))
    gain_grad = jnp.where(is_child[:, None], gain_grad, 0.0)
    return (hidden_grad, key_grad, value_grad, gain_grad)
```

```python
import jax
import jax.numpy as jnp
from jax import lax
from jax.experimental import pallas as pl
from jax.experimental.pallas import tpu as pltpu
from jax.sharding import Mesh, PartitionSpec as P

EPSILON = 1e-05
MIB = 1 << 20

SEGMENT = ("yh", "z", "c")
TENSOR = ("x", "yl")
YH, Z, C, X, YL = 2, 8, 2, 4, 2
QUARTERS = YH * C
LANES = 128


def pick_kernel(layer_map, received, picked):
    def step(layer, carry):
        picked[layer] = received[layer_map[layer]]
        return carry

    lax.fori_loop(0, picked.shape[0], step, 0)


def pick(layer_map, received):
    layers = layer_map.shape[0]
    return pl.pallas_call(
        pick_kernel,
        out_shape=jax.ShapeDtypeStruct((layers, *received.shape[1:]), received.dtype),
        in_specs=[
            pl.BlockSpec(memory_space=pltpu.SMEM),
            pl.BlockSpec(memory_space=pltpu.VMEM),
        ],
        out_specs=pl.BlockSpec(memory_space=pltpu.VMEM),
        cost_estimate=pl.CostEstimate(flops=0, bytes_accessed=1300000, transcendentals=0),
        name="pick_layers",
    )(layer_map, received)


def project_kernel(place, slot_layer, features, w0, w1, w2, w3, out, weight, product):
    blocks, layers, halves, tokens, lanes = features.shape
    piece = w0.shape[1]
    depth = halves * lanes
    for part, block in enumerate((w0, w1, w2, w3)):
        for t in range(blocks):
            row = pl.multiple_of(t * depth + place[part] * piece, piece)
            weight[pl.ds(row, piece), :] = block[t]
    group = 8
    rows = group * tokens

    def step(index, carry):
        first = index * group
        left = jnp.concatenate(
            [
                features[t, pl.ds(first, group), h].reshape(rows, lanes)
                for t in range(blocks)
                for h in range(halves)
            ],
            axis=1,
        )
        value = jnp.dot(left, weight[...], preferred_element_type=jnp.float32)
        product[pl.ds(first, group)] = value.astype(product.dtype).reshape(group, tokens, value.shape[1])
        return carry

    lax.fori_loop(0, layers // group, step, 0)

    def place_slot(slot, carry):
        out[slot] = product[slot_layer[slot]]
        return carry

    lax.fori_loop(0, out.shape[0], place_slot, 0)


def project(place, slot_layer, features, weights):
    blocks, layers, halves, tokens, lanes = features.shape
    columns = weights[0].shape[2]
    slots = slot_layer.shape[0]
    depth = blocks * halves * lanes
    vmem = pl.BlockSpec(memory_space=pltpu.VMEM)
    smem = pl.BlockSpec(memory_space=pltpu.SMEM)
    return pl.pallas_call(
        project_kernel,
        out_shape=jax.ShapeDtypeStruct((slots, tokens, columns), jnp.bfloat16),
        in_specs=[smem, smem] + [vmem] * 5,
        out_specs=vmem,
        scratch_shapes=[
            pltpu.VMEM((depth, columns), jnp.bfloat16),
            pltpu.VMEM((layers, tokens, columns), jnp.bfloat16),
        ],
        compiler_params=pltpu.CompilerParams(vmem_limit_bytes=40 * MIB),
        cost_estimate=pl.CostEstimate(
            flops=2 * layers * tokens * depth * columns, bytes_accessed=11 * MIB, transcendentals=0
        ),
        name="project",
    )(place, slot_layer, features, *weights)


def body(
    teacher_slabs,
    proj_weight,
    child_hidden,
    norm_gain,
    key_weight,
    value_weight,
    key_cotangent,
    value_cotangent,
    layer_map,
    layer_counts,
):
    yh, z, c = lax.axis_index("yh"), lax.axis_index("z"), lax.axis_index("c")
    slab_count, tokens, slab_width = teacher_slabs.shape
    layers = layer_map.shape[0]
    columns = proj_weight.shape[2]
    full_width = columns * X * YL
    slot_count = child_hidden.shape[0]
    quarter = tokens // QUARTERS
    segments = YH * Z * C
    middle = segments // 2

    swap = [(0, 1), (1, 0)]
    w_own = proj_weight
    w_sib = lax.ppermute(w_own, "c", swap)
    w_far = lax.ppermute(w_own, "yh", swap)
    w_far_sib = lax.ppermute(w_far, "c", swap)
    place = jnp.stack([2 * yh + c, 2 * yh + 1 - c, 2 * (1 - yh) + c, 2 * (1 - yh) + 1 - c]).astype(jnp.int32)

    arranged = (
        teacher_slabs.reshape(slab_count, YH, C, quarter, YH, Z, LANES)
        .transpose(1, 5, 2, 0, 4, 3, 6)
        .reshape(segments, slab_count * YH * quarter, LANES)
    )
    received = lax.all_to_all(arranged, SEGMENT, split_axis=0, concat_axis=0, tiled=True)
    received = received[:middle].reshape(middle * slab_count, YH * quarter, LANES)
    picked = pick(layer_map, received)
    gathered = lax.all_gather(picked, TENSOR, axis=0, tiled=False)
    features = gathered.reshape(X * YL, layers, YH, quarter, LANES)

    prefix_end = jnp.cumsum(layer_counts)
    prefix_start = prefix_end - layer_counts
    slot_ids = jnp.arange(slot_count)
    slot_layer = jnp.clip(prefix_start[:, None] + slot_ids[None, :], 0, layers - 1).reshape(-1).astype(jnp.int32)
    partial = project(place, slot_layer, features, (w_own, w_sib, w_far, w_far_sib))
    per_z = C * slot_count
    mine = lax.psum_scatter(
        partial.reshape(Z, per_z * quarter, columns), "z", scatter_dimension=0, tiled=False
    ).reshape(C, slot_count, quarter, columns)
    from_teacher = lax.ppermute(mine, "yh", [(0, 1)])
    both = jnp.stack([from_teacher, mine])
    keep = jnp.where(c == 0, both[:, 0], both[:, 1])
    give = jnp.where(c == 0, both[:, 1], both[:, 0])
    other = lax.ppermute(give, "c", swap)
    low = jnp.where(c == 0, keep, other)
    high = jnp.where(c == 0, other, keep)
    target = jnp.stack([low, high], axis=2).transpose(1, 0, 2, 3, 4).reshape(slot_count, tokens, columns)

    is_child = yh == 1
    child_slot = 2 * z + c
    own_count = jnp.where(is_child, layer_counts[child_slot], 0)
    owned = slot_ids < own_count
    regression = jnp.where(
        owned[:, None, None], child_hidden.astype(jnp.float32) - target.astype(jnp.float32), 0.0
    )

    first_hidden = child_hidden[0].astype(jnp.float32)
    norm_scale = norm_gain[0]
    contract_last = (((1,), (1,)), ((), ()))
    delta_norm = lax.dot_general(
        key_cotangent[0], key_weight[0], contract_last, preferred_element_type=jnp.float32
    )
    delta_norm = delta_norm + lax.dot_general(
        value_cotangent[0], value_weight[0], contract_last, preferred_element_type=jnp.float32
    )
    sums = lax.psum(
        jnp.stack(
            [
                jnp.sum(first_hidden * first_hidden, axis=1),
                jnp.sum(first_hidden * norm_scale * delta_norm, axis=1),
            ]
        ),
        TENSOR,
    )
    squares, inner_sum = sums[0], sums[1]
    inverse_rms = lax.rsqrt(squares / full_width + EPSILON)[:, None]
    normed = (first_hidden * inverse_rms * norm_scale).astype(jnp.bfloat16)
    contract_rows = (((0,), (0,)), ((), ()))
    key_grad = lax.dot_general(
        normed, key_cotangent[0], contract_rows, preferred_element_type=jnp.float32
    ).astype(jnp.bfloat16)
    value_grad = lax.dot_general(
        normed, value_cotangent[0], contract_rows, preferred_element_type=jnp.float32
    ).astype(jnp.bfloat16)
    gain_grad = jnp.sum(first_hidden * inverse_rms * delta_norm, axis=0)
    layer_grad = (
        inverse_rms * norm_scale * delta_norm
        - first_hidden * inverse_rms**3 * inner_sum[:, None] / full_width
    )
    layer_grad = jnp.where(is_child, layer_grad, 0.0)
    hidden_grad = regression.at[0].add(layer_grad).astype(jnp.bfloat16)
    key_grad = jnp.where(is_child, key_grad, jnp.zeros_like(key_grad))
    value_grad = jnp.where(is_child, value_grad, jnp.zeros_like(value_grad))
    gain_grad = jnp.where(is_child, gain_grad, 0.0)
    return (hidden_grad, key_grad[None], value_grad[None], gain_grad[None])


def solution(mesh):
    fine = Mesh(mesh.devices.reshape(YH, Z, C, X, YL), (*SEGMENT, *TENSOR))
    placed = (
        P(SEGMENT, None, TENSOR),
        P(None, SEGMENT, TENSOR),
        P(SEGMENT, None, TENSOR),
        P(SEGMENT, TENSOR),
        P(SEGMENT, TENSOR, None),
        P(SEGMENT, TENSOR, None),
        P(SEGMENT, None, None),
        P(SEGMENT, None, None),
        P(),
        P(),
    )
    return jax.shard_map(
        body,
        mesh=fine,
        in_specs=placed,
        out_specs=(
            P(SEGMENT, None, TENSOR),
            P(SEGMENT, TENSOR, None),
            P(SEGMENT, TENSOR, None),
            P(SEGMENT, TENSOR),
        ),
        check_vma=False,
    )
```

```python
import jax
import jax.numpy as jnp
from jax import lax
from jax.experimental import pallas as pl
from jax.experimental.pallas import tpu as pltpu
from jax.sharding import Mesh, PartitionSpec as P

EPSILON = 1e-05
MIB = 1 << 20

SEGMENT = ("yh", "z", "c")
TENSOR = ("x", "yl")
YH, Z, C, X, YL = 2, 8, 2, 4, 2
QUARTERS = YH * C
LANES = 128


def pick_kernel(layer_map, received, picked):
    def step(layer, carry):
        picked[layer] = received[layer_map[layer]]
        return carry

    lax.fori_loop(0, picked.shape[0], step, 0)


def pick(layer_map, received):
    layers = layer_map.shape[0]
    return pl.pallas_call(
        pick_kernel,
        out_shape=jax.ShapeDtypeStruct((layers, *received.shape[1:]), received.dtype),
        in_specs=[
            pl.BlockSpec(memory_space=pltpu.SMEM),
            pl.BlockSpec(memory_space=pltpu.VMEM),
        ],
        out_specs=pl.BlockSpec(memory_space=pltpu.VMEM),
        cost_estimate=pl.CostEstimate(flops=0, bytes_accessed=1300000, transcendentals=0),
        name="pick_layers",
    )(layer_map, received)


def project_kernel(
    place, block_row, slot_layer, f0, f1, f2a, f2b, f3, g0, g1, g2a, g2b, g3,
    w_own, w_sib, w_far_a, w_far_b, w_fs_a, w_fs_b, out, weight, product,
):
    layers, halves, tokens, lanes = f0.shape
    piece = w_own.shape[1]
    depth = halves * lanes
    blocks = block_row.shape[0]
    far = w_far_a.shape[0]
    for t in range(blocks):
        first, second = (w_far_a, w_fs_a) if t < far else (w_far_b, w_fs_b)
        for part, block in enumerate((w_own[t], w_sib[t], first[t % far], second[t % far])):
            row = pl.multiple_of(block_row[t] * depth + place[part] * piece, piece)
            weight[pl.ds(row, piece), :] = block
    rows = 256
    group = rows // tokens
    half = layers // 2
    for side in range(2):
        f2, g2 = ((f2a, g2a), (f2b, g2b))[side]

        def step(index, carry):
            near = pl.ds(side * half + index * group, group)
            far_off = pl.ds(index * group, group)
            left = jnp.concatenate(
                [
                    ref[far_off if place_of % 4 == 2 else near, h].reshape(rows, lanes)
                    for place_of, ref in enumerate((f0, f1, f2, f3, g0, g1, g2, g3))
                    for h in range(halves)
                ],
                axis=1,
            )
            value = jnp.dot(left, weight[...], preferred_element_type=jnp.float32)
            product[near] = value.astype(product.dtype).reshape(group, tokens, value.shape[1])
            return carry

        lax.fori_loop(0, half // group, step, 0)

    def place_slot(slot, carry):
        out[slot] = product[slot_layer[slot]]
        return carry

    lax.fori_loop(0, out.shape[0], place_slot, 0)


def project(place, block_row, slot_layer, features, weights):
    layers, halves, tokens, lanes = features[0].shape
    columns = weights[0].shape[2]
    slots = slot_layer.shape[0]
    depth = block_row.shape[0] * halves * lanes
    vmem = pl.BlockSpec(memory_space=pltpu.VMEM)
    smem = pl.BlockSpec(memory_space=pltpu.SMEM)
    return pl.pallas_call(
        project_kernel,
        out_shape=jax.ShapeDtypeStruct((slots, tokens, columns), jnp.bfloat16),
        in_specs=[smem] * 3 + [vmem] * (len(features) + len(weights)),
        out_specs=vmem,
        scratch_shapes=[
            pltpu.VMEM((depth, columns), jnp.bfloat16),
            pltpu.VMEM((layers, tokens, columns), jnp.bfloat16),
        ],
        compiler_params=pltpu.CompilerParams(vmem_limit_bytes=40 * MIB),
        cost_estimate=pl.CostEstimate(
            flops=2 * layers * tokens * depth * columns, bytes_accessed=11 * MIB, transcendentals=0
        ),
        name="project",
    )(place, block_row, slot_layer, *features, *weights)


def gather_tensor(own):
    up = [(i, (i + 1) % X) for i in range(X)]
    down = [(i, (i - 1) % X) for i in range(X)]
    swap = [(0, 1), (1, 0)]
    half = own.shape[0] // 2
    f3 = lax.ppermute(own, "x", up)
    f1 = lax.ppermute(own, "x", down)
    g0 = lax.ppermute(own, "yl", swap)
    f2a = lax.ppermute(f3[:half], "x", up)
    f2b = lax.ppermute(f1[half:], "x", down)
    g3 = lax.ppermute(g0, "x", up)
    g1 = lax.ppermute(g0, "x", down)
    g2a = lax.ppermute(f2a, "yl", swap)
    g2b = lax.ppermute(f2b, "yl", swap)
    return (own, f1, f2a, f2b, f3, g0, g1, g2a, g2b, g3)


def body(
    teacher_slabs,
    proj_weight,
    child_hidden,
    norm_gain,
    key_weight,
    value_weight,
    key_cotangent,
    value_cotangent,
    layer_map,
    layer_counts,
):
    yh, z, c = lax.axis_index("yh"), lax.axis_index("z"), lax.axis_index("c")
    x, yl = lax.axis_index("x"), lax.axis_index("yl")
    slab_count, tokens, slab_width = teacher_slabs.shape
    layers = layer_map.shape[0]
    columns = proj_weight.shape[2]
    full_width = columns * X * YL
    slot_count = child_hidden.shape[0]
    quarter = tokens // QUARTERS

    swap = [(0, 1), (1, 0)]
    ring = YH * YL
    up = [(i, (i + 1) % ring) for i in range(ring)]
    down = [(i, (i - 1) % ring) for i in range(ring)]
    side = ("yh", "yl")
    half_blocks = proj_weight.shape[0] // 2
    w_far_a = lax.ppermute(lax.ppermute(proj_weight[:half_blocks], side, up), side, up)
    w_far_b = lax.ppermute(lax.ppermute(proj_weight[half_blocks:], side, down), side, down)
    w_sib = lax.ppermute(proj_weight, "c", swap)
    w_fs_a = lax.ppermute(w_far_a, "c", swap)
    w_fs_b = lax.ppermute(w_far_b, "c", swap)
    weights = (proj_weight, w_sib, w_far_a, w_far_b, w_fs_a, w_fs_b)
    place = jnp.stack([2 * yh + c, 2 * yh + 1 - c, 2 * (1 - yh) + c, 2 * (1 - yh) + 1 - c]).astype(jnp.int32)

    def arrange(section):
        width = tokens // YH
        return (
            teacher_slabs[:, section * width : (section + 1) * width]
            .reshape(slab_count, C, quarter, YH, Z, LANES)
            .transpose(4, 1, 0, 3, 2, 5)
            .reshape(Z * C, slab_count * YH * quarter, LANES)
        )

    sent = lax.ppermute(arrange(1), side, [(0, 3), (1, 2)])
    arranged = jnp.where(yh == 0, arrange(0), sent)
    received = lax.all_to_all(arranged, ("z", "c"), split_axis=0, concat_axis=0, tiled=True)
    received = received.reshape(Z * C * slab_count, YH, quarter, LANES)
    features = gather_tensor(pick(layer_map, received))
    block = jnp.arange(X * YL)
    block_row = ((block // YL - x) % X + X * (block % YL != (yl + yh) % 2)).astype(jnp.int32)

    prefix_end = jnp.cumsum(layer_counts)
    prefix_start = prefix_end - layer_counts
    slot_ids = jnp.arange(slot_count)
    slot_layer = jnp.clip(prefix_start[:, None] + slot_ids[None, :], 0, layers - 1).reshape(-1).astype(jnp.int32)
    partial = project(place, block_row, slot_layer, features, weights)
    per_z = C * slot_count
    mine = lax.psum_scatter(
        partial.reshape(Z, per_z * quarter, columns), "z", scatter_dimension=0, tiled=False
    ).reshape(C, slot_count, quarter, columns)
    from_teacher = lax.ppermute(mine, "yh", [(0, 1)])
    both = jnp.stack([from_teacher, mine])
    keep = jnp.where(c == 0, both[:, 0], both[:, 1])
    give = jnp.where(c == 0, both[:, 1], both[:, 0])
    other = lax.ppermute(give, "c", swap)
    low = jnp.where(c == 0, keep, other)
    high = jnp.where(c == 0, other, keep)
    target = jnp.stack([low, high], axis=2).transpose(1, 0, 2, 3, 4).reshape(slot_count, tokens, columns)

    is_child = yh == 1
    child_slot = 2 * z + c
    own_count = jnp.where(is_child, layer_counts[child_slot], 0)
    owned = slot_ids < own_count
    regression = jnp.where(
        owned[:, None, None], child_hidden.astype(jnp.float32) - target.astype(jnp.float32), 0.0
    )

    first_hidden = child_hidden[0].astype(jnp.float32)
    norm_scale = norm_gain[0]
    contract_last = (((1,), (1,)), ((), ()))
    delta_norm = lax.dot_general(
        key_cotangent[0], key_weight[0], contract_last, preferred_element_type=jnp.float32
    )
    delta_norm = delta_norm + lax.dot_general(
        value_cotangent[0], value_weight[0], contract_last, preferred_element_type=jnp.float32
    )
    sums = lax.psum(
        jnp.stack(
            [
                jnp.sum(first_hidden * first_hidden, axis=1),
                jnp.sum(first_hidden * norm_scale * delta_norm, axis=1),
            ]
        ),
        TENSOR,
    )
    squares, inner_sum = sums[0], sums[1]
    inverse_rms = lax.rsqrt(squares / full_width + EPSILON)[:, None]
    normed = (first_hidden * inverse_rms * norm_scale).astype(jnp.bfloat16)
    contract_rows = (((0,), (0,)), ((), ()))
    key_grad = lax.dot_general(
        normed, key_cotangent[0], contract_rows, preferred_element_type=jnp.float32
    ).astype(jnp.bfloat16)
    value_grad = lax.dot_general(
        normed, value_cotangent[0], contract_rows, preferred_element_type=jnp.float32
    ).astype(jnp.bfloat16)
    gain_grad = jnp.sum(first_hidden * inverse_rms * delta_norm, axis=0)
    layer_grad = (
        inverse_rms * norm_scale * delta_norm
        - first_hidden * inverse_rms**3 * inner_sum[:, None] / full_width
    )
    layer_grad = jnp.where(is_child, layer_grad, 0.0)
    hidden_grad = regression.at[0].add(layer_grad).astype(jnp.bfloat16)
    key_grad = jnp.where(is_child, key_grad, jnp.zeros_like(key_grad))
    value_grad = jnp.where(is_child, value_grad, jnp.zeros_like(value_grad))
    gain_grad = jnp.where(is_child, gain_grad, 0.0)
    return (hidden_grad, key_grad[None], value_grad[None], gain_grad[None])


def solution(mesh):
    fine = Mesh(mesh.devices.reshape(YH, Z, C, X, YL), (*SEGMENT, *TENSOR))
    placed = (
        P(SEGMENT, None, TENSOR),
        P(None, SEGMENT, TENSOR),
        P(SEGMENT, None, TENSOR),
        P(SEGMENT, TENSOR),
        P(SEGMENT, TENSOR, None),
        P(SEGMENT, TENSOR, None),
        P(SEGMENT, None, None),
        P(SEGMENT, None, None),
        P(),
        P(),
    )
    return jax.shard_map(
        body,
        mesh=fine,
        in_specs=placed,
        out_specs=(
            P(SEGMENT, None, TENSOR),
            P(SEGMENT, TENSOR, None),
            P(SEGMENT, TENSOR, None),
            P(SEGMENT, TENSOR),
        ),
        check_vma=False,
    )
```

```python
import jax
import jax.numpy as jnp
from jax import lax
from jax.experimental import pallas as pl
from jax.experimental.pallas import tpu as pltpu
from jax.sharding import Mesh, PartitionSpec as P

EPSILON = 1e-05
MIB = 1 << 20

SEGMENT = ("yh", "z", "c")
TENSOR = ("x", "yl")
YH, Z, C, X, YL = 2, 8, 2, 4, 2
QUARTERS = YH * C
LANES = 128
PARTS = 2


def arrange_kernel(slabs, *out):
    slab_count, width, _ = slabs.shape
    tokens = width // (C * PARTS)
    for part in range(PARTS):
        for c in range(C):
            first = (c * PARTS + part) * tokens
            for z in range(Z):
                for slab in range(slab_count):
                    for h in range(YH):
                        lane = (h * Z + z) * LANES
                        row = (slab * YH + h) * tokens
                        out[part][z * C + c, row : row + tokens, :] = slabs[
                            slab, first : first + tokens, lane : lane + LANES
                        ]


def arrange(teacher_slabs, section):
    slab_count, tokens, width = teacher_slabs.shape
    rows = slab_count * YH * (tokens // (QUARTERS * PARTS))
    shape = jax.ShapeDtypeStruct((Z * C, rows, LANES), teacher_slabs.dtype)
    return pl.pallas_call(
        arrange_kernel,
        grid=(1,),
        out_shape=[shape] * PARTS,
        in_specs=[pl.BlockSpec((slab_count, tokens // YH, width), lambda i: (0, section, 0))],
        out_specs=[pl.BlockSpec(shape.shape, lambda i: (0, 0, 0))] * PARTS,
        cost_estimate=pl.CostEstimate(flops=0, bytes_accessed=1600000, transcendentals=0),
        name="arrange",
    )(teacher_slabs)


def pick_kernel(layer_map, received, picked):
    def step(layer, carry):
        picked[layer] = received[layer_map[layer]]
        return carry

    lax.fori_loop(0, picked.shape[0], step, 0)


def pick(layer_map, received):
    layers = layer_map.shape[0]
    return pl.pallas_call(
        pick_kernel,
        out_shape=jax.ShapeDtypeStruct((layers, *received.shape[1:]), received.dtype),
        in_specs=[
            pl.BlockSpec(memory_space=pltpu.SMEM),
            pl.BlockSpec(memory_space=pltpu.VMEM),
        ],
        out_specs=pl.BlockSpec(memory_space=pltpu.VMEM),
        cost_estimate=pl.CostEstimate(flops=0, bytes_accessed=1300000, transcendentals=0),
        name="pick_layers",
    )(layer_map, received)


def project_kernel(place, block_row, slot_layer, *refs):
    features, weights = refs[:10], refs[10:16]
    out, weight, product, *held, spare, feature_sem, weight_sem = refs[17:]
    layers, halves, tokens, lanes = features[0].shape
    w_own, w_sib, w_far_a, w_far_b, w_fs_a, w_fs_b = weights
    piece = w_own.shape[1]
    depth = halves * lanes
    blocks = block_row.shape[0]
    far = w_far_a.shape[0]
    copies = []
    for t in range(blocks):
        first, second = (w_far_a, w_fs_a) if t < far else (w_far_b, w_fs_b)
        for part, block in enumerate((w_own.at[t], w_sib.at[t], first.at[t % far], second.at[t % far])):
            row = pl.multiple_of(block_row[t] * depth + place[part] * piece, piece)
            copies.append(pltpu.make_async_copy(block, weight.at[pl.ds(row, piece)], weight_sem.at[t, part]))
    for index, (block, slot) in enumerate(zip((*features, refs[16].at[0]), (*held, spare))):
        copies.append(pltpu.make_async_copy(block, slot, feature_sem.at[index]))
    for copy in copies:
        copy.start()
    for copy in copies:
        copy.wait()
    f0, f1, f2a, f2b, f3, g0, g1, g2a, g2b, g3 = held
    rows = 256
    group = rows // tokens
    half = layers // 2
    for side in range(2):
        f2, g2 = ((f2a, g2a), (f2b, g2b))[side]

        def step(index, carry):
            near = pl.ds(side * half + index * group, group)
            far_off = pl.ds(index * group, group)
            left = jnp.concatenate(
                [
                    ref[far_off if place_of % 4 == 2 else near, h].reshape(rows, lanes)
                    for place_of, ref in enumerate((f0, f1, f2, f3, g0, g1, g2, g3))
                    for h in range(halves)
                ],
                axis=1,
            )
            value = jnp.dot(left, weight[...], preferred_element_type=jnp.float32)
            product[near] = value.astype(product.dtype).reshape(group, tokens, value.shape[1])
            return carry

        lax.fori_loop(0, half // group, step, 0)

    def place_slot(slot, carry):
        out[slot] = product[slot_layer[slot]]
        return carry

    lax.fori_loop(0, out.shape[0], place_slot, 0)


def project(place, block_row, slot_layer, features, weights, after):
    layers, halves, tokens, lanes = features[0].shape
    columns = weights[0].shape[2]
    slots = slot_layer.shape[0]
    blocks = block_row.shape[0]
    depth = blocks * halves * lanes
    smem = pl.BlockSpec(memory_space=pltpu.SMEM)
    return pl.pallas_call(
        project_kernel,
        out_shape=jax.ShapeDtypeStruct((slots, tokens, columns), jnp.bfloat16),
        in_specs=[smem] * 3 + [pl.BlockSpec(memory_space=pl.ANY)] * (len(features) + len(weights) + 1),
        out_specs=pl.BlockSpec(memory_space=pltpu.VMEM),
        scratch_shapes=[
            pltpu.VMEM((depth, columns), jnp.bfloat16),
            pltpu.VMEM((layers, tokens, columns), jnp.bfloat16),
            *[pltpu.VMEM(feature.shape, feature.dtype) for feature in features],
            pltpu.VMEM(after.shape[1:], after.dtype),
            pltpu.SemaphoreType.DMA((len(features) + 1,)),
            pltpu.SemaphoreType.DMA((blocks, QUARTERS)),
        ],
        compiler_params=pltpu.CompilerParams(vmem_limit_bytes=40 * MIB),
        cost_estimate=pl.CostEstimate(
            flops=2 * layers * tokens * depth * columns, bytes_accessed=8 * MIB, transcendentals=0
        ),
        name="project",
    )(place, block_row, slot_layer, *features, *weights, after)


def gather_tensor(own):
    up = [(i, (i + 1) % X) for i in range(X)]
    down = [(i, (i - 1) % X) for i in range(X)]
    swap = [(0, 1), (1, 0)]
    half = own.shape[0] // 2
    f3 = lax.ppermute(own, "x", up)
    f1 = lax.ppermute(own, "x", down)
    g0 = lax.ppermute(own, "yl", swap)
    f2a = lax.ppermute(f3[:half], "x", up)
    f2b = lax.ppermute(f1[half:], "x", down)
    g3 = lax.ppermute(g0, "x", up)
    g1 = lax.ppermute(g0, "x", down)
    g2a = lax.ppermute(f2a, "yl", swap)
    g2b = lax.ppermute(f2b, "yl", swap)
    return (own, f1, f2a, f2b, f3, g0, g1, g2a, g2b, g3)


def body(
    teacher_slabs,
    proj_weight,
    child_hidden,
    norm_gain,
    key_weight,
    value_weight,
    key_cotangent,
    value_cotangent,
    layer_map,
    layer_counts,
):
    yh, z, c = lax.axis_index("yh"), lax.axis_index("z"), lax.axis_index("c")
    x, yl = lax.axis_index("x"), lax.axis_index("yl")
    slab_count, tokens, slab_width = teacher_slabs.shape
    layers = layer_map.shape[0]
    columns = proj_weight.shape[2]
    full_width = columns * X * YL
    slot_count = child_hidden.shape[0]
    quarter = tokens // QUARTERS

    swap = [(0, 1), (1, 0)]
    ring = YH * YL
    up = [(i, (i + 1) % ring) for i in range(ring)]
    down = [(i, (i - 1) % ring) for i in range(ring)]
    side = ("yh", "yl")
    half_blocks = proj_weight.shape[0] // 2
    w_far_a = lax.ppermute(lax.ppermute(proj_weight[:half_blocks], side, up), side, up)
    w_far_b = lax.ppermute(lax.ppermute(proj_weight[half_blocks:], side, down), side, down)
    w_sib = lax.ppermute(proj_weight, "c", swap)
    w_fs_a = lax.ppermute(w_far_a, "c", swap)
    w_fs_b = lax.ppermute(w_far_b, "c", swap)
    weights = (proj_weight, w_sib, w_far_a, w_far_b, w_fs_a, w_fs_b)
    place = jnp.stack([2 * yh + c, 2 * yh + 1 - c, 2 * (1 - yh) + c, 2 * (1 - yh) + 1 - c]).astype(jnp.int32)

    block = jnp.arange(X * YL)
    block_row = ((block // YL - x) % X + X * (block % YL != (yl + yh) % 2)).astype(jnp.int32)
    prefix_end = jnp.cumsum(layer_counts)
    prefix_start = prefix_end - layer_counts
    slot_ids = jnp.arange(slot_count)
    slot_layer = jnp.clip(prefix_start[:, None] + slot_ids[None, :], 0, layers - 1).reshape(-1).astype(jnp.int32)

    part_tokens = quarter // PARTS
    sent = [lax.ppermute(part, side, [(0, 3), (1, 2)]) for part in arrange(teacher_slabs, 1)]
    kept = arrange(teacher_slabs, 0)

    received = []
    for part in range(PARTS):
        arranged = jnp.where(yh == 0, kept[part], sent[part])
        blocks = lax.all_to_all(arranged, ("z", "c"), split_axis=0, concat_axis=0, tiled=True)
        received.append(blocks.reshape(Z * C * slab_count, YH, part_tokens, LANES))

    def part_target(part):
        features = gather_tensor(pick(layer_map, received[part]))
        after = received[(part + 1) % PARTS]
        partial = project(place, block_row, slot_layer, features, weights, after)
        mine = lax.psum_scatter(
            partial.reshape(Z, C * slot_count * part_tokens, columns), "z", scatter_dimension=0, tiled=False
        ).reshape(C, slot_count, part_tokens, columns)
        from_teacher = lax.ppermute(mine, "yh", [(0, 1)])
        both = jnp.stack([from_teacher, mine])
        keep = jnp.where(c == 0, both[:, 0], both[:, 1])
        give = jnp.where(c == 0, both[:, 1], both[:, 0])
        other = lax.ppermute(give, "c", swap)
        low = jnp.where(c == 0, keep, other)
        high = jnp.where(c == 0, other, keep)
        return jnp.stack([low, high], axis=2)

    target = jnp.stack([part_target(part) for part in range(PARTS)], axis=3)
    target = target.transpose(1, 0, 2, 3, 4, 5).reshape(slot_count, tokens, columns)

    is_child = yh == 1
    child_slot = 2 * z + c
    own_count = jnp.where(is_child, layer_counts[child_slot], 0)
    owned = slot_ids < own_count
    regression = jnp.where(
        owned[:, None, None], child_hidden.astype(jnp.float32) - target.astype(jnp.float32), 0.0
    )

    first_hidden = child_hidden[0].astype(jnp.float32)
    norm_scale = norm_gain[0]
    contract_last = (((1,), (1,)), ((), ()))
    delta_norm = lax.dot_general(
        key_cotangent[0], key_weight[0], contract_last, preferred_element_type=jnp.float32
    )
    delta_norm = delta_norm + lax.dot_general(
        value_cotangent[0], value_weight[0], contract_last, preferred_element_type=jnp.float32
    )
    sums = lax.psum(
        jnp.stack(
            [
                jnp.sum(first_hidden * first_hidden, axis=1),
                jnp.sum(first_hidden * norm_scale * delta_norm, axis=1),
            ]
        ),
        TENSOR,
    )
    squares, inner_sum = sums[0], sums[1]
    inverse_rms = lax.rsqrt(squares / full_width + EPSILON)[:, None]
    normed = (first_hidden * inverse_rms * norm_scale).astype(jnp.bfloat16)
    contract_rows = (((0,), (0,)), ((), ()))
    key_grad = lax.dot_general(
        normed, key_cotangent[0], contract_rows, preferred_element_type=jnp.float32
    ).astype(jnp.bfloat16)
    value_grad = lax.dot_general(
        normed, value_cotangent[0], contract_rows, preferred_element_type=jnp.float32
    ).astype(jnp.bfloat16)
    gain_grad = jnp.sum(first_hidden * inverse_rms * delta_norm, axis=0)
    layer_grad = (
        inverse_rms * norm_scale * delta_norm
        - first_hidden * inverse_rms**3 * inner_sum[:, None] / full_width
    )
    layer_grad = jnp.where(is_child, layer_grad, 0.0)
    hidden_grad = regression.at[0].add(layer_grad).astype(jnp.bfloat16)
    key_grad = jnp.where(is_child, key_grad, jnp.zeros_like(key_grad))
    value_grad = jnp.where(is_child, value_grad, jnp.zeros_like(value_grad))
    gain_grad = jnp.where(is_child, gain_grad, 0.0)
    return (hidden_grad, key_grad[None], value_grad[None], gain_grad[None])


def solution(mesh):
    fine = Mesh(mesh.devices.reshape(YH, Z, C, X, YL), (*SEGMENT, *TENSOR))
    placed = (
        P(SEGMENT, None, TENSOR),
        P(None, SEGMENT, TENSOR),
        P(SEGMENT, None, TENSOR),
        P(SEGMENT, TENSOR),
        P(SEGMENT, TENSOR, None),
        P(SEGMENT, TENSOR, None),
        P(SEGMENT, None, None),
        P(SEGMENT, None, None),
        P(),
        P(),
    )
    return jax.shard_map(
        body,
        mesh=fine,
        in_specs=placed,
        out_specs=(
            P(SEGMENT, None, TENSOR),
            P(SEGMENT, TENSOR, None),
            P(SEGMENT, TENSOR, None),
            P(SEGMENT, TENSOR),
        ),
        check_vma=False,
    )
```

```python
import jax
import jax.numpy as jnp
from jax import lax
from jax.experimental import pallas as pl
from jax.experimental.pallas import tpu as pltpu
from jax.sharding import Mesh, PartitionSpec as P

EPSILON = 1e-05
MIB = 1 << 20

SEGMENT = ("yh", "z", "c")
TENSOR = ("x", "yl")
YH, Z, C, X, YL = 2, 8, 2, 4, 2
QUARTERS = YH * C
LANES = 128


def arrange_kernel(slabs, *refs):
    if len(refs) > 1:
        after, out, spare, sem = refs
        copy = pltpu.make_async_copy(after, spare, sem)
        copy.start()
        copy.wait()
    else:
        (out,) = refs
    slab_count, width, _ = slabs.shape
    tokens = width // C
    for c in range(C):
        for z in range(Z):
            for slab in range(slab_count):
                for h in range(YH):
                    lane = (h * Z + z) * LANES
                    row = (slab * YH + h) * tokens
                    out[z * C + c, row : row + tokens, :] = slabs[
                        slab, c * tokens : (c + 1) * tokens, lane : lane + LANES
                    ]


def arrange(teacher_slabs, section, after=()):
    slab_count, tokens, width = teacher_slabs.shape
    rows = slab_count * YH * (tokens // QUARTERS)
    shape = jax.ShapeDtypeStruct((Z * C, rows, LANES), teacher_slabs.dtype)
    return pl.pallas_call(
        arrange_kernel,
        grid=(1,),
        out_shape=shape,
        in_specs=[pl.BlockSpec((slab_count, tokens // YH, width), lambda i: (0, section, 0))]
        + [pl.BlockSpec(memory_space=pl.ANY)] * len(after),
        out_specs=pl.BlockSpec(shape.shape, lambda i: (0, 0, 0)),
        scratch_shapes=[pltpu.VMEM(array.shape, array.dtype) for array in after]
        + [pltpu.SemaphoreType.DMA] * len(after),
        cost_estimate=pl.CostEstimate(flops=0, bytes_accessed=1600000, transcendentals=0),
        name="arrange",
    )(teacher_slabs, *after)


def pick_kernel(layer_map, received, picked):
    def step(layer, carry):
        picked[layer] = received[layer_map[layer]]
        return carry

    lax.fori_loop(0, picked.shape[0], step, 0)


def pick(layer_map, received):
    layers = layer_map.shape[0]
    return pl.pallas_call(
        pick_kernel,
        out_shape=jax.ShapeDtypeStruct((layers, *received.shape[1:]), received.dtype),
        in_specs=[
            pl.BlockSpec(memory_space=pltpu.SMEM),
            pl.BlockSpec(memory_space=pltpu.VMEM),
        ],
        out_specs=pl.BlockSpec(memory_space=pltpu.VMEM),
        cost_estimate=pl.CostEstimate(flops=0, bytes_accessed=1300000, transcendentals=0),
        name="pick_layers",
    )(layer_map, received)


DISTANCES = (4, 3, -3, 2, -2, 1, -1, 0)
FIRST = ((0, 0), (1, 0), (3, 0), (0, 1))
REST = ((2, 0), (1, 1), (2, 1), (3, 1))
GROUPS = 4
WEIGHTS = 6


def load_weight(place, blocks, weights, weight, sem):
    piece = weights[0].shape[1]
    half = piece // 2
    copies = []
    for index in range(sem.shape[0]):
        for source, ref in enumerate(weights):
            part = source if source < 2 else 2 + (source - 2) // 2
            shift = half if source in (3, 5) else 0
            row = pl.multiple_of(index * QUARTERS * piece + place[part] * piece + shift, half)
            target = weight.at[pl.ds(row, ref.shape[1])]
            copies.append(pltpu.make_async_copy(ref.at[blocks[index]], target, sem.at[index, source]))
    for copy in copies:
        copy.start()
    return copies


def load_features(features, held, sem):
    copies = [
        pltpu.make_async_copy(ref, slot, sem.at[index]) for index, (ref, slot) in enumerate(zip(features, held))
    ]
    for copy in copies:
        copy.start()
    return copies


def left_rows(refs, firsts, group):
    _, halves, tokens, lanes = refs[0].shape
    return jnp.concatenate(
        [
            ref[pl.ds(first, group), h].reshape(group * tokens, lanes)
            for ref, first in zip(refs, firsts)
            for h in range(halves)
        ],
        axis=1,
    )


def project_first_kernel(place, blocks, *refs):
    features, refs = refs[: len(FIRST)], refs[len(FIRST) :]
    weights, (out, weight, *held, feature_sem, weight_sem) = refs[:WEIGHTS], refs[WEIGHTS:]
    copies = load_weight(place, blocks, weights, weight, weight_sem) + load_features(features, held, feature_sem)
    for copy in copies:
        copy.wait()
    group = features[0].shape[0] // GROUPS
    for number in range(GROUPS):
        left = left_rows(held, [number * group] * len(held), group)
        out[number] = jnp.dot(left, weight[...], preferred_element_type=jnp.float32)


def project_rest_kernel(place, blocks, slot_layer, partial, *refs):
    count = len(REST) + 2
    features, refs = refs[:count], refs[count:]
    weights, refs = refs[:WEIGHTS], refs[WEIGHTS:]
    outs, refs = refs[: len(DISTANCES) + 1], refs[len(DISTANCES) + 1 :]
    weight, before, product, *held, feature_sem, weight_sem, before_sem = refs
    copies = load_weight(place, blocks, weights, weight, weight_sem) + load_features(features, held, feature_sem)
    befores = [
        pltpu.make_async_copy(partial.at[number], before.at[number], before_sem.at[number]) for number in range(GROUPS)
    ]
    for copy in befores:
        copy.start()
    for copy in copies:
        copy.wait()
    layers, halves, tokens, lanes = features[2].shape
    group = layers // GROUPS
    near_a, near_b, row_1, row_2a, row_2b, row_3 = held
    for number in range(GROUPS):
        first = number * group
        side = number // (GROUPS // 2)
        offset = (number - side * (GROUPS // 2)) * group
        refs = ((near_a, near_b)[side], row_1, (row_2a, row_2b)[side], row_3)
        left = left_rows(refs, (offset, first, offset, first), group)
        value = jnp.dot(left, weight[...], preferred_element_type=jnp.float32)
        befores[number].wait()
        value = (value + before[number]).astype(product.dtype)
        product[pl.ds(first, group)] = value.reshape(group, tokens, value.shape[1])
    slots = outs[-1].shape[1]
    for index, out in enumerate(outs):
        chunk = max(index - 1, 0)
        for c in range(C):
            for slot in range(slots):
                value = product[slot_layer[(chunk * C + c) * slots + slot]]
                if index > 1:
                    out[c, slot] = value
                elif index == c:
                    out[slot] = value


def project_first(place, blocks, features, weights):
    layers, halves, tokens, lanes = features[0].shape
    columns = weights[0].shape[2]
    depth = len(FIRST) * halves * lanes
    shape = (GROUPS, layers * tokens // GROUPS, columns)
    smem, anywhere = pl.BlockSpec(memory_space=pltpu.SMEM), pl.BlockSpec(memory_space=pl.ANY)
    return pl.pallas_call(
        project_first_kernel,
        out_shape=jax.ShapeDtypeStruct(shape, jnp.float32),
        in_specs=[smem] * 2 + [anywhere] * (len(features) + len(weights)),
        out_specs=pl.BlockSpec(memory_space=pltpu.VMEM),
        scratch_shapes=[
            pltpu.VMEM((depth, columns), jnp.bfloat16),
            *[pltpu.VMEM(feature.shape, feature.dtype) for feature in features],
            pltpu.SemaphoreType.DMA((len(features),)),
            pltpu.SemaphoreType.DMA((len(FIRST), WEIGHTS)),
        ],
        compiler_params=pltpu.CompilerParams(vmem_limit_bytes=40 * MIB),
        cost_estimate=pl.CostEstimate(
            flops=2 * layers * tokens * depth * columns, bytes_accessed=8 * MIB, transcendentals=0
        ),
        name="project_first",
    )(place, blocks, *features, *weights)


def project_rest(place, blocks, slot_layer, partial, features, weights):
    layers, halves, tokens, lanes = features[2].shape
    columns = weights[0].shape[2]
    depth = len(REST) * halves * lanes
    slots = slot_layer.shape[0] // (len(DISTANCES) * C)
    smem, vmem = pl.BlockSpec(memory_space=pltpu.SMEM), pl.BlockSpec(memory_space=pltpu.VMEM)
    shapes = [(slots, tokens, columns)] * C + [(C, slots, tokens, columns)] * (len(DISTANCES) - 1)
    return pl.pallas_call(
        project_rest_kernel,
        out_shape=[jax.ShapeDtypeStruct(shape, jnp.bfloat16) for shape in shapes],
        in_specs=[smem] * 3 + [pl.BlockSpec(memory_space=pl.ANY)] * (1 + len(features) + len(weights)),
        out_specs=[vmem] * len(shapes),
        scratch_shapes=[
            pltpu.VMEM((depth, columns), jnp.bfloat16),
            pltpu.VMEM(partial.shape, partial.dtype),
            pltpu.VMEM((layers, tokens, columns), jnp.bfloat16),
            *[pltpu.VMEM(feature.shape, feature.dtype) for feature in features],
            pltpu.SemaphoreType.DMA((len(features),)),
            pltpu.SemaphoreType.DMA((len(REST), WEIGHTS)),
            pltpu.SemaphoreType.DMA((GROUPS,)),
        ],
        compiler_params=pltpu.CompilerParams(vmem_limit_bytes=62 * MIB),
        cost_estimate=pl.CostEstimate(
            flops=2 * layers * tokens * depth * columns, bytes_accessed=11 * MIB, transcendentals=0
        ),
        name="project_rest",
    )(place, blocks, slot_layer, partial, *features, *weights)


def reduce_z(chunks):
    up = [(i, (i + 1) % Z) for i in range(Z)]
    down = [(i, (i - 1) % Z) for i in range(Z)]
    low, high, up3, down3, up2, down2, up1, down1, own = chunks

    def add(left, right):
        return (left.astype(jnp.float32) + right.astype(jnp.float32)).astype(left.dtype)

    rest = [(0, 0)] * low.ndim
    from_below = jnp.pad(lax.ppermute(high, "z", up)[None], [(1, 0), *rest])
    from_above = jnp.pad(lax.ppermute(low, "z", down)[None], [(0, 1), *rest])
    for to_up, to_down in ((up3, down3), (up2, down2), (up1, down1)):
        from_below = lax.ppermute(add(to_up, from_below), "z", up)
        from_above = lax.ppermute(add(to_down, from_above), "z", down)
    return own, from_below, from_above


def combine_kernel(core, own, below, above, kept, given):
    for out, c in ((kept, core[0]), (given, 1 - core[0])):
        total = own[c].astype(jnp.float32) + below[c].astype(jnp.float32) + above[c].astype(jnp.float32)
        out[...] = total.astype(out.dtype)


def combine(c, own, below, above):
    vmem = pl.BlockSpec(memory_space=pltpu.VMEM)
    shape = jax.ShapeDtypeStruct(own.shape[1:], own.dtype)
    return pl.pallas_call(
        combine_kernel,
        out_shape=[shape] * 2,
        in_specs=[pl.BlockSpec(memory_space=pltpu.SMEM)] + [vmem] * 3,
        out_specs=[vmem] * 2,
        cost_estimate=pl.CostEstimate(flops=3 * own.size, bytes_accessed=8 * own.size, transcendentals=0),
        name="combine",
    )(c.reshape(1).astype(jnp.int32), own, below, above)


def finish_kernel(state, hidden, layer_grad, near, across, teacher, teacher_across, out):
    core, count = state[0], state[1]
    slots, quarter, _ = near.shape
    quarters = ((C + core, near), (C + 1 - core, across), (core, teacher), (1 - core, teacher_across))
    for index, ref in quarters:
        rows = pl.ds(pl.multiple_of(index * quarter, quarter), quarter)
        for slot in range(slots):
            value = hidden[slot, rows, :].astype(jnp.float32) - ref[slot].astype(jnp.float32)
            value = jnp.where(slot < count, value, 0.0)
            if slot == 0:
                value = value + layer_grad[rows, :]
            out[slot, rows, :] = value.astype(out.dtype)


def finish(c, own_count, hidden, layer_grad, pieces):
    vmem = pl.BlockSpec(memory_space=pltpu.VMEM)
    return pl.pallas_call(
        finish_kernel,
        out_shape=jax.ShapeDtypeStruct(hidden.shape, hidden.dtype),
        in_specs=[pl.BlockSpec(memory_space=pltpu.SMEM)] + [vmem] * 6,
        out_specs=vmem,
        cost_estimate=pl.CostEstimate(flops=2 * hidden.size, bytes_accessed=8 * hidden.size, transcendentals=0),
        name="finish",
    )(jnp.stack([c, own_count]).astype(jnp.int32), hidden, layer_grad, *pieces)


def gather_tensor(own):
    up = [(i, (i + 1) % X) for i in range(X)]
    down = [(i, (i - 1) % X) for i in range(X)]
    swap = [(0, 1), (1, 0)]
    half = own.shape[0] // 2
    f3 = lax.ppermute(own, "x", up)
    f1 = lax.ppermute(own, "x", down)
    g0 = lax.ppermute(own, "yl", swap)
    f2a = lax.ppermute(f3[:half], "x", up)
    f2b = lax.ppermute(f1[half:], "x", down)
    g3 = lax.ppermute(g0, "x", up)
    g1 = lax.ppermute(g0, "x", down)
    g2a = lax.ppermute(f2a, "yl", swap)
    g2b = lax.ppermute(f2b, "yl", swap)
    return (own, f1, f2a, f2b, f3, g0, g1, g2a, g2b, g3)


def body(
    teacher_slabs,
    proj_weight,
    child_hidden,
    norm_gain,
    key_weight,
    value_weight,
    key_cotangent,
    value_cotangent,
    layer_map,
    layer_counts,
):
    yh, z, c = lax.axis_index("yh"), lax.axis_index("z"), lax.axis_index("c")
    x, yl = lax.axis_index("x"), lax.axis_index("yl")
    slab_count, tokens, slab_width = teacher_slabs.shape
    layers = layer_map.shape[0]
    columns = proj_weight.shape[2]
    full_width = columns * X * YL
    slot_count = child_hidden.shape[0]
    quarter = tokens // QUARTERS

    swap = [(0, 1), (1, 0)]
    ring = YH * YL
    up = [(i, (i + 1) % ring) for i in range(ring)]
    down = [(i, (i - 1) % ring) for i in range(ring)]
    side = ("yh", "yl")
    half_rows = proj_weight.shape[1] // 2
    w_far_a = lax.ppermute(lax.ppermute(proj_weight[:, :half_rows], side, up), side, up)
    w_far_b = lax.ppermute(lax.ppermute(proj_weight[:, half_rows:], side, down), side, down)
    w_sib = lax.ppermute(proj_weight, "c", swap)
    w_fs_a = lax.ppermute(w_far_a, "c", swap)
    w_fs_b = lax.ppermute(w_far_b, "c", swap)
    weights = (proj_weight, w_sib, w_far_a, w_far_b, w_fs_a, w_fs_b)
    place = jnp.stack([2 * yh + c, 2 * yh + 1 - c, 2 * (1 - yh) + c, 2 * (1 - yh) + 1 - c]).astype(jnp.int32)

    is_child = yh == 1
    first_hidden = child_hidden[0].astype(jnp.float32)
    norm_scale = norm_gain[0]
    contract_last = (((1,), (1,)), ((), ()))
    delta_norm = lax.dot_general(
        key_cotangent[0], key_weight[0], contract_last, preferred_element_type=jnp.float32
    )
    delta_norm = delta_norm + lax.dot_general(
        value_cotangent[0], value_weight[0], contract_last, preferred_element_type=jnp.float32
    )
    sums = lax.psum(
        jnp.stack(
            [
                jnp.sum(first_hidden * first_hidden, axis=1),
                jnp.sum(first_hidden * norm_scale * delta_norm, axis=1),
            ]
        ),
        TENSOR,
    )
    squares, inner_sum = sums[0], sums[1]
    inverse_rms = lax.rsqrt(squares / full_width + EPSILON)[:, None]
    normed = (first_hidden * inverse_rms * norm_scale).astype(jnp.bfloat16)
    contract_rows = (((0,), (0,)), ((), ()))
    key_grad = lax.dot_general(
        normed, key_cotangent[0], contract_rows, preferred_element_type=jnp.float32
    ).astype(jnp.bfloat16)
    value_grad = lax.dot_general(
        normed, value_cotangent[0], contract_rows, preferred_element_type=jnp.float32
    ).astype(jnp.bfloat16)
    gain_grad = jnp.sum(first_hidden * inverse_rms * delta_norm, axis=0)
    layer_grad = (
        inverse_rms * norm_scale * delta_norm
        - first_hidden * inverse_rms**3 * inner_sum[:, None] / full_width
    )
    layer_grad = jnp.where(is_child, layer_grad, 0.0)
    sent = lax.ppermute(arrange(teacher_slabs, 1), side, [(0, 3), (1, 2)])
    arranged = jnp.where(yh == 0, arrange(teacher_slabs, 0, (sums,)), sent)
    received = lax.all_to_all(arranged, ("z", "c"), split_axis=0, concat_axis=0, tiled=True)
    received = received.reshape(Z * C * slab_count, YH, quarter, LANES)

    f0, f1, f2a, f2b, f3, g0, g1, g2a, g2b, g3 = gather_tensor(pick(layer_map, received))
    first_blocks, rest_blocks = (
        jnp.stack([(x + step) % X * YL + (yl + yh + other) % YL for step, other in places]).astype(jnp.int32)
        for places in (FIRST, REST)
    )
    prefix_end = jnp.cumsum(layer_counts)
    prefix_start = prefix_end - layer_counts
    slot_layer = jnp.clip(prefix_start[:, None] + jnp.arange(slot_count)[None, :], 0, layers - 1)
    slot_layer = slot_layer.reshape(Z, C * slot_count)[(z + jnp.array(DISTANCES)) % Z].reshape(-1).astype(jnp.int32)
    partial = project_first(place, first_blocks, (f0, f1, f3, g0), weights)
    chunks = project_rest(place, rest_blocks, slot_layer, partial, (f2a, f2b, g1, g2a, g2b, g3), weights)
    kept, given = combine(c, *reduce_z(chunks))
    across = lax.ppermute(given, "c", swap)
    teacher = lax.ppermute(kept, "yh", [(0, 1)])
    teacher_across = lax.ppermute(given, ("yh", "c"), [(0, 3), (1, 2)])
    own_count = jnp.where(is_child, layer_counts[2 * z + c], 0)
    hidden_grad = finish(c, own_count, child_hidden, layer_grad, (kept, across, teacher, teacher_across))
    key_grad = jnp.where(is_child, key_grad, jnp.zeros_like(key_grad))
    value_grad = jnp.where(is_child, value_grad, jnp.zeros_like(value_grad))
    gain_grad = jnp.where(is_child, gain_grad, 0.0)
    return (hidden_grad, key_grad[None], value_grad[None], gain_grad[None])


def solution(mesh):
    fine = Mesh(mesh.devices.reshape(YH, Z, C, X, YL), (*SEGMENT, *TENSOR))
    placed = (
        P(SEGMENT, None, TENSOR),
        P(None, SEGMENT, TENSOR),
        P(SEGMENT, None, TENSOR),
        P(SEGMENT, TENSOR),
        P(SEGMENT, TENSOR, None),
        P(SEGMENT, TENSOR, None),
        P(SEGMENT, None, None),
        P(SEGMENT, None, None),
        P(),
        P(),
    )
    return jax.shard_map(
        body,
        mesh=fine,
        in_specs=placed,
        out_specs=(
            P(SEGMENT, None, TENSOR),
            P(SEGMENT, TENSOR, None),
            P(SEGMENT, TENSOR, None),
            P(SEGMENT, TENSOR),
        ),
        check_vma=False,
    )
```

```python
import functools

import jax
import jax.numpy as jnp
from jax import lax
from jax.experimental import pallas as pl
from jax.experimental.pallas import tpu as pltpu
from jax.sharding import Mesh, PartitionSpec as P

EPSILON = 1e-05
MIB = 1 << 20

SEGMENT = ("yh", "z", "c")
TENSOR = ("x", "yl")
YH, Z, C, X, YL = 2, 8, 2, 4, 2
QUARTERS = YH * C
LANES = 128


def arrange_kernel(slabs, out):
    slab_count, width, _ = slabs.shape
    tokens = width // C
    for c in range(C):
        for z in range(Z):
            for slab in range(slab_count):
                for h in range(YH):
                    lane = (h * Z + z) * LANES
                    row = (slab * YH + h) * tokens
                    out[z * C + c, row : row + tokens, :] = slabs[
                        slab, c * tokens : (c + 1) * tokens, lane : lane + LANES
                    ]


def arrange(teacher_slabs, section):
    slab_count, tokens, width = teacher_slabs.shape
    rows = slab_count * YH * (tokens // QUARTERS)
    shape = jax.ShapeDtypeStruct((Z * C, rows, LANES), teacher_slabs.dtype)
    return pl.pallas_call(
        arrange_kernel,
        grid=(1,),
        out_shape=shape,
        in_specs=[pl.BlockSpec((slab_count, tokens // YH, width), lambda i: (0, section, 0))],
        out_specs=pl.BlockSpec(shape.shape, lambda i: (0, 0, 0)),
        cost_estimate=pl.CostEstimate(flops=0, bytes_accessed=1600000, transcendentals=0),
        name="arrange",
    )(teacher_slabs)


def choose_kernel(count, section, first, second, *refs):
    afters, out, sem, spares = refs[:count], refs[count], refs[count + 1], refs[count + 2 :]
    copies = [
        pltpu.make_async_copy(ref, spare, sem.at[1 + index])
        for index, (ref, spare) in enumerate(zip(afters, spares))
    ]
    for copy in copies:
        copy.start()

    @pl.when(section[0] == 0)
    def _():
        copy = pltpu.make_async_copy(first, out, sem.at[0])
        copy.start()
        copy.wait()

    @pl.when(section[0] != 0)
    def _():
        copy = pltpu.make_async_copy(second, out, sem.at[0])
        copy.start()
        copy.wait()

    for copy in copies:
        copy.wait()


def choose(yh, first, second, after=()):
    after = [array[:1] for array in after]
    return pl.pallas_call(
        functools.partial(choose_kernel, len(after)),
        out_shape=jax.ShapeDtypeStruct(first.shape, first.dtype),
        in_specs=[pl.BlockSpec(memory_space=pltpu.SMEM)] + [pl.BlockSpec(memory_space=pl.ANY)] * (2 + len(after)),
        out_specs=pl.BlockSpec(memory_space=pltpu.VMEM),
        scratch_shapes=[pltpu.SemaphoreType.DMA((1 + len(after),))]
        + [pltpu.VMEM(array.shape, array.dtype) for array in after],
        cost_estimate=pl.CostEstimate(flops=0, bytes_accessed=4 * first.size, transcendentals=0),
        name="choose",
    )(yh.reshape(1).astype(jnp.int32), first, second, *after)


def pick_kernel(layer_map, received, picked, low, high):
    half = low.shape[0]

    def step(layer, carry):
        value = received[layer_map[layer]]
        picked[layer] = value
        low[layer] = value
        value = received[layer_map[half + layer]]
        picked[half + layer] = value
        high[layer] = value
        return carry

    lax.fori_loop(0, half, step, 0)


def pick(layer_map, received):
    layers = layer_map.shape[0]
    shapes = [(count, *received.shape[1:]) for count in (layers, layers // 2, layers // 2)]
    return pl.pallas_call(
        pick_kernel,
        out_shape=[jax.ShapeDtypeStruct(shape, received.dtype) for shape in shapes],
        in_specs=[
            pl.BlockSpec(memory_space=pltpu.SMEM),
            pl.BlockSpec(memory_space=pltpu.VMEM),
        ],
        out_specs=[pl.BlockSpec(memory_space=pltpu.VMEM)] * len(shapes),
        cost_estimate=pl.CostEstimate(flops=0, bytes_accessed=1300000, transcendentals=0),
        name="pick_layers",
    )(layer_map, received)


DISTANCES = (4, 3, -3, 2, -2, 1, -1, 0)
FIRST = ((0, 0), (1, 0), (3, 0), (0, 1))
REST = ((2, 0), (1, 1), (2, 1), (3, 1))
GROUPS = 4


def load_weight(place, blocks, weights, weight, sem):
    piece = weights[0].shape[1]
    copies = []
    for index in range(sem.shape[0]):
        for source, ref in enumerate(weights):
            row = pl.multiple_of(index * QUARTERS * piece + place[source] * piece, piece)
            target = weight.at[pl.ds(row, piece)]
            copies.append(pltpu.make_async_copy(ref.at[blocks[index]], target, sem.at[index, source]))
    for copy in copies:
        copy.start()
    return copies


def load_features(features, held, sem):
    copies = [
        pltpu.make_async_copy(ref, slot, sem.at[index]) for index, (ref, slot) in enumerate(zip(features, held))
    ]
    for copy in copies:
        copy.start()
    return copies


def left_rows(refs, firsts, group):
    _, halves, tokens, lanes = refs[0].shape
    return jnp.concatenate(
        [
            ref[pl.ds(first, group), h].reshape(group * tokens, lanes)
            for ref, first in zip(refs, firsts)
            for h in range(halves)
        ],
        axis=1,
    )


def project_first_kernel(place, blocks, *refs):
    count = len(FIRST) + 2
    features, refs = refs[:count], refs[count:]
    weights, (out, weight, *held, feature_sem, weight_sem) = refs[:QUARTERS], refs[QUARTERS:]
    copies = load_weight(place, blocks, weights, weight, weight_sem) + load_features(features, held, feature_sem)
    for copy in copies:
        copy.wait()
    own, up_a, up_b, down_a, down_b, row = held
    group = own.shape[0] // GROUPS
    for number in range(GROUPS):
        first = number * group
        side = number // (GROUPS // 2)
        offset = (number - side * (GROUPS // 2)) * group
        refs = (own, (up_a, up_b)[side], (down_a, down_b)[side], row)
        left = left_rows(refs, (first, offset, offset, first), group)
        out[number] = jnp.dot(left, weight[...], preferred_element_type=jnp.float32).astype(out.dtype)


def project_rest_kernel(place, blocks, slot_layer, partial, *refs):
    count = len(REST) + 2
    features, refs = refs[:count], refs[count:]
    weights, refs = refs[:QUARTERS], refs[QUARTERS:]
    outs, refs = refs[: len(DISTANCES) + 1], refs[len(DISTANCES) + 1 :]
    weight, before, product, *held, feature_sem, weight_sem, before_sem = refs
    copies = load_weight(place, blocks, weights, weight, weight_sem) + load_features(features, held, feature_sem)
    befores = [
        pltpu.make_async_copy(partial.at[number], before.at[number], before_sem.at[number]) for number in range(GROUPS)
    ]
    for copy in befores:
        copy.start()
    for copy in copies:
        copy.wait()
    layers, halves, tokens, lanes = features[2].shape
    group = layers // GROUPS
    near_a, near_b, row_1, row_2a, row_2b, row_3 = held
    for number in range(GROUPS):
        first = number * group
        side = number // (GROUPS // 2)
        offset = (number - side * (GROUPS // 2)) * group
        refs = ((near_a, near_b)[side], row_1, (row_2a, row_2b)[side], row_3)
        left = left_rows(refs, (offset, first, offset, first), group)
        value = jnp.dot(left, weight[...], preferred_element_type=jnp.float32)
        befores[number].wait()
        value = (value + before[number].astype(jnp.float32)).astype(product.dtype)
        product[pl.ds(first, group)] = value.reshape(group, tokens, value.shape[1])
    slots = outs[-1].shape[1]
    for index, out in enumerate(outs):
        chunk = max(index - 1, 0)
        for c in range(C):
            for slot in range(slots):
                value = product[slot_layer[(chunk * C + c) * slots + slot]]
                if index > 1:
                    out[c, slot] = value
                elif index == c:
                    out[slot] = value


def project_first(place, blocks, features, weights):
    layers, halves, tokens, lanes = features[0].shape
    columns = weights[0].shape[2]
    depth = len(FIRST) * halves * lanes
    shape = (GROUPS, layers * tokens // GROUPS, columns)
    smem, anywhere = pl.BlockSpec(memory_space=pltpu.SMEM), pl.BlockSpec(memory_space=pltpu.HBM)
    return pl.pallas_call(
        project_first_kernel,
        out_shape=jax.ShapeDtypeStruct(shape, jnp.bfloat16),
        in_specs=[smem] * 2 + [anywhere] * (len(features) + len(weights)),
        out_specs=pl.BlockSpec(memory_space=pltpu.VMEM),
        scratch_shapes=[
            pltpu.VMEM((depth, columns), jnp.bfloat16),
            *[pltpu.VMEM(feature.shape, feature.dtype) for feature in features],
            pltpu.SemaphoreType.DMA((len(features),)),
            pltpu.SemaphoreType.DMA((len(FIRST), QUARTERS)),
        ],
        compiler_params=pltpu.CompilerParams(vmem_limit_bytes=40 * MIB),
        cost_estimate=pl.CostEstimate(
            flops=2 * layers * tokens * depth * columns, bytes_accessed=8 * MIB, transcendentals=0
        ),
        name="project_first",
    )(place, blocks, *features, *weights)


def project_rest(place, blocks, slot_layer, partial, features, weights):
    layers, halves, tokens, lanes = features[2].shape
    columns = weights[0].shape[2]
    depth = len(REST) * halves * lanes
    slots = slot_layer.shape[0] // (len(DISTANCES) * C)
    smem, vmem = pl.BlockSpec(memory_space=pltpu.SMEM), pl.BlockSpec(memory_space=pltpu.VMEM)
    shapes = [(slots, tokens, columns)] * C + [(C, slots, tokens, columns)] * (len(DISTANCES) - 1)
    return pl.pallas_call(
        project_rest_kernel,
        out_shape=[jax.ShapeDtypeStruct(shape, jnp.bfloat16) for shape in shapes],
        in_specs=[smem] * 3 + [pl.BlockSpec(memory_space=pltpu.HBM)] * (1 + len(features) + len(weights)),
        out_specs=[vmem] * len(shapes),
        scratch_shapes=[
            pltpu.VMEM((depth, columns), jnp.bfloat16),
            pltpu.VMEM(partial.shape, partial.dtype),
            pltpu.VMEM((layers, tokens, columns), jnp.bfloat16),
            *[pltpu.VMEM(feature.shape, feature.dtype) for feature in features],
            pltpu.SemaphoreType.DMA((len(features),)),
            pltpu.SemaphoreType.DMA((len(REST), QUARTERS)),
            pltpu.SemaphoreType.DMA((GROUPS,)),
        ],
        compiler_params=pltpu.CompilerParams(vmem_limit_bytes=62 * MIB),
        cost_estimate=pl.CostEstimate(
            flops=2 * layers * tokens * depth * columns, bytes_accessed=11 * MIB, transcendentals=0
        ),
        name="project_rest",
    )(place, blocks, slot_layer, partial, *features, *weights)


def reduce_z(chunks):
    up = [(i, (i + 1) % Z) for i in range(Z)]
    down = [(i, (i - 1) % Z) for i in range(Z)]
    low, high, up3, down3, up2, down2, up1, down1, own = chunks

    def add(left, right):
        return (left.astype(jnp.float32) + right.astype(jnp.float32)).astype(left.dtype)

    rest = [(0, 0)] * low.ndim
    from_below = jnp.pad(lax.ppermute(high, "z", up)[None], [(1, 0), *rest])
    from_above = jnp.pad(lax.ppermute(low, "z", down)[None], [(0, 1), *rest])
    for to_up, to_down in ((up3, down3), (up2, down2), (up1, down1)):
        from_below = lax.ppermute(add(to_up, from_below), "z", up)
        from_above = lax.ppermute(add(to_down, from_above), "z", down)
    return own, from_below, from_above


def combine_kernel(core, own, below, above, kept, given):
    for out, c in ((kept, core[0]), (given, 1 - core[0])):
        total = own[c].astype(jnp.float32) + below[c].astype(jnp.float32) + above[c].astype(jnp.float32)
        out[...] = total.astype(out.dtype)


def combine(c, own, below, above):
    vmem = pl.BlockSpec(memory_space=pltpu.VMEM)
    shape = jax.ShapeDtypeStruct(own.shape[1:], own.dtype)
    return pl.pallas_call(
        combine_kernel,
        out_shape=[shape] * 2,
        in_specs=[pl.BlockSpec(memory_space=pltpu.SMEM)] + [vmem] * 3,
        out_specs=[vmem] * 2,
        cost_estimate=pl.CostEstimate(flops=3 * own.size, bytes_accessed=8 * own.size, transcendentals=0),
        name="combine",
    )(c.reshape(1).astype(jnp.int32), own, below, above)


def finish_kernel(state, hidden, layer_grad, near, across, teacher, teacher_across, out):
    core, count = state[0], state[1]
    slots, quarter, _ = near.shape
    quarters = ((C + core, near), (C + 1 - core, across), (core, teacher), (1 - core, teacher_across))
    for index, ref in quarters:
        rows = pl.ds(pl.multiple_of(index * quarter, quarter), quarter)
        for slot in range(slots):
            value = hidden[slot, rows, :].astype(jnp.float32) - ref[slot].astype(jnp.float32)
            value = jnp.where(slot < count, value, 0.0)
            if slot == 0:
                value = value + layer_grad[rows, :]
            out[slot, rows, :] = value.astype(out.dtype)


def finish(c, own_count, hidden, layer_grad, pieces):
    vmem = pl.BlockSpec(memory_space=pltpu.VMEM)
    return pl.pallas_call(
        finish_kernel,
        out_shape=jax.ShapeDtypeStruct(hidden.shape, hidden.dtype),
        in_specs=[pl.BlockSpec(memory_space=pltpu.SMEM)] + [vmem] * 6,
        out_specs=vmem,
        cost_estimate=pl.CostEstimate(flops=2 * hidden.size, bytes_accessed=8 * hidden.size, transcendentals=0),
        name="finish",
    )(jnp.stack([c, own_count]).astype(jnp.int32), hidden, layer_grad, *pieces)


def gather_tensor(own, low, high):
    up = [(i, (i + 1) % X) for i in range(X)]
    down = [(i, (i - 1) % X) for i in range(X)]
    swap = [(0, 1), (1, 0)]
    f3a = lax.ppermute(low, "x", up)
    f1b = lax.ppermute(high, "x", down)
    g0 = lax.ppermute(own, "yl", swap)
    f3b = lax.ppermute(high, "x", up)
    f1a = lax.ppermute(low, "x", down)
    f2a = lax.ppermute(f3a, "x", up)
    f2b = lax.ppermute(f1b, "x", down)
    g3 = lax.ppermute(g0, "x", up)
    g1 = lax.ppermute(g0, "x", down)
    g2a = lax.ppermute(f2a, "yl", swap)
    g2b = lax.ppermute(f2b, "yl", swap)
    return (own, f1a, f1b, f3a, f3b, g0), (f2a, f2b, g1, g2a, g2b, g3)


def body(
    teacher_slabs,
    proj_weight,
    child_hidden,
    norm_gain,
    key_weight,
    value_weight,
    key_cotangent,
    value_cotangent,
    layer_map,
    layer_counts,
):
    yh, z, c = lax.axis_index("yh"), lax.axis_index("z"), lax.axis_index("c")
    x, yl = lax.axis_index("x"), lax.axis_index("yl")
    slab_count, tokens, slab_width = teacher_slabs.shape
    layers = layer_map.shape[0]
    columns = proj_weight.shape[2]
    full_width = columns * X * YL
    slot_count = child_hidden.shape[0]
    quarter = tokens // QUARTERS

    swap = [(0, 1), (1, 0)]
    side = ("yh", "yl")
    across_y = [(0, 3), (1, 2)]
    w_row = lax.ppermute(proj_weight, side, [(0, 1), (1, 0)])
    w_child = lax.ppermute(proj_weight, side, [(3, 0), (2, 1)])
    w_teacher = lax.ppermute(w_row, side, across_y)
    w_near = choose(yh, w_row, proj_weight)
    place = jnp.stack([2 * yh + c, 2 * yh + 1 - c, 2 * (1 - yh) + c, 2 * (1 - yh) + 1 - c]).astype(jnp.int32)

    is_child = yh == 1
    first_hidden = child_hidden[0].astype(jnp.float32)
    norm_scale = norm_gain[0]
    contract_last = (((1,), (1,)), ((), ()))
    delta_norm = lax.dot_general(
        key_cotangent[0], key_weight[0], contract_last, preferred_element_type=jnp.float32
    )
    delta_norm = delta_norm + lax.dot_general(
        value_cotangent[0], value_weight[0], contract_last, preferred_element_type=jnp.float32
    )
    sums = lax.psum(
        jnp.stack(
            [
                jnp.sum(first_hidden * first_hidden, axis=1),
                jnp.sum(first_hidden * norm_scale * delta_norm, axis=1),
            ]
        ),
        TENSOR,
    )
    squares, inner_sum = sums[0], sums[1]
    inverse_rms = lax.rsqrt(squares / full_width + EPSILON)[:, None]
    normed = (first_hidden * inverse_rms * norm_scale).astype(jnp.bfloat16)
    contract_rows = (((0,), (0,)), ((), ()))
    key_grad = lax.dot_general(
        normed, key_cotangent[0], contract_rows, preferred_element_type=jnp.float32
    ).astype(jnp.bfloat16)
    value_grad = lax.dot_general(
        normed, value_cotangent[0], contract_rows, preferred_element_type=jnp.float32
    ).astype(jnp.bfloat16)
    gain_grad = jnp.sum(first_hidden * inverse_rms * delta_norm, axis=0)
    layer_grad = (
        inverse_rms * norm_scale * delta_norm
        - first_hidden * inverse_rms**3 * inner_sum[:, None] / full_width
    )
    layer_grad = jnp.where(is_child, layer_grad, 0.0)
    sent = lax.ppermute(arrange(teacher_slabs, 1), side, across_y)
    arranged = choose(yh, arrange(teacher_slabs, 0), sent, (sums, w_row))
    received = lax.all_to_all(arranged, ("z", "c"), split_axis=0, concat_axis=0, tiled=True)
    received = received.reshape(Z * C * slab_count, YH, quarter, LANES)

    picked, low, high = pick(layer_map, received)
    w_far = choose(yh, w_child, w_teacher, (low,))
    weights = (w_near, lax.ppermute(w_near, "c", swap), w_far, lax.ppermute(w_far, "c", swap))
    first_features, rest_features = gather_tensor(picked, low, high)
    first_blocks, rest_blocks = (
        jnp.stack([(x + step) % X * YL + (yl + yh + other) % YL for step, other in places]).astype(jnp.int32)
        for places in (FIRST, REST)
    )
    prefix_end = jnp.cumsum(layer_counts)
    prefix_start = prefix_end - layer_counts
    slot_layer = jnp.clip(prefix_start[:, None] + jnp.arange(slot_count)[None, :], 0, layers - 1)
    slot_layer = slot_layer.reshape(Z, C * slot_count)[(z + jnp.array(DISTANCES)) % Z].reshape(-1).astype(jnp.int32)
    partial = project_first(place, first_blocks, first_features, weights)
    chunks = project_rest(place, rest_blocks, slot_layer, partial, rest_features, weights)
    kept, given = combine(c, *reduce_z(chunks))
    across = lax.ppermute(given, "c", swap)
    teacher = lax.ppermute(kept, side, across_y)
    teacher_across = lax.ppermute(given, ("yh", "c", "yl"), [(0, 7), (1, 6), (2, 5), (3, 4)])
    own_count = jnp.where(is_child, layer_counts[2 * z + c], 0)
    hidden_grad = finish(c, own_count, child_hidden, layer_grad, (kept, across, teacher, teacher_across))
    key_grad = jnp.where(is_child, key_grad, jnp.zeros_like(key_grad))
    value_grad = jnp.where(is_child, value_grad, jnp.zeros_like(value_grad))
    gain_grad = jnp.where(is_child, gain_grad, 0.0)
    return (hidden_grad, key_grad[None], value_grad[None], gain_grad[None])


def solution(mesh):
    fine = Mesh(mesh.devices.reshape(YH, Z, C, X, YL), (*SEGMENT, *TENSOR))
    placed = (
        P(SEGMENT, None, TENSOR),
        P(None, SEGMENT, TENSOR),
        P(SEGMENT, None, TENSOR),
        P(SEGMENT, TENSOR),
        P(SEGMENT, TENSOR, None),
        P(SEGMENT, TENSOR, None),
        P(SEGMENT, None, None),
        P(SEGMENT, None, None),
        P(),
        P(),
    )
    return jax.shard_map(
        body,
        mesh=fine,
        in_specs=placed,
        out_specs=(
            P(SEGMENT, None, TENSOR),
            P(SEGMENT, TENSOR, None),
            P(SEGMENT, TENSOR, None),
            P(SEGMENT, TENSOR),
        ),
        check_vma=False,
    )
```

```python
import jax
import jax.numpy as jnp
from jax import lax
from jax.experimental import pallas as pl
from jax.experimental.pallas import tpu as pltpu
from jax.sharding import Mesh, PartitionSpec as P

EPSILON = 1e-05
MIB = 1 << 20

SEGMENT = ("yh", "z", "c")
TENSOR = ("x", "yl")
YH, Z, C, X, YL = 2, 8, 2, 4, 2
QUARTERS = YH * C
LANES = 128


def arrange_kernel(slabs, out):
    slab_count, width, _ = slabs.shape
    tokens = width // C
    for c in range(C):
        for z in range(Z):
            for slab in range(slab_count):
                for h in range(YH):
                    lane = (h * Z + z) * LANES
                    row = (slab * YH + h) * tokens
                    out[z * C + c, row : row + tokens, :] = slabs[
                        slab, c * tokens : (c + 1) * tokens, lane : lane + LANES
                    ]


def arrange(teacher_slabs, section):
    slab_count, tokens, width = teacher_slabs.shape
    rows = slab_count * YH * (tokens // QUARTERS)
    shape = jax.ShapeDtypeStruct((Z * C, rows, LANES), teacher_slabs.dtype)
    return pl.pallas_call(
        arrange_kernel,
        grid=(1,),
        out_shape=shape,
        in_specs=[pl.BlockSpec((slab_count, tokens // YH, width), lambda i: (0, section, 0))],
        out_specs=pl.BlockSpec(shape.shape, lambda i: (0, 0, 0)),
        cost_estimate=pl.CostEstimate(flops=0, bytes_accessed=1600000, transcendentals=0),
        name="arrange",
    )(teacher_slabs)


def pick_kernel(layer_map, received, picked, low, high):
    half = low.shape[0]

    def step(layer, carry):
        value = received[layer_map[layer]]
        picked[layer] = value
        low[layer] = value
        value = received[layer_map[half + layer]]
        picked[half + layer] = value
        high[layer] = value
        return carry

    lax.fori_loop(0, half, step, 0)


def pick(layer_map, received):
    layers = layer_map.shape[0]
    shapes = [(count, *received.shape[1:]) for count in (layers, layers // 2, layers // 2)]
    return pl.pallas_call(
        pick_kernel,
        out_shape=[jax.ShapeDtypeStruct(shape, received.dtype) for shape in shapes],
        in_specs=[
            pl.BlockSpec(memory_space=pltpu.SMEM),
            pl.BlockSpec(memory_space=pltpu.VMEM),
        ],
        out_specs=[pl.BlockSpec(memory_space=pltpu.VMEM)] * len(shapes),
        cost_estimate=pl.CostEstimate(flops=0, bytes_accessed=1300000, transcendentals=0),
        name="pick_layers",
    )(layer_map, received)


DISTANCES = (4, 3, -3, 2, -2, 1, -1, 0)
FIRST = ((0, 0), (1, 0), (3, 0), (0, 1))
REST = ((2, 0), (1, 1), (2, 1), (3, 1))
GROUPS = 4


def load_weight(place, blocks, weights, weight, sem):
    piece = weights[0].shape[1]
    copies = []
    for index in range(sem.shape[0]):
        for source, ref in enumerate(weights):
            row = pl.multiple_of(index * QUARTERS * piece + place[source] * piece, piece)
            target = weight.at[pl.ds(row, piece)]
            copies.append(pltpu.make_async_copy(ref.at[blocks[index]], target, sem.at[index, source]))
    for copy in copies:
        copy.start()
    return copies


def load_features(features, held, sem):
    copies = [
        pltpu.make_async_copy(ref, slot, sem.at[index]) for index, (ref, slot) in enumerate(zip(features, held))
    ]
    for copy in copies:
        copy.start()
    return copies


def left_rows(refs, firsts, group):
    _, halves, tokens, lanes = refs[0].shape
    return jnp.concatenate(
        [
            ref[pl.ds(first, group), h].reshape(group * tokens, lanes)
            for ref, first in zip(refs, firsts)
            for h in range(halves)
        ],
        axis=1,
    )


def project_first_kernel(place, blocks, *refs):
    count = len(FIRST) + 2
    features, refs = refs[:count], refs[count:]
    weights, (out, weight, *held, feature_sem, weight_sem) = refs[:QUARTERS], refs[QUARTERS:]
    copies = load_weight(place, blocks, weights, weight, weight_sem) + load_features(features, held, feature_sem)
    for copy in copies:
        copy.wait()
    own, up_a, up_b, down_a, down_b, row = held
    group = own.shape[0] // GROUPS
    for number in range(GROUPS):
        first = number * group
        side = number // (GROUPS // 2)
        offset = (number - side * (GROUPS // 2)) * group
        refs = (own, (up_a, up_b)[side], (down_a, down_b)[side], row)
        left = left_rows(refs, (first, offset, offset, first), group)
        out[number] = jnp.dot(left, weight[...], preferred_element_type=jnp.float32).astype(out.dtype)


def project_rest_kernel(place, blocks, slot_layer, partial, *refs):
    count = len(REST) + 2
    features, refs = refs[:count], refs[count:]
    weights, refs = refs[:QUARTERS], refs[QUARTERS:]
    outs, refs = refs[: len(DISTANCES) + 1], refs[len(DISTANCES) + 1 :]
    weight, before, product, *held, feature_sem, weight_sem, before_sem = refs
    copies = load_weight(place, blocks, weights, weight, weight_sem) + load_features(features, held, feature_sem)
    befores = [
        pltpu.make_async_copy(partial.at[number], before.at[number], before_sem.at[number]) for number in range(GROUPS)
    ]
    for copy in befores:
        copy.start()
    for copy in copies:
        copy.wait()
    layers, halves, tokens, lanes = features[2].shape
    group = layers // GROUPS
    near_a, near_b, row_1, row_2a, row_2b, row_3 = held
    for number in range(GROUPS):
        first = number * group
        side = number // (GROUPS // 2)
        offset = (number - side * (GROUPS // 2)) * group
        refs = ((near_a, near_b)[side], row_1, (row_2a, row_2b)[side], row_3)
        left = left_rows(refs, (offset, first, offset, first), group)
        value = jnp.dot(left, weight[...], preferred_element_type=jnp.float32)
        befores[number].wait()
        value = (value + before[number].astype(jnp.float32)).astype(product.dtype)
        product[pl.ds(first, group)] = value.reshape(group, tokens, value.shape[1])
    slots = outs[-1].shape[1]
    for index, out in enumerate(outs):
        chunk = max(index - 1, 0)
        for c in range(C):
            for slot in range(slots):
                value = product[slot_layer[(chunk * C + c) * slots + slot]]
                if index > 1:
                    out[c, slot] = value
                elif index == c:
                    out[slot] = value


def project_first(place, blocks, features, weights):
    layers, halves, tokens, lanes = features[0].shape
    columns = weights[0].shape[2]
    depth = len(FIRST) * halves * lanes
    shape = (GROUPS, layers * tokens // GROUPS, columns)
    smem, anywhere = pl.BlockSpec(memory_space=pltpu.SMEM), pl.BlockSpec(memory_space=pltpu.HBM)
    return pl.pallas_call(
        project_first_kernel,
        out_shape=jax.ShapeDtypeStruct(shape, jnp.bfloat16),
        in_specs=[smem] * 2 + [anywhere] * (len(features) + len(weights)),
        out_specs=pl.BlockSpec(memory_space=pltpu.VMEM),
        scratch_shapes=[
            pltpu.VMEM((depth, columns), jnp.bfloat16),
            *[pltpu.VMEM(feature.shape, feature.dtype) for feature in features],
            pltpu.SemaphoreType.DMA((len(features),)),
            pltpu.SemaphoreType.DMA((len(FIRST), QUARTERS)),
        ],
        compiler_params=pltpu.CompilerParams(vmem_limit_bytes=40 * MIB),
        cost_estimate=pl.CostEstimate(
            flops=2 * layers * tokens * depth * columns, bytes_accessed=8 * MIB, transcendentals=0
        ),
        name="project_first",
    )(place, blocks, *features, *weights)


def project_rest(place, blocks, slot_layer, partial, features, weights):
    layers, halves, tokens, lanes = features[2].shape
    columns = weights[0].shape[2]
    depth = len(REST) * halves * lanes
    slots = slot_layer.shape[0] // (len(DISTANCES) * C)
    smem, vmem = pl.BlockSpec(memory_space=pltpu.SMEM), pl.BlockSpec(memory_space=pltpu.VMEM)
    shapes = [(slots, tokens, columns)] * C + [(C, slots, tokens, columns)] * (len(DISTANCES) - 1)
    return pl.pallas_call(
        project_rest_kernel,
        out_shape=[jax.ShapeDtypeStruct(shape, jnp.bfloat16) for shape in shapes],
        in_specs=[smem] * 3 + [pl.BlockSpec(memory_space=pltpu.HBM)] * (1 + len(features) + len(weights)),
        out_specs=[vmem] * len(shapes),
        scratch_shapes=[
            pltpu.VMEM((depth, columns), jnp.bfloat16),
            pltpu.VMEM(partial.shape, partial.dtype),
            pltpu.VMEM((layers, tokens, columns), jnp.bfloat16),
            *[pltpu.VMEM(feature.shape, feature.dtype) for feature in features],
            pltpu.SemaphoreType.DMA((len(features),)),
            pltpu.SemaphoreType.DMA((len(REST), QUARTERS)),
            pltpu.SemaphoreType.DMA((GROUPS,)),
        ],
        compiler_params=pltpu.CompilerParams(vmem_limit_bytes=62 * MIB),
        cost_estimate=pl.CostEstimate(
            flops=2 * layers * tokens * depth * columns, bytes_accessed=11 * MIB, transcendentals=0
        ),
        name="project_rest",
    )(place, blocks, slot_layer, partial, *features, *weights)


def reduce_z(chunks):
    up = [(i, (i + 1) % Z) for i in range(Z)]
    down = [(i, (i - 1) % Z) for i in range(Z)]
    low, high, up3, down3, up2, down2, up1, down1, own = chunks

    def add(left, right):
        return (left.astype(jnp.float32) + right.astype(jnp.float32)).astype(left.dtype)

    rest = [(0, 0)] * low.ndim
    from_below = jnp.pad(lax.ppermute(high, "z", up)[None], [(1, 0), *rest])
    from_above = jnp.pad(lax.ppermute(low, "z", down)[None], [(0, 1), *rest])
    for to_up, to_down in ((up3, down3), (up2, down2), (up1, down1)):
        from_below = lax.ppermute(add(to_up, from_below), "z", up)
        from_above = lax.ppermute(add(to_down, from_above), "z", down)
    return own, from_below, from_above


def combine_kernel(core, own, below, above, kept, given):
    for out, c in ((kept, core[0]), (given, 1 - core[0])):
        total = own[c].astype(jnp.float32) + below[c].astype(jnp.float32) + above[c].astype(jnp.float32)
        out[...] = total.astype(out.dtype)


def combine(c, own, below, above):
    vmem = pl.BlockSpec(memory_space=pltpu.VMEM)
    shape = jax.ShapeDtypeStruct(own.shape[1:], own.dtype)
    return pl.pallas_call(
        combine_kernel,
        out_shape=[shape] * 2,
        in_specs=[pl.BlockSpec(memory_space=pltpu.SMEM)] + [vmem] * 3,
        out_specs=[vmem] * 2,
        cost_estimate=pl.CostEstimate(flops=3 * own.size, bytes_accessed=8 * own.size, transcendentals=0),
        name="combine",
    )(c.reshape(1).astype(jnp.int32), own, below, above)


def finish_kernel(state, hidden, layer_grad, near, across, teacher, teacher_across, out):
    core, count = state[0], state[1]
    slots, quarter, _ = near.shape
    quarters = ((C + core, near), (C + 1 - core, across), (core, teacher), (1 - core, teacher_across))
    for index, ref in quarters:
        rows = pl.ds(pl.multiple_of(index * quarter, quarter), quarter)
        for slot in range(slots):
            value = hidden[slot, rows, :].astype(jnp.float32) - ref[slot].astype(jnp.float32)
            value = jnp.where(slot < count, value, 0.0)
            if slot == 0:
                value = value + layer_grad[rows, :]
            out[slot, rows, :] = value.astype(out.dtype)


def finish(c, own_count, hidden, layer_grad, pieces):
    vmem = pl.BlockSpec(memory_space=pltpu.VMEM)
    return pl.pallas_call(
        finish_kernel,
        out_shape=jax.ShapeDtypeStruct(hidden.shape, hidden.dtype),
        in_specs=[pl.BlockSpec(memory_space=pltpu.SMEM)] + [vmem] * 6,
        out_specs=vmem,
        cost_estimate=pl.CostEstimate(flops=2 * hidden.size, bytes_accessed=8 * hidden.size, transcendentals=0),
        name="finish",
    )(jnp.stack([c, own_count]).astype(jnp.int32), hidden, layer_grad, *pieces)


def gather_tensor(own, low, high, before):
    up = [(i, (i + 1) % X) for i in range(X)]
    down = [(i, (i - 1) % X) for i in range(X)]
    swap = [(0, 1), (1, 0)]
    f3a = lax.ppermute(low, "x", up)
    f1b = lax.ppermute(high, "x", down)
    g0 = lax.ppermute(own, "yl", swap)
    f3b = lax.ppermute(high, "x", up)
    f1a = lax.ppermute(low, "x", down)
    f3a, _ = lax.optimization_barrier((f3a, before))
    f2a = lax.ppermute(f3a, "x", up)
    f2b = lax.ppermute(f1b, "x", down)
    g3 = lax.ppermute(g0, "x", up)
    g1 = lax.ppermute(g0, "x", down)
    g2a = lax.ppermute(f2a, "yl", swap)
    g2b = lax.ppermute(f2b, "yl", swap)
    return (own, f1a, f1b, f3a, f3b, g0), (f2a, f2b, g1, g2a, g2b, g3)


def body(
    teacher_slabs,
    proj_weight,
    child_hidden,
    norm_gain,
    key_weight,
    value_weight,
    key_cotangent,
    value_cotangent,
    layer_map,
    layer_counts,
):
    yh, z, c = lax.axis_index("yh"), lax.axis_index("z"), lax.axis_index("c")
    x, yl = lax.axis_index("x"), lax.axis_index("yl")
    slab_count, tokens, slab_width = teacher_slabs.shape
    layers = layer_map.shape[0]
    columns = proj_weight.shape[2]
    full_width = columns * X * YL
    slot_count = child_hidden.shape[0]
    quarter = tokens // QUARTERS

    swap = [(0, 1), (1, 0)]
    side = ("yh", "yl")
    w_sib = lax.ppermute(proj_weight, "c", swap)
    w_row = lax.ppermute(proj_weight, "yl", swap)
    place = jnp.stack([2 * yh + c, 2 * yh + 1 - c, 2 * (1 - yh) + c, 2 * (1 - yh) + 1 - c]).astype(jnp.int32)

    is_child = yh == 1
    first_hidden = child_hidden[0].astype(jnp.float32)
    norm_scale = norm_gain[0]
    contract_last = (((1,), (1,)), ((), ()))
    delta_norm = lax.dot_general(
        key_cotangent[0], key_weight[0], contract_last, preferred_element_type=jnp.float32
    )
    delta_norm = delta_norm + lax.dot_general(
        value_cotangent[0], value_weight[0], contract_last, preferred_element_type=jnp.float32
    )
    sums = jnp.stack(
        [
            jnp.sum(first_hidden * first_hidden, axis=1),
            jnp.sum(first_hidden * norm_scale * delta_norm, axis=1),
        ]
    )
    sums = sums + lax.ppermute(sums, "x", [(i, i ^ 1) for i in range(X)])
    sums = sums + lax.ppermute(sums, "x", [(i, i ^ 2) for i in range(X)])
    sums = sums + lax.ppermute(sums, "yl", swap)
    sent = lax.ppermute(arrange(teacher_slabs, 1), side, [(0, 3), (1, 2)])
    w_row, _ = lax.optimization_barrier((w_row, sent))
    w_far = lax.ppermute(w_row, side, [(0, 3), (3, 0), (1, 2), (2, 1)])
    arranged = jnp.where(yh == 0, arrange(teacher_slabs, 0), sent)
    arranged, w_sib, sums = lax.optimization_barrier((arranged, w_sib, sums))
    received = lax.all_to_all(arranged, ("z", "c"), split_axis=0, concat_axis=0, tiled=True)
    received = received.reshape(Z * C * slab_count, YH, quarter, LANES)

    received, w_far = lax.optimization_barrier((received, w_far))
    w_far_sib = lax.ppermute(w_far, "c", swap)
    weights = (proj_weight, w_sib, w_far, w_far_sib)
    first_features, rest_features = gather_tensor(*pick(layer_map, received), w_far_sib)
    squares, inner_sum = sums[0], sums[1]
    inverse_rms = lax.rsqrt(squares / full_width + EPSILON)[:, None]
    normed = (first_hidden * inverse_rms * norm_scale).astype(jnp.bfloat16)
    contract_rows = (((0,), (0,)), ((), ()))
    key_grad = lax.dot_general(
        normed, key_cotangent[0], contract_rows, preferred_element_type=jnp.float32
    ).astype(jnp.bfloat16)
    value_grad = lax.dot_general(
        normed, value_cotangent[0], contract_rows, preferred_element_type=jnp.float32
    ).astype(jnp.bfloat16)
    gain_grad = jnp.sum(first_hidden * inverse_rms * delta_norm, axis=0)
    layer_grad = (
        inverse_rms * norm_scale * delta_norm
        - first_hidden * inverse_rms**3 * inner_sum[:, None] / full_width
    )
    layer_grad = jnp.where(is_child, layer_grad, 0.0)
    first_blocks, rest_blocks = (
        jnp.stack([(x + step) % X * YL + (yl + yh + other) % YL for step, other in places]).astype(jnp.int32)
        for places in (FIRST, REST)
    )
    prefix_end = jnp.cumsum(layer_counts)
    prefix_start = prefix_end - layer_counts
    slot_layer = jnp.clip(prefix_start[:, None] + jnp.arange(slot_count)[None, :], 0, layers - 1)
    slot_layer = slot_layer.reshape(Z, C * slot_count)[(z + jnp.array(DISTANCES)) % Z].reshape(-1).astype(jnp.int32)
    partial = project_first(place, first_blocks, first_features, weights)
    chunks = project_rest(place, rest_blocks, slot_layer, partial, rest_features, weights)
    kept, given = combine(c, *reduce_z(chunks))
    across = lax.ppermute(given, "c", swap)
    teacher = lax.ppermute(kept, "yh", [(0, 1)])
    teacher_across = lax.ppermute(given, ("yh", "c"), [(0, 3), (1, 2)])
    own_count = jnp.where(is_child, layer_counts[2 * z + c], 0)
    hidden_grad = finish(c, own_count, child_hidden, layer_grad, (kept, across, teacher, teacher_across))
    key_grad = jnp.where(is_child, key_grad, jnp.zeros_like(key_grad))
    value_grad = jnp.where(is_child, value_grad, jnp.zeros_like(value_grad))
    gain_grad = jnp.where(is_child, gain_grad, 0.0)
    return (hidden_grad, key_grad[None], value_grad[None], gain_grad[None])


def solution(mesh):
    fine = Mesh(mesh.devices.reshape(YH, Z, C, X, YL), (*SEGMENT, *TENSOR))
    placed = (
        P(SEGMENT, None, TENSOR),
        P(None, SEGMENT, TENSOR),
        P(SEGMENT, None, TENSOR),
        P(SEGMENT, TENSOR),
        P(SEGMENT, TENSOR, None),
        P(SEGMENT, TENSOR, None),
        P(SEGMENT, None, None),
        P(SEGMENT, None, None),
        P(),
        P(),
    )
    return jax.shard_map(
        body,
        mesh=fine,
        in_specs=placed,
        out_specs=(
            P(SEGMENT, None, TENSOR),
            P(SEGMENT, TENSOR, None),
            P(SEGMENT, TENSOR, None),
            P(SEGMENT, TENSOR),
        ),
        check_vma=False,
    )
```

```python
import jax
import jax.numpy as jnp
from jax import lax
from jax.experimental import pallas as pl
from jax.experimental.pallas import tpu as pltpu
from jax.sharding import Mesh, PartitionSpec as P

EPSILON = 1e-05
MIB = 1 << 20

SEGMENT = ("yh", "z", "c")
TENSOR = ("x", "yl")
YH, Z, C, X, YL = 2, 8, 2, 4, 2
QUARTERS = YH * C
LANES = 128


def arrange_kernel(slabs, out):
    slab_count, width, _ = slabs.shape
    tokens = width // C
    for c in range(C):
        for z in range(Z):
            for slab in range(slab_count):
                for h in range(YH):
                    lane = (h * Z + z) * LANES
                    row = (slab * YH + h) * tokens
                    out[z * C + c, row : row + tokens, :] = slabs[
                        slab, c * tokens : (c + 1) * tokens, lane : lane + LANES
                    ]


def arrange(teacher_slabs, section):
    slab_count, tokens, width = teacher_slabs.shape
    rows = slab_count * YH * (tokens // QUARTERS)
    shape = jax.ShapeDtypeStruct((Z * C, rows, LANES), teacher_slabs.dtype)
    return pl.pallas_call(
        arrange_kernel,
        grid=(1,),
        out_shape=shape,
        in_specs=[pl.BlockSpec((slab_count, tokens // YH, width), lambda i: (0, section, 0))],
        out_specs=pl.BlockSpec(shape.shape, lambda i: (0, 0, 0)),
        cost_estimate=pl.CostEstimate(flops=0, bytes_accessed=1600000, transcendentals=0),
        name="arrange",
    )(teacher_slabs)


def pick_kernel(layer_map, received, picked, low, high):
    half = low.shape[0]

    def step(layer, carry):
        value = received[layer_map[layer]]
        picked[layer] = value
        low[layer] = value
        value = received[layer_map[half + layer]]
        picked[half + layer] = value
        high[layer] = value
        return carry

    lax.fori_loop(0, half, step, 0)


def pick(layer_map, received):
    layers = layer_map.shape[0]
    shapes = [(count, *received.shape[1:]) for count in (layers, layers // 2, layers // 2)]
    return pl.pallas_call(
        pick_kernel,
        out_shape=[jax.ShapeDtypeStruct(shape, received.dtype) for shape in shapes],
        in_specs=[
            pl.BlockSpec(memory_space=pltpu.SMEM),
            pl.BlockSpec(memory_space=pltpu.VMEM),
        ],
        out_specs=[pl.BlockSpec(memory_space=pltpu.VMEM)] * len(shapes),
        cost_estimate=pl.CostEstimate(flops=0, bytes_accessed=1300000, transcendentals=0),
        name="pick_layers",
    )(layer_map, received)


DISTANCES = (4, 3, -3, 2, -2, 1, -1, 0)
FIRST = ((0, 0), (1, 0), (3, 0), (0, 1))
REST = ((2, 0), (1, 1), (2, 1), (3, 1))
GROUPS = 4
WEIGHTS = 6


def load_weight(place, blocks, weights, weight, sem):
    piece = weights[0].shape[1]
    half = piece // 2
    copies = []
    for index in range(sem.shape[0]):
        for source, ref in enumerate(weights):
            part = source if source < 2 else 2 + (source - 2) // 2
            shift = half if source in (3, 5) else 0
            row = pl.multiple_of(index * QUARTERS * piece + place[part] * piece + shift, half)
            target = weight.at[pl.ds(row, ref.shape[1])]
            copies.append(pltpu.make_async_copy(ref.at[blocks[index]], target, sem.at[index, source]))
    for copy in copies:
        copy.start()
    return copies


def load_features(features, held, sem):
    copies = [
        pltpu.make_async_copy(ref, slot, sem.at[index]) for index, (ref, slot) in enumerate(zip(features, held))
    ]
    for copy in copies:
        copy.start()
    return copies


def left_rows(refs, firsts, group):
    _, halves, tokens, lanes = refs[0].shape
    return jnp.concatenate(
        [
            ref[pl.ds(first, group), h].reshape(group * tokens, lanes)
            for ref, first in zip(refs, firsts)
            for h in range(halves)
        ],
        axis=1,
    )


def project_first_kernel(place, blocks, *refs):
    count = len(FIRST) + 2
    features, refs = refs[:count], refs[count:]
    weights, (out, weight, *held, feature_sem, weight_sem) = refs[:WEIGHTS], refs[WEIGHTS:]
    copies = load_weight(place, blocks, weights, weight, weight_sem) + load_features(features, held, feature_sem)
    for copy in copies:
        copy.wait()
    own, up_a, up_b, down_a, down_b, row = held
    group = own.shape[0] // GROUPS
    for number in range(GROUPS):
        first = number * group
        side = number // (GROUPS // 2)
        offset = (number - side * (GROUPS // 2)) * group
        refs = (own, (up_a, up_b)[side], (down_a, down_b)[side], row)
        left = left_rows(refs, (first, offset, offset, first), group)
        out[number] = jnp.dot(left, weight[...], preferred_element_type=jnp.float32).astype(out.dtype)


def project_rest_kernel(place, blocks, slot_layer, partial, *refs):
    count = len(REST) + 2
    features, refs = refs[:count], refs[count:]
    weights, refs = refs[:WEIGHTS], refs[WEIGHTS:]
    outs, refs = refs[: len(DISTANCES) + 1], refs[len(DISTANCES) + 1 :]
    weight, before, product, *held, feature_sem, weight_sem, before_sem = refs
    copies = load_weight(place, blocks, weights, weight, weight_sem) + load_features(features, held, feature_sem)
    befores = [
        pltpu.make_async_copy(partial.at[number], before.at[number], before_sem.at[number]) for number in range(GROUPS)
    ]
    for copy in befores:
        copy.start()
    for copy in copies:
        copy.wait()
    layers, halves, tokens, lanes = features[2].shape
    group = layers // GROUPS
    near_a, near_b, row_1, row_2a, row_2b, row_3 = held
    for number in range(GROUPS):
        first = number * group
        side = number // (GROUPS // 2)
        offset = (number - side * (GROUPS // 2)) * group
        refs = ((near_a, near_b)[side], row_1, (row_2a, row_2b)[side], row_3)
        left = left_rows(refs, (offset, first, offset, first), group)
        value = jnp.dot(left, weight[...], preferred_element_type=jnp.float32)
        befores[number].wait()
        value = (value + before[number].astype(jnp.float32)).astype(product.dtype)
        product[pl.ds(first, group)] = value.reshape(group, tokens, value.shape[1])
    slots = outs[-1].shape[1]
    for index, out in enumerate(outs):
        chunk = max(index - 1, 0)
        for c in range(C):
            for slot in range(slots):
                value = product[slot_layer[(chunk * C + c) * slots + slot]]
                if index > 1:
                    out[c, slot] = value
                elif index == c:
                    out[slot] = value


def project_first(place, blocks, features, weights):
    layers, halves, tokens, lanes = features[0].shape
    columns = weights[0].shape[2]
    depth = len(FIRST) * halves * lanes
    shape = (GROUPS, layers * tokens // GROUPS, columns)
    smem, anywhere = pl.BlockSpec(memory_space=pltpu.SMEM), pl.BlockSpec(memory_space=pltpu.HBM)
    return pl.pallas_call(
        project_first_kernel,
        out_shape=jax.ShapeDtypeStruct(shape, jnp.bfloat16),
        in_specs=[smem] * 2 + [anywhere] * (len(features) + len(weights)),
        out_specs=pl.BlockSpec(memory_space=pltpu.VMEM),
        scratch_shapes=[
            pltpu.VMEM((depth, columns), jnp.bfloat16),
            *[pltpu.VMEM(feature.shape, feature.dtype) for feature in features],
            pltpu.SemaphoreType.DMA((len(features),)),
            pltpu.SemaphoreType.DMA((len(FIRST), WEIGHTS)),
        ],
        compiler_params=pltpu.CompilerParams(vmem_limit_bytes=40 * MIB),
        cost_estimate=pl.CostEstimate(
            flops=2 * layers * tokens * depth * columns, bytes_accessed=8 * MIB, transcendentals=0
        ),
        name="project_first",
    )(place, blocks, *features, *weights)


def project_rest(place, blocks, slot_layer, partial, features, weights):
    layers, halves, tokens, lanes = features[2].shape
    columns = weights[0].shape[2]
    depth = len(REST) * halves * lanes
    slots = slot_layer.shape[0] // (len(DISTANCES) * C)
    smem, vmem = pl.BlockSpec(memory_space=pltpu.SMEM), pl.BlockSpec(memory_space=pltpu.VMEM)
    shapes = [(slots, tokens, columns)] * C + [(C, slots, tokens, columns)] * (len(DISTANCES) - 1)
    return pl.pallas_call(
        project_rest_kernel,
        out_shape=[jax.ShapeDtypeStruct(shape, jnp.bfloat16) for shape in shapes],
        in_specs=[smem] * 3 + [pl.BlockSpec(memory_space=pltpu.HBM)] * (1 + len(features) + len(weights)),
        out_specs=[vmem] * len(shapes),
        scratch_shapes=[
            pltpu.VMEM((depth, columns), jnp.bfloat16),
            pltpu.VMEM(partial.shape, partial.dtype),
            pltpu.VMEM((layers, tokens, columns), jnp.bfloat16),
            *[pltpu.VMEM(feature.shape, feature.dtype) for feature in features],
            pltpu.SemaphoreType.DMA((len(features),)),
            pltpu.SemaphoreType.DMA((len(REST), WEIGHTS)),
            pltpu.SemaphoreType.DMA((GROUPS,)),
        ],
        compiler_params=pltpu.CompilerParams(vmem_limit_bytes=62 * MIB),
        cost_estimate=pl.CostEstimate(
            flops=2 * layers * tokens * depth * columns, bytes_accessed=11 * MIB, transcendentals=0
        ),
        name="project_rest",
    )(place, blocks, slot_layer, partial, *features, *weights)


def reduce_z(chunks):
    up = [(i, (i + 1) % Z) for i in range(Z)]
    down = [(i, (i - 1) % Z) for i in range(Z)]
    low, high, up3, down3, up2, down2, up1, down1, own = chunks

    def add(left, right):
        return (left.astype(jnp.float32) + right.astype(jnp.float32)).astype(left.dtype)

    rest = [(0, 0)] * low.ndim
    from_below = jnp.pad(lax.ppermute(high, "z", up)[None], [(1, 0), *rest])
    from_above = jnp.pad(lax.ppermute(low, "z", down)[None], [(0, 1), *rest])
    for to_up, to_down in ((up3, down3), (up2, down2), (up1, down1)):
        from_below = lax.ppermute(add(to_up, from_below), "z", up)
        from_above = lax.ppermute(add(to_down, from_above), "z", down)
    return own, from_below, from_above


def combine_kernel(core, own, below, above, kept, given):
    for out, c in ((kept, core[0]), (given, 1 - core[0])):
        total = own[c].astype(jnp.float32) + below[c].astype(jnp.float32) + above[c].astype(jnp.float32)
        out[...] = total.astype(out.dtype)


def combine(c, own, below, above):
    vmem = pl.BlockSpec(memory_space=pltpu.VMEM)
    shape = jax.ShapeDtypeStruct(own.shape[1:], own.dtype)
    return pl.pallas_call(
        combine_kernel,
        out_shape=[shape] * 2,
        in_specs=[pl.BlockSpec(memory_space=pltpu.SMEM)] + [vmem] * 3,
        out_specs=[vmem] * 2,
        cost_estimate=pl.CostEstimate(flops=3 * own.size, bytes_accessed=8 * own.size, transcendentals=0),
        name="combine",
    )(c.reshape(1).astype(jnp.int32), own, below, above)


def finish_kernel(state, hidden, layer_grad, near, teacher, across, teacher_across, out):
    core, count = state[0], state[1]
    slots, quarter, _ = near.shape
    quarters = ((C + core, near), (C + 1 - core, across), (core, teacher), (1 - core, teacher_across))
    for index, ref in quarters:
        rows = pl.ds(pl.multiple_of(index * quarter, quarter), quarter)
        for slot in range(slots):
            value = hidden[slot, rows, :].astype(jnp.float32) - ref[slot].astype(jnp.float32)
            value = jnp.where(slot < count, value, 0.0)
            if slot == 0:
                value = value + layer_grad[rows, :]
            out[slot, rows, :] = value.astype(out.dtype)


def finish(c, own_count, hidden, layer_grad, pieces):
    vmem = pl.BlockSpec(memory_space=pltpu.VMEM)
    return pl.pallas_call(
        finish_kernel,
        out_shape=jax.ShapeDtypeStruct(hidden.shape, hidden.dtype),
        in_specs=[pl.BlockSpec(memory_space=pltpu.SMEM)] + [vmem] * 6,
        out_specs=vmem,
        cost_estimate=pl.CostEstimate(flops=2 * hidden.size, bytes_accessed=8 * hidden.size, transcendentals=0),
        name="finish",
    )(jnp.stack([c, own_count]).astype(jnp.int32), hidden, layer_grad, *pieces)


def gather_tensor(own, low, high):
    up = [(i, (i + 1) % X) for i in range(X)]
    down = [(i, (i - 1) % X) for i in range(X)]
    swap = [(0, 1), (1, 0)]
    f3a = lax.ppermute(low, "x", up)
    f1b = lax.ppermute(high, "x", down)
    g0 = lax.ppermute(own, "yl", swap)
    f3b = lax.ppermute(high, "x", up)
    f1a = lax.ppermute(low, "x", down)
    f2a = lax.ppermute(f3a, "x", up)
    f2b = lax.ppermute(f1b, "x", down)
    g3 = lax.ppermute(g0, "x", up)
    g1 = lax.ppermute(g0, "x", down)
    g2a = lax.ppermute(f2a, "yl", swap)
    g2b = lax.ppermute(f2b, "yl", swap)
    return (own, f1a, f1b, f3a, f3b, g0), (f2a, f2b, g1, g2a, g2b, g3)


def body(
    teacher_slabs,
    proj_weight,
    child_hidden,
    norm_gain,
    key_weight,
    value_weight,
    key_cotangent,
    value_cotangent,
    layer_map,
    layer_counts,
):
    yh, z, c = lax.axis_index("yh"), lax.axis_index("z"), lax.axis_index("c")
    x, yl = lax.axis_index("x"), lax.axis_index("yl")
    slab_count, tokens, slab_width = teacher_slabs.shape
    layers = layer_map.shape[0]
    columns = proj_weight.shape[2]
    full_width = columns * X * YL
    slot_count = child_hidden.shape[0]
    quarter = tokens // QUARTERS

    swap = [(0, 1), (1, 0)]
    side = ("yh", "yl")
    ring = YH * YL
    up = [(i, (i + 1) % ring) for i in range(ring)]
    down = [(i, (i - 1) % ring) for i in range(ring)]
    half_rows = proj_weight.shape[1] // 2
    w_sib = lax.ppermute(proj_weight, "c", swap)
    place = jnp.stack([2 * yh + c, 2 * yh + 1 - c, 2 * (1 - yh) + c, 2 * (1 - yh) + 1 - c]).astype(jnp.int32)

    is_child = yh == 1
    first_hidden = child_hidden[0].astype(jnp.float32)
    norm_scale = norm_gain[0]
    contract_last = (((1,), (1,)), ((), ()))
    delta_norm = lax.dot_general(
        key_cotangent[0], key_weight[0], contract_last, preferred_element_type=jnp.float32
    )
    delta_norm = delta_norm + lax.dot_general(
        value_cotangent[0], value_weight[0], contract_last, preferred_element_type=jnp.float32
    )
    sums = jnp.stack(
        [
            jnp.sum(first_hidden * first_hidden, axis=1),
            jnp.sum(first_hidden * norm_scale * delta_norm, axis=1),
        ]
    )
    sums = sums + lax.ppermute(sums, "x", [(i, i ^ 1) for i in range(X)])
    sums = sums + lax.ppermute(sums, "x", [(i, i ^ 2) for i in range(X)])
    sums = sums + lax.ppermute(sums, "yl", swap)
    sent = lax.ppermute(arrange(teacher_slabs, 1), side, [(0, 3), (1, 2)])
    arranged = jnp.where(yh == 0, arrange(teacher_slabs, 0), sent)
    arranged, w_sib, sums, weight_rows = lax.optimization_barrier((arranged, w_sib, sums, proj_weight))
    w_far_a = lax.ppermute(lax.ppermute(weight_rows[:, :half_rows], side, up), side, up)
    w_far_b = lax.ppermute(lax.ppermute(weight_rows[:, half_rows:], side, down), side, down)
    received = lax.all_to_all(arranged, ("z", "c"), split_axis=0, concat_axis=0, tiled=True)
    received = received.reshape(Z * C * slab_count, YH, quarter, LANES)

    first_features, rest_features = gather_tensor(*pick(layer_map, received))
    w_far_a, w_far_b, _ = lax.optimization_barrier((w_far_a, w_far_b, first_features[3]))
    weights = (proj_weight, w_sib, w_far_a, w_far_b, lax.ppermute(w_far_a, "c", swap), lax.ppermute(w_far_b, "c", swap))
    squares, inner_sum = sums[0], sums[1]
    inverse_rms = lax.rsqrt(squares / full_width + EPSILON)[:, None]
    normed = (first_hidden * inverse_rms * norm_scale).astype(jnp.bfloat16)
    contract_rows = (((0,), (0,)), ((), ()))
    key_grad = lax.dot_general(
        normed, key_cotangent[0], contract_rows, preferred_element_type=jnp.float32
    ).astype(jnp.bfloat16)
    value_grad = lax.dot_general(
        normed, value_cotangent[0], contract_rows, preferred_element_type=jnp.float32
    ).astype(jnp.bfloat16)
    gain_grad = jnp.sum(first_hidden * inverse_rms * delta_norm, axis=0)
    layer_grad = (
        inverse_rms * norm_scale * delta_norm
        - first_hidden * inverse_rms**3 * inner_sum[:, None] / full_width
    )
    layer_grad = jnp.where(is_child, layer_grad, 0.0)
    first_blocks, rest_blocks = (
        jnp.stack([(x + step) % X * YL + (yl + yh + other) % YL for step, other in places]).astype(jnp.int32)
        for places in (FIRST, REST)
    )
    prefix_end = jnp.cumsum(layer_counts)
    prefix_start = prefix_end - layer_counts
    slot_layer = jnp.clip(prefix_start[:, None] + jnp.arange(slot_count)[None, :], 0, layers - 1)
    slot_layer = slot_layer.reshape(Z, C * slot_count)[(z + jnp.array(DISTANCES)) % Z].reshape(-1).astype(jnp.int32)
    partial = project_first(place, first_blocks, first_features, weights)
    chunks = project_rest(place, rest_blocks, slot_layer, partial, rest_features, weights)
    kept, given = combine(c, *reduce_z(chunks))
    across = lax.ppermute(given, "c", swap)
    teacher = lax.ppermute(kept, "yh", [(0, 1)])
    teacher_across = lax.ppermute(given, ("yh", "c"), [(0, 3), (1, 2)])
    own_count = jnp.where(is_child, layer_counts[2 * z + c], 0)
    hidden_grad = finish(c, own_count, child_hidden, layer_grad, (kept, teacher, across, teacher_across))
    key_grad = jnp.where(is_child, key_grad, jnp.zeros_like(key_grad))
    value_grad = jnp.where(is_child, value_grad, jnp.zeros_like(value_grad))
    gain_grad = jnp.where(is_child, gain_grad, 0.0)
    return (hidden_grad, key_grad[None], value_grad[None], gain_grad[None])


def solution(mesh):
    fine = Mesh(mesh.devices.reshape(YH, Z, C, X, YL), (*SEGMENT, *TENSOR))
    placed = (
        P(SEGMENT, None, TENSOR),
        P(None, SEGMENT, TENSOR),
        P(SEGMENT, None, TENSOR),
        P(SEGMENT, TENSOR),
        P(SEGMENT, TENSOR, None),
        P(SEGMENT, TENSOR, None),
        P(SEGMENT, None, None),
        P(SEGMENT, None, None),
        P(),
        P(),
    )
    return jax.shard_map(
        body,
        mesh=fine,
        in_specs=placed,
        out_specs=(
            P(SEGMENT, None, TENSOR),
            P(SEGMENT, TENSOR, None),
            P(SEGMENT, TENSOR, None),
            P(SEGMENT, TENSOR),
        ),
        check_vma=False,
    )
```

```python
import jax
import jax.numpy as jnp
from jax import lax
from jax.experimental import pallas as pl
from jax.experimental.pallas import tpu as pltpu
from jax.sharding import Mesh, PartitionSpec as P

EPSILON = 1e-05
MIB = 1 << 20

SEGMENT = ("yh", "z", "c")
TENSOR = ("x", "yl")
YH, Z, C, X, YL = 2, 8, 2, 4, 2
QUARTERS = YH * C
LANES = 128


def arrange_kernel(slabs, out):
    slab_count, width, _ = slabs.shape
    tokens = width // C
    for c in range(C):
        for z in range(Z):
            for slab in range(slab_count):
                for h in range(YH):
                    lane = (h * Z + z) * LANES
                    row = (slab * YH + h) * tokens
                    out[z * C + c, row : row + tokens, :] = slabs[
                        slab, c * tokens : (c + 1) * tokens, lane : lane + LANES
                    ]


def arrange(teacher_slabs, section):
    slab_count, tokens, width = teacher_slabs.shape
    rows = slab_count * YH * (tokens // QUARTERS)
    shape = jax.ShapeDtypeStruct((Z * C, rows, LANES), teacher_slabs.dtype)
    return pl.pallas_call(
        arrange_kernel,
        grid=(1,),
        out_shape=shape,
        in_specs=[pl.BlockSpec((slab_count, tokens // YH, width), lambda i: (0, section, 0))],
        out_specs=pl.BlockSpec(shape.shape, lambda i: (0, 0, 0)),
        cost_estimate=pl.CostEstimate(flops=0, bytes_accessed=1600000, transcendentals=0),
        name="arrange",
    )(teacher_slabs)


def pick_kernel(layer_map, received, picked, low, high):
    half = low.shape[0]

    def step(layer, carry):
        value = received[layer_map[layer]]
        picked[layer] = value
        low[layer] = value
        value = received[layer_map[half + layer]]
        picked[half + layer] = value
        high[layer] = value
        return carry

    lax.fori_loop(0, half, step, 0)


def pick(layer_map, received):
    layers = layer_map.shape[0]
    shapes = [(count, *received.shape[1:]) for count in (layers, layers // 2, layers // 2)]
    return pl.pallas_call(
        pick_kernel,
        out_shape=[jax.ShapeDtypeStruct(shape, received.dtype) for shape in shapes],
        in_specs=[
            pl.BlockSpec(memory_space=pltpu.SMEM),
            pl.BlockSpec(memory_space=pltpu.VMEM),
        ],
        out_specs=[pl.BlockSpec(memory_space=pltpu.VMEM)] * len(shapes),
        cost_estimate=pl.CostEstimate(flops=0, bytes_accessed=1300000, transcendentals=0),
        name="pick_layers",
    )(layer_map, received)


DISTANCES = (4, 3, -3, 2, -2, 1, -1, 0)
FIRST = ((0, 0), (1, 0), (3, 0), (0, 1))
REST = ((2, 0), (1, 1), (2, 1), (3, 1))
GROUPS = 4
WEIGHTS = 6


def load_weight(place, blocks, weights, weight, sem):
    piece = weights[0].shape[1]
    half = piece // 2
    copies = []
    for index in range(sem.shape[0]):
        for source, ref in enumerate(weights):
            part = source if source < 2 else 2 + (source - 2) // 2
            shift = half if source in (3, 5) else 0
            row = pl.multiple_of(index * QUARTERS * piece + place[part] * piece + shift, half)
            target = weight.at[pl.ds(row, ref.shape[1])]
            copies.append(pltpu.make_async_copy(ref.at[blocks[index]], target, sem.at[index, source]))
    for copy in copies:
        copy.start()
    return copies


def load_features(features, held, sem):
    copies = [
        pltpu.make_async_copy(ref, slot, sem.at[index]) for index, (ref, slot) in enumerate(zip(features, held))
    ]
    for copy in copies:
        copy.start()
    return copies


def left_rows(refs, firsts, group):
    _, halves, tokens, lanes = refs[0].shape
    return jnp.concatenate(
        [
            ref[pl.ds(first, group), h].reshape(group * tokens, lanes)
            for ref, first in zip(refs, firsts)
            for h in range(halves)
        ],
        axis=1,
    )


def project_first_kernel(place, blocks, *refs):
    count = len(FIRST) + 2
    features, refs = refs[:count], refs[count:]
    weights, (out, weight, *held, feature_sem, weight_sem) = refs[:WEIGHTS], refs[WEIGHTS:]
    copies = load_weight(place, blocks, weights, weight, weight_sem) + load_features(features, held, feature_sem)
    for copy in copies:
        copy.wait()
    own, up_a, up_b, down_a, down_b, row = held
    group = own.shape[0] // GROUPS
    for number in range(GROUPS):
        first = number * group
        side = number // (GROUPS // 2)
        offset = (number - side * (GROUPS // 2)) * group
        refs = (own, (up_a, up_b)[side], (down_a, down_b)[side], row)
        left = left_rows(refs, (first, offset, offset, first), group)
        out[number] = jnp.dot(left, weight[...], preferred_element_type=jnp.float32).astype(out.dtype)


def project_rest_kernel(place, blocks, slot_layer, partial, *refs):
    count = len(REST) + 2
    features, refs = refs[:count], refs[count:]
    weights, refs = refs[:WEIGHTS], refs[WEIGHTS:]
    outs, refs = refs[: C * len(DISTANCES)], refs[C * len(DISTANCES) :]
    weight, before, product, *held, feature_sem, weight_sem, before_sem = refs
    copies = load_weight(place, blocks, weights, weight, weight_sem) + load_features(features, held, feature_sem)
    befores = [
        pltpu.make_async_copy(partial.at[number], before.at[number], before_sem.at[number]) for number in range(GROUPS)
    ]
    for copy in befores:
        copy.start()
    for copy in copies:
        copy.wait()
    layers, halves, tokens, lanes = features[2].shape
    group = layers // GROUPS
    near_a, near_b, row_1, row_2a, row_2b, row_3 = held
    for number in range(GROUPS):
        first = number * group
        side = number // (GROUPS // 2)
        offset = (number - side * (GROUPS // 2)) * group
        refs = ((near_a, near_b)[side], row_1, (row_2a, row_2b)[side], row_3)
        left = left_rows(refs, (offset, first, offset, first), group)
        value = jnp.dot(left, weight[...], preferred_element_type=jnp.float32)
        befores[number].wait()
        value = (value + before[number].astype(jnp.float32)).astype(product.dtype)
        product[pl.ds(first, group)] = value.reshape(group, tokens, value.shape[1])
    slots = outs[0].shape[0]
    for index, out in enumerate(outs):
        for slot in range(slots):
            out[slot] = product[slot_layer[index * slots + slot]]


def project_first(place, blocks, features, weights):
    layers, halves, tokens, lanes = features[0].shape
    columns = weights[0].shape[2]
    depth = len(FIRST) * halves * lanes
    shape = (GROUPS, layers * tokens // GROUPS, columns)
    smem, anywhere = pl.BlockSpec(memory_space=pltpu.SMEM), pl.BlockSpec(memory_space=pltpu.HBM)
    return pl.pallas_call(
        project_first_kernel,
        out_shape=jax.ShapeDtypeStruct(shape, jnp.bfloat16),
        in_specs=[smem] * 2 + [anywhere] * (len(features) + len(weights)),
        out_specs=pl.BlockSpec(memory_space=pltpu.VMEM),
        scratch_shapes=[
            pltpu.VMEM((depth, columns), jnp.bfloat16),
            *[pltpu.VMEM(feature.shape, feature.dtype) for feature in features],
            pltpu.SemaphoreType.DMA((len(features),)),
            pltpu.SemaphoreType.DMA((len(FIRST), WEIGHTS)),
        ],
        compiler_params=pltpu.CompilerParams(vmem_limit_bytes=40 * MIB),
        cost_estimate=pl.CostEstimate(
            flops=2 * layers * tokens * depth * columns, bytes_accessed=8 * MIB, transcendentals=0
        ),
        name="project_first",
    )(place, blocks, *features, *weights)


def project_rest(place, blocks, slot_layer, partial, features, weights):
    layers, halves, tokens, lanes = features[2].shape
    columns = weights[0].shape[2]
    depth = len(REST) * halves * lanes
    slots = slot_layer.shape[0] // (len(DISTANCES) * C)
    smem, vmem = pl.BlockSpec(memory_space=pltpu.SMEM), pl.BlockSpec(memory_space=pltpu.VMEM)
    shapes = [(slots, tokens, columns)] * (C * len(DISTANCES))
    return pl.pallas_call(
        project_rest_kernel,
        out_shape=[jax.ShapeDtypeStruct(shape, jnp.bfloat16) for shape in shapes],
        in_specs=[smem] * 3 + [pl.BlockSpec(memory_space=pltpu.HBM)] * (1 + len(features) + len(weights)),
        out_specs=[vmem] * len(shapes),
        scratch_shapes=[
            pltpu.VMEM((depth, columns), jnp.bfloat16),
            pltpu.VMEM(partial.shape, partial.dtype),
            pltpu.VMEM((layers, tokens, columns), jnp.bfloat16),
            *[pltpu.VMEM(feature.shape, feature.dtype) for feature in features],
            pltpu.SemaphoreType.DMA((len(features),)),
            pltpu.SemaphoreType.DMA((len(REST), WEIGHTS)),
            pltpu.SemaphoreType.DMA((GROUPS,)),
        ],
        compiler_params=pltpu.CompilerParams(vmem_limit_bytes=62 * MIB),
        cost_estimate=pl.CostEstimate(
            flops=2 * layers * tokens * depth * columns, bytes_accessed=11 * MIB, transcendentals=0
        ),
        name="project_rest",
    )(place, blocks, slot_layer, partial, *features, *weights)


def reduce_z(chunks):
    up = [(i, (i + 1) % Z) for i in range(Z)]
    down = [(i, (i - 1) % Z) for i in range(Z)]
    given = dict(zip(DISTANCES, chunks[0::2]))
    kept = dict(zip(DISTANCES, chunks[1::2]))

    def add(*terms):
        return sum(term.astype(jnp.float32) for term in terms).astype(terms[0].dtype)

    given_up = lax.ppermute(given[4], "z", up)
    kept_down = lax.ppermute(kept[4], "z", down)
    given_down = lax.ppermute(given[-3], "z", down)
    kept_up = lax.ppermute(kept[3], "z", up)
    for distance in (3, 2, 1):
        given_up = lax.ppermute(add(given[distance], given_up), "z", up)
        if distance < 3:
            given_down = lax.ppermute(add(given[-distance], given_down), "z", down)
        kept_down = lax.ppermute(add(kept[-distance], kept_down), "z", down)
        if distance < 3:
            kept_up = lax.ppermute(add(kept[distance], kept_up), "z", up)
    return add(given[0], given_up, given_down), add(kept[0], kept_up, kept_down)


def finish_kernel(state, hidden, layer_grad, near, teacher, across, teacher_across, out):
    core, count = state[0], state[1]
    slots, quarter, _ = near.shape
    quarters = ((C + core, near), (C + 1 - core, across), (core, teacher), (1 - core, teacher_across))
    for index, ref in quarters:
        rows = pl.ds(pl.multiple_of(index * quarter, quarter), quarter)
        for slot in range(slots):
            value = hidden[slot, rows, :].astype(jnp.float32) - ref[slot].astype(jnp.float32)
            value = jnp.where(slot < count, value, 0.0)
            if slot == 0:
                value = value + layer_grad[rows, :]
            out[slot, rows, :] = value.astype(out.dtype)


def finish(c, own_count, hidden, layer_grad, pieces):
    vmem = pl.BlockSpec(memory_space=pltpu.VMEM)
    return pl.pallas_call(
        finish_kernel,
        out_shape=jax.ShapeDtypeStruct(hidden.shape, hidden.dtype),
        in_specs=[pl.BlockSpec(memory_space=pltpu.SMEM)] + [vmem] * 6,
        out_specs=vmem,
        cost_estimate=pl.CostEstimate(flops=2 * hidden.size, bytes_accessed=8 * hidden.size, transcendentals=0),
        name="finish",
    )(jnp.stack([c, own_count]).astype(jnp.int32), hidden, layer_grad, *pieces)


def gather_tensor(own, low, high):
    up = [(i, (i + 1) % X) for i in range(X)]
    down = [(i, (i - 1) % X) for i in range(X)]
    swap = [(0, 1), (1, 0)]
    f3a = lax.ppermute(low, "x", up)
    f1b = lax.ppermute(high, "x", down)
    g0 = lax.ppermute(own, "yl", swap)
    f3b = lax.ppermute(high, "x", up)
    f1a = lax.ppermute(low, "x", down)
    f2a = lax.ppermute(f3a, "x", up)
    f2b = lax.ppermute(f1b, "x", down)
    g3 = lax.ppermute(g0, "x", up)
    g1 = lax.ppermute(g0, "x", down)
    g2a = lax.ppermute(f2a, "yl", swap)
    g2b = lax.ppermute(f2b, "yl", swap)
    return (own, f1a, f1b, f3a, f3b, g0), (f2a, f2b, g1, g2a, g2b, g3)


def body(
    teacher_slabs,
    proj_weight,
    child_hidden,
    norm_gain,
    key_weight,
    value_weight,
    key_cotangent,
    value_cotangent,
    layer_map,
    layer_counts,
):
    yh, z, c = lax.axis_index("yh"), lax.axis_index("z"), lax.axis_index("c")
    x, yl = lax.axis_index("x"), lax.axis_index("yl")
    slab_count, tokens, slab_width = teacher_slabs.shape
    layers = layer_map.shape[0]
    columns = proj_weight.shape[2]
    full_width = columns * X * YL
    slot_count = child_hidden.shape[0]
    quarter = tokens // QUARTERS

    swap = [(0, 1), (1, 0)]
    side = ("yh", "yl")
    ring = YH * YL
    up = [(i, (i + 1) % ring) for i in range(ring)]
    down = [(i, (i - 1) % ring) for i in range(ring)]
    half_rows = proj_weight.shape[1] // 2
    w_sib = lax.ppermute(proj_weight, "c", swap)
    place = jnp.stack([2 * yh + c, 2 * yh + 1 - c, 2 * (1 - yh) + c, 2 * (1 - yh) + 1 - c]).astype(jnp.int32)

    is_child = yh == 1
    first_hidden = child_hidden[0].astype(jnp.float32)
    norm_scale = norm_gain[0]
    contract_last = (((1,), (1,)), ((), ()))
    delta_norm = lax.dot_general(
        key_cotangent[0], key_weight[0], contract_last, preferred_element_type=jnp.float32
    )
    delta_norm = delta_norm + lax.dot_general(
        value_cotangent[0], value_weight[0], contract_last, preferred_element_type=jnp.float32
    )
    sums = jnp.stack(
        [
            jnp.sum(first_hidden * first_hidden, axis=1),
            jnp.sum(first_hidden * norm_scale * delta_norm, axis=1),
        ]
    )
    sums = sums + lax.ppermute(sums, "x", [(i, i ^ 1) for i in range(X)])
    sums = sums + lax.ppermute(sums, "x", [(i, i ^ 2) for i in range(X)])
    sums = sums + lax.ppermute(sums, "yl", swap)
    sent = lax.ppermute(arrange(teacher_slabs, 1), side, [(0, 3), (1, 2)])
    arranged = jnp.where(yh == 0, arrange(teacher_slabs, 0), sent)
    arranged, w_sib, sums, weight_rows = lax.optimization_barrier((arranged, w_sib, sums, proj_weight))
    w_far_a = lax.ppermute(lax.ppermute(weight_rows[:, :half_rows], side, up), side, up)
    w_far_b = lax.ppermute(lax.ppermute(weight_rows[:, half_rows:], side, down), side, down)
    received = lax.all_to_all(arranged, ("z", "c"), split_axis=0, concat_axis=0, tiled=True)
    received = received.reshape(Z * C * slab_count, YH, quarter, LANES)

    first_features, rest_features = gather_tensor(*pick(layer_map, received))
    w_far_a, w_far_b, _ = lax.optimization_barrier((w_far_a, w_far_b, first_features[3]))
    weights = (proj_weight, w_sib, w_far_a, w_far_b, lax.ppermute(w_far_a, "c", swap), lax.ppermute(w_far_b, "c", swap))
    squares, inner_sum = sums[0], sums[1]
    inverse_rms = lax.rsqrt(squares / full_width + EPSILON)[:, None]
    normed = (first_hidden * inverse_rms * norm_scale).astype(jnp.bfloat16)
    contract_rows = (((0,), (0,)), ((), ()))
    key_grad = lax.dot_general(
        normed, key_cotangent[0], contract_rows, preferred_element_type=jnp.float32
    ).astype(jnp.bfloat16)
    value_grad = lax.dot_general(
        normed, value_cotangent[0], contract_rows, preferred_element_type=jnp.float32
    ).astype(jnp.bfloat16)
    gain_grad = jnp.sum(first_hidden * inverse_rms * delta_norm, axis=0)
    layer_grad = (
        inverse_rms * norm_scale * delta_norm
        - first_hidden * inverse_rms**3 * inner_sum[:, None] / full_width
    )
    layer_grad = jnp.where(is_child, layer_grad, 0.0)
    first_blocks, rest_blocks = (
        jnp.stack([(x + step) % X * YL + (yl + yh + other) % YL for step, other in places]).astype(jnp.int32)
        for places in (FIRST, REST)
    )
    prefix_end = jnp.cumsum(layer_counts)
    prefix_start = prefix_end - layer_counts
    slot_layer = jnp.clip(prefix_start[:, None] + jnp.arange(slot_count)[None, :], 0, layers - 1)
    slot_layer = slot_layer.reshape(Z, C, slot_count)[(z + jnp.array(DISTANCES)) % Z]
    slot_layer = jnp.where(c == 0, slot_layer[:, ::-1], slot_layer).reshape(-1).astype(jnp.int32)
    partial = project_first(place, first_blocks, first_features, weights)
    chunks = project_rest(place, rest_blocks, slot_layer, partial, rest_features, weights)
    given, kept = reduce_z(chunks)
    across = lax.ppermute(given, "c", swap)
    teacher = lax.ppermute(kept, "yh", [(0, 1)])
    teacher_across = lax.ppermute(given, ("yh", "c"), [(0, 3), (1, 2)])
    own_count = jnp.where(is_child, layer_counts[2 * z + c], 0)
    hidden_grad = finish(c, own_count, child_hidden, layer_grad, (kept, teacher, across, teacher_across))
    key_grad = jnp.where(is_child, key_grad, jnp.zeros_like(key_grad))
    value_grad = jnp.where(is_child, value_grad, jnp.zeros_like(value_grad))
    gain_grad = jnp.where(is_child, gain_grad, 0.0)
    return (hidden_grad, key_grad[None], value_grad[None], gain_grad[None])


def solution(mesh):
    fine = Mesh(mesh.devices.reshape(YH, Z, C, X, YL), (*SEGMENT, *TENSOR))
    placed = (
        P(SEGMENT, None, TENSOR),
        P(None, SEGMENT, TENSOR),
        P(SEGMENT, None, TENSOR),
        P(SEGMENT, TENSOR),
        P(SEGMENT, TENSOR, None),
        P(SEGMENT, TENSOR, None),
        P(SEGMENT, None, None),
        P(SEGMENT, None, None),
        P(),
        P(),
    )
    return jax.shard_map(
        body,
        mesh=fine,
        in_specs=placed,
        out_specs=(
            P(SEGMENT, None, TENSOR),
            P(SEGMENT, TENSOR, None),
            P(SEGMENT, TENSOR, None),
            P(SEGMENT, TENSOR),
        ),
        check_vma=False,
    )
```

```python
import jax
import jax.numpy as jnp
from jax import lax
from jax.experimental import pallas as pl
from jax.experimental.pallas import tpu as pltpu
from jax.sharding import Mesh, PartitionSpec as P

EPSILON = 1e-05
MIB = 1 << 20

SEGMENT = ("yh", "z", "c")
TENSOR = ("x", "yl")
YH, Z, C, X, YL = 2, 8, 2, 4, 2
QUARTERS = YH * C
LANES = 128


def arrange_kernel(slabs, out):
    slab_count, width, _ = slabs.shape
    tokens = width // C
    for c in range(C):
        for z in range(Z):
            for slab in range(slab_count):
                for h in range(YH):
                    lane = (h * Z + z) * LANES
                    row = (slab * YH + h) * tokens
                    out[z * C + c, row : row + tokens, :] = slabs[
                        slab, c * tokens : (c + 1) * tokens, lane : lane + LANES
                    ]


def arrange(teacher_slabs, section):
    slab_count, tokens, width = teacher_slabs.shape
    rows = slab_count * YH * (tokens // QUARTERS)
    shape = jax.ShapeDtypeStruct((Z * C, rows, LANES), teacher_slabs.dtype)
    return pl.pallas_call(
        arrange_kernel,
        grid=(1,),
        out_shape=shape,
        in_specs=[pl.BlockSpec((slab_count, tokens // YH, width), lambda i: (0, section, 0))],
        out_specs=pl.BlockSpec(shape.shape, lambda i: (0, 0, 0)),
        cost_estimate=pl.CostEstimate(flops=0, bytes_accessed=1600000, transcendentals=0),
        name="arrange",
    )(teacher_slabs)


def pick_kernel(layer_map, received, picked, low, high):
    half = low.shape[0]

    def step(layer, carry):
        value = received[layer_map[layer]]
        picked[layer] = value
        low[layer] = value
        value = received[layer_map[half + layer]]
        picked[half + layer] = value
        high[layer] = value
        return carry

    lax.fori_loop(0, half, step, 0)


def pick(layer_map, received):
    layers = layer_map.shape[0]
    shapes = [(count, *received.shape[1:]) for count in (layers, layers // 2, layers // 2)]
    return pl.pallas_call(
        pick_kernel,
        out_shape=[jax.ShapeDtypeStruct(shape, received.dtype) for shape in shapes],
        in_specs=[
            pl.BlockSpec(memory_space=pltpu.SMEM),
            pl.BlockSpec(memory_space=pltpu.VMEM),
        ],
        out_specs=[pl.BlockSpec(memory_space=pltpu.VMEM)] * len(shapes),
        cost_estimate=pl.CostEstimate(flops=0, bytes_accessed=1300000, transcendentals=0),
        name="pick_layers",
    )(layer_map, received)


DISTANCES = (4, 3, -3, 2, -2, 1, -1, 0)
FIRST = ((0, 0), (1, 0), (3, 0), (0, 1))
REST = ((2, 0), (1, 1), (2, 1), (3, 1))
GROUPS = 4
WEIGHTS = 6


def load_weight(place, blocks, weights, weight, sem):
    piece = weights[0].shape[1]
    half = piece // 2
    copies = []
    for index in range(sem.shape[0]):
        for source, ref in enumerate(weights):
            part = source if source < 2 else 2 + (source - 2) // 2
            shift = half if source in (3, 5) else 0
            row = pl.multiple_of(index * QUARTERS * piece + place[part] * piece + shift, half)
            target = weight.at[pl.ds(row, ref.shape[1])]
            copies.append(pltpu.make_async_copy(ref.at[blocks[index]], target, sem.at[index, source]))
    for copy in copies:
        copy.start()
    return copies


def load_features(features, held, sem):
    copies = [
        pltpu.make_async_copy(ref, slot, sem.at[index]) for index, (ref, slot) in enumerate(zip(features, held))
    ]
    for copy in copies:
        copy.start()
    return copies


def left_rows(refs, firsts, group):
    _, halves, tokens, lanes = refs[0].shape
    return jnp.concatenate(
        [
            ref[pl.ds(first, group), h].reshape(group * tokens, lanes)
            for ref, first in zip(refs, firsts)
            for h in range(halves)
        ],
        axis=1,
    )


def project_first_kernel(place, blocks, *refs):
    count = len(FIRST) + 2
    features, refs = refs[:count], refs[count:]
    weights, (out, weight, *held, feature_sem, weight_sem) = refs[:WEIGHTS], refs[WEIGHTS:]
    copies = load_weight(place, blocks, weights, weight, weight_sem) + load_features(features, held, feature_sem)
    for copy in copies:
        copy.wait()
    own, up_a, up_b, down_a, down_b, row = held
    group = own.shape[0] // GROUPS
    for number in range(GROUPS):
        first = number * group
        side = number // (GROUPS // 2)
        offset = (number - side * (GROUPS // 2)) * group
        refs = (own, (up_a, up_b)[side], (down_a, down_b)[side], row)
        left = left_rows(refs, (first, offset, offset, first), group)
        out[number] = jnp.dot(left, weight[...], preferred_element_type=jnp.float32).astype(out.dtype)


def project_rest_kernel(place, blocks, slot_layer, partial, *refs):
    count = len(REST) + 2
    features, refs = refs[:count], refs[count:]
    weights, refs = refs[:WEIGHTS], refs[WEIGHTS:]
    outs, refs = refs[: C * len(DISTANCES)], refs[C * len(DISTANCES) :]
    weight, before, product, *held, feature_sem, weight_sem, before_sem = refs
    copies = load_weight(place, blocks, weights, weight, weight_sem) + load_features(features, held, feature_sem)
    befores = [
        pltpu.make_async_copy(partial.at[number], before.at[number], before_sem.at[number]) for number in range(GROUPS)
    ]
    for copy in befores:
        copy.start()
    for copy in copies:
        copy.wait()
    layers, halves, tokens, lanes = features[2].shape
    group = layers // GROUPS
    near_a, near_b, row_1, row_2a, row_2b, row_3 = held
    for number in range(GROUPS):
        first = number * group
        side = number // (GROUPS // 2)
        offset = (number - side * (GROUPS // 2)) * group
        refs = ((near_a, near_b)[side], row_1, (row_2a, row_2b)[side], row_3)
        left = left_rows(refs, (offset, first, offset, first), group)
        value = jnp.dot(left, weight[...], preferred_element_type=jnp.float32)
        befores[number].wait()
        value = (value + before[number].astype(jnp.float32)).astype(product.dtype)
        product[pl.ds(first, group)] = value.reshape(group, tokens, value.shape[1])
    slots = outs[0].shape[0]
    for index, out in enumerate(outs):
        for slot in range(slots):
            out[slot] = product[slot_layer[index * slots + slot]]


def project_first(place, blocks, features, weights):
    layers, halves, tokens, lanes = features[0].shape
    columns = weights[0].shape[2]
    depth = len(FIRST) * halves * lanes
    shape = (GROUPS, layers * tokens // GROUPS, columns)
    smem, anywhere = pl.BlockSpec(memory_space=pltpu.SMEM), pl.BlockSpec(memory_space=pltpu.HBM)
    return pl.pallas_call(
        project_first_kernel,
        out_shape=jax.ShapeDtypeStruct(shape, jnp.bfloat16),
        in_specs=[smem] * 2 + [anywhere] * (len(features) + len(weights)),
        out_specs=pl.BlockSpec(memory_space=pltpu.VMEM),
        scratch_shapes=[
            pltpu.VMEM((depth, columns), jnp.bfloat16),
            *[pltpu.VMEM(feature.shape, feature.dtype) for feature in features],
            pltpu.SemaphoreType.DMA((len(features),)),
            pltpu.SemaphoreType.DMA((len(FIRST), WEIGHTS)),
        ],
        compiler_params=pltpu.CompilerParams(vmem_limit_bytes=40 * MIB),
        cost_estimate=pl.CostEstimate(
            flops=2 * layers * tokens * depth * columns, bytes_accessed=8 * MIB, transcendentals=0
        ),
        name="project_first",
    )(place, blocks, *features, *weights)


def project_rest(place, blocks, slot_layer, partial, features, weights):
    layers, halves, tokens, lanes = features[2].shape
    columns = weights[0].shape[2]
    depth = len(REST) * halves * lanes
    slots = slot_layer.shape[0] // (len(DISTANCES) * C)
    smem, vmem = pl.BlockSpec(memory_space=pltpu.SMEM), pl.BlockSpec(memory_space=pltpu.VMEM)
    shapes = [(slots, tokens, columns)] * (C * len(DISTANCES))
    return pl.pallas_call(
        project_rest_kernel,
        out_shape=[jax.ShapeDtypeStruct(shape, jnp.bfloat16) for shape in shapes],
        in_specs=[smem] * 3 + [pl.BlockSpec(memory_space=pltpu.HBM)] * (1 + len(features) + len(weights)),
        out_specs=[vmem] * len(shapes),
        scratch_shapes=[
            pltpu.VMEM((depth, columns), jnp.bfloat16),
            pltpu.VMEM(partial.shape, partial.dtype),
            pltpu.VMEM((layers, tokens, columns), jnp.bfloat16),
            *[pltpu.VMEM(feature.shape, feature.dtype) for feature in features],
            pltpu.SemaphoreType.DMA((len(features),)),
            pltpu.SemaphoreType.DMA((len(REST), WEIGHTS)),
            pltpu.SemaphoreType.DMA((GROUPS,)),
        ],
        compiler_params=pltpu.CompilerParams(vmem_limit_bytes=62 * MIB),
        cost_estimate=pl.CostEstimate(
            flops=2 * layers * tokens * depth * columns, bytes_accessed=11 * MIB, transcendentals=0
        ),
        name="project_rest",
    )(place, blocks, slot_layer, partial, *features, *weights)


def reduce_z(chunks):
    up = [(i, (i + 1) % Z) for i in range(Z)]
    down = [(i, (i - 1) % Z) for i in range(Z)]
    given = dict(zip(DISTANCES, chunks[0::2]))
    kept = dict(zip(DISTANCES, chunks[1::2]))

    def add(*terms):
        return sum(term.astype(jnp.float32) for term in terms).astype(terms[0].dtype)

    given_up = lax.ppermute(given[4], "z", up)
    kept_down = lax.ppermute(kept[4], "z", down)
    given_down = lax.ppermute(given[-3], "z", down)
    kept_up = lax.ppermute(kept[3], "z", up)
    for distance in (3, 2, 1):
        given_up = lax.ppermute(add(given[distance], given_up), "z", up)
        if distance < 3:
            given_down = lax.ppermute(add(given[-distance], given_down), "z", down)
        kept_down = lax.ppermute(add(kept[-distance], kept_down), "z", down)
        if distance < 3:
            kept_up = lax.ppermute(add(kept[distance], kept_up), "z", up)
    return add(given[0], given_up, given_down), add(kept[0], kept_up, kept_down)


def finish_kernel(state, hidden, layer_grad, near, teacher, across, teacher_across, out):
    core, count = state[0], state[1]
    slots, quarter, _ = near.shape
    quarters = ((C + core, near), (C + 1 - core, across), (core, teacher), (1 - core, teacher_across))
    for index, ref in quarters:
        rows = pl.ds(pl.multiple_of(index * quarter, quarter), quarter)
        for slot in range(slots):
            value = hidden[slot, rows, :].astype(jnp.float32) - ref[slot].astype(jnp.float32)
            value = jnp.where(slot < count, value, 0.0)
            if slot == 0:
                value = value + layer_grad[rows, :]
            out[slot, rows, :] = value.astype(out.dtype)


def finish(c, own_count, hidden, layer_grad, pieces):
    vmem = pl.BlockSpec(memory_space=pltpu.VMEM)
    return pl.pallas_call(
        finish_kernel,
        out_shape=jax.ShapeDtypeStruct(hidden.shape, hidden.dtype),
        in_specs=[pl.BlockSpec(memory_space=pltpu.SMEM)] + [vmem] * 6,
        out_specs=vmem,
        cost_estimate=pl.CostEstimate(flops=2 * hidden.size, bytes_accessed=8 * hidden.size, transcendentals=0),
        name="finish",
    )(jnp.stack([c, own_count]).astype(jnp.int32), hidden, layer_grad, *pieces)


def gather_tensor(own, low, high):
    up = [(i, (i + 1) % X) for i in range(X)]
    down = [(i, (i - 1) % X) for i in range(X)]
    swap = [(0, 1), (1, 0)]
    f3a = lax.ppermute(low, "x", up)
    f1b = lax.ppermute(high, "x", down)
    g0 = lax.ppermute(own, "yl", swap)
    low, high, f3a, f1b = lax.optimization_barrier((low, high, f3a, f1b))
    f3b = lax.ppermute(high, "x", up)
    f1a = lax.ppermute(low, "x", down)
    f2a = lax.ppermute(f3a, "x", up)
    f2b = lax.ppermute(f1b, "x", down)
    g3 = lax.ppermute(g0, "x", up)
    g1 = lax.ppermute(g0, "x", down)
    g2a = lax.ppermute(f2a, "yl", swap)
    g2b = lax.ppermute(f2b, "yl", swap)
    return (own, f1a, f1b, f3a, f3b, g0), (f2a, f2b, g1, g2a, g2b, g3)


def body(
    teacher_slabs,
    proj_weight,
    child_hidden,
    norm_gain,
    key_weight,
    value_weight,
    key_cotangent,
    value_cotangent,
    layer_map,
    layer_counts,
):
    yh, z, c = lax.axis_index("yh"), lax.axis_index("z"), lax.axis_index("c")
    x, yl = lax.axis_index("x"), lax.axis_index("yl")
    slab_count, tokens, slab_width = teacher_slabs.shape
    layers = layer_map.shape[0]
    columns = proj_weight.shape[2]
    full_width = columns * X * YL
    slot_count = child_hidden.shape[0]
    quarter = tokens // QUARTERS

    swap = [(0, 1), (1, 0)]
    side = ("yh", "yl")
    ring = YH * YL
    up = [(i, (i + 1) % ring) for i in range(ring)]
    down = [(i, (i - 1) % ring) for i in range(ring)]
    half_rows = proj_weight.shape[1] // 2
    w_sib = lax.ppermute(proj_weight, "c", swap)
    place = jnp.stack([2 * yh + c, 2 * yh + 1 - c, 2 * (1 - yh) + c, 2 * (1 - yh) + 1 - c]).astype(jnp.int32)

    is_child = yh == 1
    first_hidden = child_hidden[0].astype(jnp.float32)
    norm_scale = norm_gain[0]
    contract_last = (((1,), (1,)), ((), ()))
    delta_norm = lax.dot_general(
        key_cotangent[0], key_weight[0], contract_last, preferred_element_type=jnp.float32
    )
    delta_norm = delta_norm + lax.dot_general(
        value_cotangent[0], value_weight[0], contract_last, preferred_element_type=jnp.float32
    )
    sums = jnp.stack(
        [
            jnp.sum(first_hidden * first_hidden, axis=1),
            jnp.sum(first_hidden * norm_scale * delta_norm, axis=1),
        ]
    )
    sums = sums + lax.ppermute(sums, "x", [(i, i ^ 1) for i in range(X)])
    sums = sums + lax.ppermute(sums, "x", [(i, i ^ 2) for i in range(X)])
    sums = sums + lax.ppermute(sums, "yl", swap)
    sent = lax.ppermute(arrange(teacher_slabs, 1), side, [(0, 3), (1, 2)])
    arranged = jnp.where(yh == 0, arrange(teacher_slabs, 0), sent)
    arranged, w_sib, sums, weight_rows = lax.optimization_barrier((arranged, w_sib, sums, proj_weight))
    w_far_a = lax.ppermute(lax.ppermute(weight_rows[:, :half_rows], side, up), side, up)
    w_far_b = lax.ppermute(lax.ppermute(weight_rows[:, half_rows:], side, down), side, down)
    received = lax.all_to_all(arranged, ("z", "c"), split_axis=0, concat_axis=0, tiled=True)
    received = received.reshape(Z * C * slab_count, YH, quarter, LANES)

    squares, inner_sum = sums[0], sums[1]
    inverse_rms = lax.rsqrt(squares / full_width + EPSILON)[:, None]
    normed = (first_hidden * inverse_rms * norm_scale).astype(jnp.bfloat16)
    contract_rows = (((0,), (0,)), ((), ()))
    key_grad = lax.dot_general(
        normed, key_cotangent[0], contract_rows, preferred_element_type=jnp.float32
    ).astype(jnp.bfloat16)
    value_grad = lax.dot_general(
        normed, value_cotangent[0], contract_rows, preferred_element_type=jnp.float32
    ).astype(jnp.bfloat16)
    gain_grad = jnp.sum(first_hidden * inverse_rms * delta_norm, axis=0)
    layer_grad = (
        inverse_rms * norm_scale * delta_norm
        - first_hidden * inverse_rms**3 * inner_sum[:, None] / full_width
    )
    layer_grad = jnp.where(is_child, layer_grad, 0.0)
    key_grad = jnp.where(is_child, key_grad, jnp.zeros_like(key_grad))
    value_grad = jnp.where(is_child, value_grad, jnp.zeros_like(value_grad))
    gain_grad = jnp.where(is_child, gain_grad, 0.0)
    first_blocks, rest_blocks = (
        jnp.stack([(x + step) % X * YL + (yl + yh + other) % YL for step, other in places]).astype(jnp.int32)
        for places in (FIRST, REST)
    )
    prefix_end = jnp.cumsum(layer_counts)
    prefix_start = prefix_end - layer_counts
    slot_layer = jnp.clip(prefix_start[:, None] + jnp.arange(slot_count)[None, :], 0, layers - 1)
    slot_layer = slot_layer.reshape(Z, C, slot_count)[(z + jnp.array(DISTANCES)) % Z]
    slot_layer = jnp.where(c == 0, slot_layer[:, ::-1], slot_layer).reshape(-1).astype(jnp.int32)
    own_count = jnp.where(is_child, layer_counts[2 * z + c], 0)
    received, key_grad, value_grad, gain_grad, layer_grad, slot_layer, own_count = lax.optimization_barrier(
        (received, key_grad, value_grad, gain_grad, layer_grad, slot_layer, own_count)
    )
    first_features, rest_features = gather_tensor(*pick(layer_map, received))
    w_far_a, w_far_b, _ = lax.optimization_barrier((w_far_a, w_far_b, first_features[3]))
    weights = (proj_weight, w_sib, w_far_a, w_far_b, lax.ppermute(w_far_a, "c", swap), lax.ppermute(w_far_b, "c", swap))
    partial = project_first(place, first_blocks, first_features, weights)
    chunks = project_rest(place, rest_blocks, slot_layer, partial, rest_features, weights)
    given, kept = reduce_z(chunks)
    across = lax.ppermute(given, "c", swap)
    teacher = lax.ppermute(kept, "yh", [(0, 1)])
    teacher_across = lax.ppermute(given, ("yh", "c"), [(0, 3), (1, 2)])
    hidden_grad = finish(c, own_count, child_hidden, layer_grad, (kept, teacher, across, teacher_across))
    return (hidden_grad, key_grad[None], value_grad[None], gain_grad[None])


def solution(mesh):
    fine = Mesh(mesh.devices.reshape(YH, Z, C, X, YL), (*SEGMENT, *TENSOR))
    placed = (
        P(SEGMENT, None, TENSOR),
        P(None, SEGMENT, TENSOR),
        P(SEGMENT, None, TENSOR),
        P(SEGMENT, TENSOR),
        P(SEGMENT, TENSOR, None),
        P(SEGMENT, TENSOR, None),
        P(SEGMENT, None, None),
        P(SEGMENT, None, None),
        P(),
        P(),
    )
    return jax.shard_map(
        body,
        mesh=fine,
        in_specs=placed,
        out_specs=(
            P(SEGMENT, None, TENSOR),
            P(SEGMENT, TENSOR, None),
            P(SEGMENT, TENSOR, None),
            P(SEGMENT, TENSOR),
        ),
        check_vma=False,
    )
```

```python
import jax
import jax.numpy as jnp
from jax import lax
from jax.experimental import pallas as pl
from jax.experimental.pallas import tpu as pltpu
from jax.sharding import Mesh, PartitionSpec as P

EPSILON = 1e-05
MIB = 1 << 20

SEGMENT = ("yh", "z", "c")
TENSOR = ("x", "yl")
YH, Z, C, X, YL = 2, 8, 2, 4, 2
QUARTERS = YH * C
LANES = 128


def arrange_kernel(slabs, out):
    _, width, _ = slabs.shape
    tokens = width // C
    for c in range(C):
        for z in range(Z):
            for h in range(YH):
                lane = (h * Z + z) * LANES
                out[z * C + c, h * tokens : (h + 1) * tokens, :] = slabs[
                    0, c * tokens : (c + 1) * tokens, lane : lane + LANES
                ]


def arrange(teacher_slabs, section):
    slab_count, tokens, width = teacher_slabs.shape
    rows = YH * (tokens // QUARTERS)
    return pl.pallas_call(
        arrange_kernel,
        grid=(slab_count,),
        out_shape=jax.ShapeDtypeStruct((Z * C, slab_count * rows, LANES), teacher_slabs.dtype),
        in_specs=[pl.BlockSpec((1, tokens // YH, width), lambda i: (i, section, 0))],
        out_specs=pl.BlockSpec((Z * C, rows, LANES), lambda i: (0, i, 0)),
        cost_estimate=pl.CostEstimate(flops=0, bytes_accessed=1600000, transcendentals=0),
        name="arrange",
    )(teacher_slabs)


def pick_kernel(layer_map, received, picked, low, high):
    half = low.shape[0]

    def step(layer, carry):
        value = received[layer_map[layer]]
        picked[layer] = value
        low[layer] = value
        value = received[layer_map[half + layer]]
        picked[half + layer] = value
        high[layer] = value
        return carry

    lax.fori_loop(0, half, step, 0)


def pick(layer_map, received):
    layers = layer_map.shape[0]
    shapes = [(count, *received.shape[1:]) for count in (layers, layers // 2, layers // 2)]
    return pl.pallas_call(
        pick_kernel,
        out_shape=[jax.ShapeDtypeStruct(shape, received.dtype) for shape in shapes],
        in_specs=[
            pl.BlockSpec(memory_space=pltpu.SMEM),
            pl.BlockSpec(memory_space=pltpu.VMEM),
        ],
        out_specs=[pl.BlockSpec(memory_space=pltpu.VMEM)] * len(shapes),
        cost_estimate=pl.CostEstimate(flops=0, bytes_accessed=1300000, transcendentals=0),
        name="pick_layers",
    )(layer_map, received)


DISTANCES = (4, 3, -3, 2, -2, 1, -1, 0)
FIRST = ((0, 0), (1, 0), (3, 0), (0, 1))
REST = ((2, 0), (1, 1), (2, 1), (3, 1))
GROUPS = 4
WEIGHTS = 6


def load_weight(place, blocks, weights, weight, sem):
    piece = weights[0].shape[1]
    half = piece // 2
    copies = []
    for index in range(sem.shape[0]):
        for source, ref in enumerate(weights):
            part = source if source < 2 else 2 + (source - 2) // 2
            shift = half if source in (3, 5) else 0
            row = pl.multiple_of(index * QUARTERS * piece + place[part] * piece + shift, half)
            target = weight.at[pl.ds(row, ref.shape[1])]
            copies.append(pltpu.make_async_copy(ref.at[blocks[index]], target, sem.at[index, source]))
    for copy in copies:
        copy.start()
    return copies


def load_features(features, held, sem):
    copies = [
        pltpu.make_async_copy(ref, slot, sem.at[index]) for index, (ref, slot) in enumerate(zip(features, held))
    ]
    for copy in copies:
        copy.start()
    return copies


def left_rows(refs, firsts, group):
    _, halves, tokens, lanes = refs[0].shape
    return jnp.concatenate(
        [
            ref[pl.ds(first, group), h].reshape(group * tokens, lanes)
            for ref, first in zip(refs, firsts)
            for h in range(halves)
        ],
        axis=1,
    )


def project_first_kernel(place, blocks, *refs):
    count = len(FIRST) + 2
    features, refs = refs[:count], refs[count:]
    weights, (out, weight, *held, feature_sem, weight_sem) = refs[:WEIGHTS], refs[WEIGHTS:]
    copies = load_weight(place, blocks, weights, weight, weight_sem) + load_features(features, held, feature_sem)
    for copy in copies:
        copy.wait()
    own, up_a, up_b, down_a, down_b, row = held
    group = own.shape[0] // GROUPS
    for number in range(GROUPS):
        first = number * group
        side = number // (GROUPS // 2)
        offset = (number - side * (GROUPS // 2)) * group
        refs = (own, (up_a, up_b)[side], (down_a, down_b)[side], row)
        left = left_rows(refs, (first, offset, offset, first), group)
        out[number] = jnp.dot(left, weight[...], preferred_element_type=jnp.float32).astype(out.dtype)


def project_rest_kernel(place, blocks, slot_layer, partial, *refs):
    count = len(REST) + 2
    features, refs = refs[:count], refs[count:]
    weights, refs = refs[:WEIGHTS], refs[WEIGHTS:]
    outs, refs = refs[: C * len(DISTANCES)], refs[C * len(DISTANCES) :]
    weight, before, product, *held, feature_sem, weight_sem, before_sem = refs
    copies = load_weight(place, blocks, weights, weight, weight_sem) + load_features(features, held, feature_sem)
    befores = [
        pltpu.make_async_copy(partial.at[number], before.at[number], before_sem.at[number]) for number in range(GROUPS)
    ]
    for copy in befores:
        copy.start()
    for copy in copies:
        copy.wait()
    layers, halves, tokens, lanes = features[2].shape
    group = layers // GROUPS
    near_a, near_b, row_1, row_2a, row_2b, row_3 = held
    for number in range(GROUPS):
        first = number * group
        side = number // (GROUPS // 2)
        offset = (number - side * (GROUPS // 2)) * group
        refs = ((near_a, near_b)[side], row_1, (row_2a, row_2b)[side], row_3)
        left = left_rows(refs, (offset, first, offset, first), group)
        value = jnp.dot(left, weight[...], preferred_element_type=jnp.float32)
        befores[number].wait()
        value = (value + before[number].astype(jnp.float32)).astype(product.dtype)
        product[pl.ds(first, group)] = value.reshape(group, tokens, value.shape[1])
    slots = outs[0].shape[0]
    for index, out in enumerate(outs):
        for slot in range(slots):
            out[slot] = product[slot_layer[index * slots + slot]]


def project_first(place, blocks, features, weights):
    layers, halves, tokens, lanes = features[0].shape
    columns = weights[0].shape[2]
    depth = len(FIRST) * halves * lanes
    shape = (GROUPS, layers * tokens // GROUPS, columns)
    smem, anywhere = pl.BlockSpec(memory_space=pltpu.SMEM), pl.BlockSpec(memory_space=pltpu.HBM)
    return pl.pallas_call(
        project_first_kernel,
        out_shape=jax.ShapeDtypeStruct(shape, jnp.bfloat16),
        in_specs=[smem] * 2 + [anywhere] * (len(features) + len(weights)),
        out_specs=pl.BlockSpec(memory_space=pltpu.VMEM),
        scratch_shapes=[
            pltpu.VMEM((depth, columns), jnp.bfloat16),
            *[pltpu.VMEM(feature.shape, feature.dtype) for feature in features],
            pltpu.SemaphoreType.DMA((len(features),)),
            pltpu.SemaphoreType.DMA((len(FIRST), WEIGHTS)),
        ],
        compiler_params=pltpu.CompilerParams(vmem_limit_bytes=40 * MIB),
        cost_estimate=pl.CostEstimate(
            flops=2 * layers * tokens * depth * columns, bytes_accessed=8 * MIB, transcendentals=0
        ),
        name="project_first",
    )(place, blocks, *features, *weights)


def project_rest(place, blocks, slot_layer, partial, features, weights):
    layers, halves, tokens, lanes = features[2].shape
    columns = weights[0].shape[2]
    depth = len(REST) * halves * lanes
    slots = slot_layer.shape[0] // (len(DISTANCES) * C)
    smem, vmem = pl.BlockSpec(memory_space=pltpu.SMEM), pl.BlockSpec(memory_space=pltpu.VMEM)
    shapes = [(slots, tokens, columns)] * (C * len(DISTANCES))
    return pl.pallas_call(
        project_rest_kernel,
        out_shape=[jax.ShapeDtypeStruct(shape, jnp.bfloat16) for shape in shapes],
        in_specs=[smem] * 3 + [pl.BlockSpec(memory_space=pltpu.HBM)] * (1 + len(features) + len(weights)),
        out_specs=[vmem] * len(shapes),
        scratch_shapes=[
            pltpu.VMEM((depth, columns), jnp.bfloat16),
            pltpu.VMEM(partial.shape, partial.dtype),
            pltpu.VMEM((layers, tokens, columns), jnp.bfloat16),
            *[pltpu.VMEM(feature.shape, feature.dtype) for feature in features],
            pltpu.SemaphoreType.DMA((len(features),)),
            pltpu.SemaphoreType.DMA((len(REST), WEIGHTS)),
            pltpu.SemaphoreType.DMA((GROUPS,)),
        ],
        compiler_params=pltpu.CompilerParams(vmem_limit_bytes=62 * MIB),
        cost_estimate=pl.CostEstimate(
            flops=2 * layers * tokens * depth * columns, bytes_accessed=11 * MIB, transcendentals=0
        ),
        name="project_rest",
    )(place, blocks, slot_layer, partial, *features, *weights)


def reduce_z(chunks):
    up = [(i, (i + 1) % Z) for i in range(Z)]
    down = [(i, (i - 1) % Z) for i in range(Z)]
    given = dict(zip(DISTANCES, chunks[0::2]))
    kept = dict(zip(DISTANCES, chunks[1::2]))

    def add(*terms):
        return sum(term.astype(jnp.float32) for term in terms).astype(terms[0].dtype)

    given_up = lax.ppermute(given[4], "z", up)
    kept_down = lax.ppermute(kept[4], "z", down)
    given_down = lax.ppermute(given[-3], "z", down)
    kept_up = lax.ppermute(kept[3], "z", up)
    for distance in (3, 2, 1):
        given_up = lax.ppermute(add(given[distance], given_up), "z", up)
        if distance < 3:
            given_down = lax.ppermute(add(given[-distance], given_down), "z", down)
        kept_down = lax.ppermute(add(kept[-distance], kept_down), "z", down)
        if distance < 3:
            kept_up = lax.ppermute(add(kept[distance], kept_up), "z", up)
    given_sum = add(given[0], given_up, given_down)
    return given_sum, add(kept[0], kept_up, kept_down)


def finish_kernel(state, hidden, layer_grad, teacher_across, across, teacher, near, out):
    core, count = state[0], state[1]
    slot = pl.program_id(0)
    quarter = near.shape[1]
    quarters = ((C + core, near), (C + 1 - core, across), (core, teacher), (1 - core, teacher_across))
    for index, ref in quarters:
        rows = pl.ds(pl.multiple_of(index * quarter, quarter), quarter)
        value = hidden[0, rows, :].astype(jnp.float32) - ref[0].astype(jnp.float32)
        value = jnp.where(slot < count, value, 0.0)
        value = value + jnp.where(slot == 0, layer_grad[rows, :], 0.0)
        out[0, rows, :] = value.astype(out.dtype)


def finish(c, own_count, hidden, layer_grad, pieces):
    slots, tokens, columns = hidden.shape
    whole = pl.BlockSpec((1, tokens, columns), lambda i: (i, 0, 0))
    piece = pl.BlockSpec((1, tokens // QUARTERS, columns), lambda i: (i, 0, 0))
    return pl.pallas_call(
        finish_kernel,
        grid=(slots,),
        out_shape=jax.ShapeDtypeStruct(hidden.shape, hidden.dtype),
        in_specs=[
            pl.BlockSpec(memory_space=pltpu.SMEM),
            whole,
            pl.BlockSpec((tokens, columns), lambda i: (0, 0)),
        ]
        + [piece] * len(pieces),
        out_specs=whole,
        cost_estimate=pl.CostEstimate(flops=2 * hidden.size, bytes_accessed=8 * hidden.size, transcendentals=0),
        name="finish",
    )(jnp.stack([c, own_count]).astype(jnp.int32), hidden, layer_grad, *pieces)


def gather_tensor(own, low, high):
    up = [(i, (i + 1) % X) for i in range(X)]
    down = [(i, (i - 1) % X) for i in range(X)]
    swap = [(0, 1), (1, 0)]
    f3a = lax.ppermute(low, "x", up)
    f1b = lax.ppermute(high, "x", down)
    g0 = lax.ppermute(own, "yl", swap)
    f3b = lax.ppermute(high, "x", up)
    f1a = lax.ppermute(low, "x", down)
    f2a = lax.ppermute(f3a, "x", up)
    f2b = lax.ppermute(f1b, "x", down)
    g3 = lax.ppermute(g0, "x", up)
    g1 = lax.ppermute(g0, "x", down)
    g2a = lax.ppermute(f2a, "yl", swap)
    g2b = lax.ppermute(f2b, "yl", swap)
    return (own, f1a, f1b, f3a, f3b, g0), (f2a, f2b, g1, g2a, g2b, g3)


def body(
    teacher_slabs,
    proj_weight,
    child_hidden,
    norm_gain,
    key_weight,
    value_weight,
    key_cotangent,
    value_cotangent,
    layer_map,
    layer_counts,
):
    yh, z, c = lax.axis_index("yh"), lax.axis_index("z"), lax.axis_index("c")
    x, yl = lax.axis_index("x"), lax.axis_index("yl")
    slab_count, tokens, slab_width = teacher_slabs.shape
    layers = layer_map.shape[0]
    columns = proj_weight.shape[2]
    full_width = columns * X * YL
    slot_count = child_hidden.shape[0]
    quarter = tokens // QUARTERS

    swap = [(0, 1), (1, 0)]
    side = ("yh", "yl")
    ring = YH * YL
    up = [(i, (i + 1) % ring) for i in range(ring)]
    down = [(i, (i - 1) % ring) for i in range(ring)]
    half_rows = proj_weight.shape[1] // 2
    w_sib = lax.ppermute(proj_weight, "c", swap)
    place = jnp.stack([2 * yh + c, 2 * yh + 1 - c, 2 * (1 - yh) + c, 2 * (1 - yh) + 1 - c]).astype(jnp.int32)

    is_child = yh == 1
    leaving, key_weight, value_weight = lax.optimization_barrier((arrange(teacher_slabs, 1), key_weight, value_weight))
    first_hidden = child_hidden[0].astype(jnp.float32)
    norm_scale = norm_gain[0]
    contract_last = (((1,), (1,)), ((), ()))
    delta_norm = lax.dot_general(
        key_cotangent[0], key_weight[0], contract_last, preferred_element_type=jnp.float32
    )
    delta_norm = delta_norm + lax.dot_general(
        value_cotangent[0], value_weight[0], contract_last, preferred_element_type=jnp.float32
    )
    sums = jnp.stack(
        [
            jnp.sum(first_hidden * first_hidden, axis=1),
            jnp.sum(first_hidden * norm_scale * delta_norm, axis=1),
        ]
    )
    sums = sums + lax.ppermute(sums, "x", [(i, i ^ 1) for i in range(X)])
    sums = sums + lax.ppermute(sums, "x", [(i, i ^ 2) for i in range(X)])
    sums = sums + lax.ppermute(sums, "yl", swap)
    sent = lax.ppermute(leaving, side, [(0, 3), (1, 2)])
    arranged = jnp.where(yh == 0, arrange(teacher_slabs, 0), sent)
    arranged, w_sib, sums, weight_rows = lax.optimization_barrier((arranged, w_sib, sums, proj_weight))
    w_far_a = lax.ppermute(lax.ppermute(weight_rows[:, :half_rows], side, up), side, up)
    w_far_b = lax.ppermute(lax.ppermute(weight_rows[:, half_rows:], side, down), side, down)
    received = lax.all_to_all(arranged, ("z", "c"), split_axis=0, concat_axis=0, tiled=True)
    received = received.reshape(Z * C * slab_count, YH, quarter, LANES)

    squares, inner_sum = sums[0], sums[1]
    inverse_rms = lax.rsqrt(squares / full_width + EPSILON)[:, None]
    normed = (first_hidden * inverse_rms * norm_scale).astype(jnp.bfloat16)
    contract_rows = (((0,), (0,)), ((), ()))
    key_grad = lax.dot_general(
        normed, key_cotangent[0], contract_rows, preferred_element_type=jnp.float32
    ).astype(jnp.bfloat16)
    value_grad = lax.dot_general(
        normed, value_cotangent[0], contract_rows, preferred_element_type=jnp.float32
    ).astype(jnp.bfloat16)
    gain_grad = jnp.sum(first_hidden * inverse_rms * delta_norm, axis=0)
    layer_grad = (
        inverse_rms * norm_scale * delta_norm
        - first_hidden * inverse_rms**3 * inner_sum[:, None] / full_width
    )
    layer_grad = jnp.where(is_child, layer_grad, 0.0)
    key_grad = jnp.where(is_child, key_grad, jnp.zeros_like(key_grad))
    value_grad = jnp.where(is_child, value_grad, jnp.zeros_like(value_grad))
    gain_grad = jnp.where(is_child, gain_grad, 0.0)
    received, key_grad, gain_grad, layer_grad = lax.optimization_barrier((received, key_grad, gain_grad, layer_grad))
    first_features, rest_features = gather_tensor(*pick(layer_map, received))
    w_far_a, w_far_b, _ = lax.optimization_barrier((w_far_a, w_far_b, first_features[3]))
    weights = (proj_weight, w_sib, w_far_a, w_far_b, lax.ppermute(w_far_a, "c", swap), lax.ppermute(w_far_b, "c", swap))
    first_blocks, rest_blocks = (
        jnp.stack([(x + step) % X * YL + (yl + yh + other) % YL for step, other in places]).astype(jnp.int32)
        for places in (FIRST, REST)
    )
    prefix_end = jnp.cumsum(layer_counts)
    prefix_start = prefix_end - layer_counts
    slot_layer = jnp.clip(prefix_start[:, None] + jnp.arange(slot_count)[None, :], 0, layers - 1)
    slot_layer = slot_layer.reshape(Z, C, slot_count)[(z + jnp.array(DISTANCES)) % Z]
    slot_layer = jnp.where(c == 0, slot_layer[:, ::-1], slot_layer).reshape(-1).astype(jnp.int32)
    partial = project_first(place, first_blocks, first_features, weights)
    chunks = project_rest(place, rest_blocks, slot_layer, partial, rest_features, weights)
    given, kept = reduce_z(chunks)
    across = lax.ppermute(given, "c", swap)
    teacher = lax.ppermute(kept, "yh", [(0, 1)])
    teacher_across = lax.ppermute(given, ("yh", "c"), [(0, 3), (1, 2)])
    own_count = jnp.where(is_child, layer_counts[2 * z + c], 0)
    hidden_grad = finish(c, own_count, child_hidden, layer_grad, (teacher_across, across, teacher, kept))
    return (hidden_grad, key_grad[None], value_grad[None], gain_grad[None])


def solution(mesh):
    fine = Mesh(mesh.devices.reshape(YH, Z, C, X, YL), (*SEGMENT, *TENSOR))
    placed = (
        P(SEGMENT, None, TENSOR),
        P(None, SEGMENT, TENSOR),
        P(SEGMENT, None, TENSOR),
        P(SEGMENT, TENSOR),
        P(SEGMENT, TENSOR, None),
        P(SEGMENT, TENSOR, None),
        P(SEGMENT, None, None),
        P(SEGMENT, None, None),
        P(),
        P(),
    )
    return jax.shard_map(
        body,
        mesh=fine,
        in_specs=placed,
        out_specs=(
            P(SEGMENT, None, TENSOR),
            P(SEGMENT, TENSOR, None),
            P(SEGMENT, TENSOR, None),
            P(SEGMENT, TENSOR),
        ),
        check_vma=False,
    )
```

```python
import jax
import jax.numpy as jnp
from jax import lax
from jax.experimental import pallas as pl
from jax.experimental.pallas import tpu as pltpu
from jax.sharding import Mesh, PartitionSpec as P

EPSILON = 1e-05
MIB = 1 << 20

SEGMENT = ("yh", "z", "c")
TENSOR = ("x", "yl")
YH, Z, C, X, YL = 2, 8, 2, 4, 2
QUARTERS = YH * C
LANES = 128


def arrange_kernel(slabs, out):
    slab_count, width, _ = slabs.shape
    tokens = width // C
    for c in range(C):
        for z in range(Z):
            for slab in range(slab_count):
                for h in range(YH):
                    lane = (h * Z + z) * LANES
                    row = (slab * YH + h) * tokens
                    out[z * C + c, row : row + tokens, :] = slabs[
                        slab, c * tokens : (c + 1) * tokens, lane : lane + LANES
                    ]


def arrange(teacher_slabs, section):
    slab_count, tokens, width = teacher_slabs.shape
    rows = slab_count * YH * (tokens // QUARTERS)
    shape = jax.ShapeDtypeStruct((Z * C, rows, LANES), teacher_slabs.dtype)
    return pl.pallas_call(
        arrange_kernel,
        grid=(1,),
        out_shape=shape,
        in_specs=[pl.BlockSpec((slab_count, tokens // YH, width), lambda i: (0, section, 0))],
        out_specs=pl.BlockSpec(shape.shape, lambda i: (0, 0, 0)),
        cost_estimate=pl.CostEstimate(flops=0, bytes_accessed=1600000, transcendentals=0),
        name="arrange",
    )(teacher_slabs)


def pick_kernel(layer_map, received, picked, low, high):
    half = low.shape[0]

    def step(layer, carry):
        value = received[layer_map[layer]]
        picked[layer] = value
        low[layer] = value
        value = received[layer_map[half + layer]]
        picked[half + layer] = value
        high[layer] = value
        return carry

    lax.fori_loop(0, half, step, 0)


def pick(layer_map, received):
    layers = layer_map.shape[0]
    shapes = [(count, *received.shape[1:]) for count in (layers, layers // 2, layers // 2)]
    return pl.pallas_call(
        pick_kernel,
        out_shape=[jax.ShapeDtypeStruct(shape, received.dtype) for shape in shapes],
        in_specs=[
            pl.BlockSpec(memory_space=pltpu.SMEM),
            pl.BlockSpec(memory_space=pltpu.VMEM),
        ],
        out_specs=[pl.BlockSpec(memory_space=pltpu.VMEM)] * len(shapes),
        cost_estimate=pl.CostEstimate(flops=0, bytes_accessed=1300000, transcendentals=0),
        name="pick_layers",
    )(layer_map, received)


DISTANCES = (4, 3, -3, 2, -2, 1, -1, 0)
FIRST = ((0, 0), (1, 0), (3, 0), (0, 1))
REST = ((2, 0), (1, 1), (2, 1), (3, 1))
GROUPS = 4
WEIGHTS = 6


def load_weight(place, blocks, weights, weight, sem):
    piece = weights[0].shape[1]
    half = piece // 2
    copies = []
    for index in range(sem.shape[0]):
        for source, ref in enumerate(weights):
            part = source if source < 2 else 2 + (source - 2) // 2
            shift = half if source in (3, 5) else 0
            row = pl.multiple_of(index * QUARTERS * piece + place[part] * piece + shift, half)
            target = weight.at[pl.ds(row, ref.shape[1])]
            copies.append(pltpu.make_async_copy(ref.at[blocks[index]], target, sem.at[index, source]))
    for copy in copies:
        copy.start()
    return copies


def load_features(features, held, sem):
    copies = [
        pltpu.make_async_copy(ref, slot, sem.at[index]) for index, (ref, slot) in enumerate(zip(features, held))
    ]
    for copy in copies:
        copy.start()
    return copies


def left_rows(refs, firsts, group):
    _, halves, tokens, lanes = refs[0].shape
    return jnp.concatenate(
        [
            ref[pl.ds(first, group), h].reshape(group * tokens, lanes)
            for ref, first in zip(refs, firsts)
            for h in range(halves)
        ],
        axis=1,
    )


def project_first_kernel(place, blocks, *refs):
    count = len(FIRST) + 2
    features, refs = refs[:count], refs[count:]
    weights, (out, weight, *held, feature_sem, weight_sem) = refs[:WEIGHTS], refs[WEIGHTS:]
    copies = load_weight(place, blocks, weights, weight, weight_sem) + load_features(features, held, feature_sem)
    for copy in copies:
        copy.wait()
    own, up_a, up_b, down_a, down_b, row = held
    group = own.shape[0] // GROUPS
    for number in range(GROUPS):
        first = number * group
        side = number // (GROUPS // 2)
        offset = (number - side * (GROUPS // 2)) * group
        refs = (own, (up_a, up_b)[side], (down_a, down_b)[side], row)
        left = left_rows(refs, (first, offset, offset, first), group)
        out[number] = jnp.dot(left, weight[...], preferred_element_type=jnp.float32).astype(out.dtype)


def project_rest_kernel(place, blocks, slot_layer, partial, *refs):
    count = len(REST) + 2
    features, refs = refs[:count], refs[count:]
    weights, refs = refs[:WEIGHTS], refs[WEIGHTS:]
    outs, refs = refs[: C * len(DISTANCES)], refs[C * len(DISTANCES) :]
    weight, before, product, *held, feature_sem, weight_sem, before_sem = refs
    copies = load_weight(place, blocks, weights, weight, weight_sem) + load_features(features, held, feature_sem)
    befores = [
        pltpu.make_async_copy(partial.at[number], before.at[number], before_sem.at[number]) for number in range(GROUPS)
    ]
    for copy in befores:
        copy.start()
    for copy in copies:
        copy.wait()
    layers, halves, tokens, lanes = features[2].shape
    group = layers // GROUPS
    near_a, near_b, row_1, row_2a, row_2b, row_3 = held
    for number in range(GROUPS):
        first = number * group
        side = number // (GROUPS // 2)
        offset = (number - side * (GROUPS // 2)) * group
        refs = ((near_a, near_b)[side], row_1, (row_2a, row_2b)[side], row_3)
        left = left_rows(refs, (offset, first, offset, first), group)
        value = jnp.dot(left, weight[...], preferred_element_type=jnp.float32)
        befores[number].wait()
        value = (value + before[number].astype(jnp.float32)).astype(product.dtype)
        product[pl.ds(first, group)] = value.reshape(group, tokens, value.shape[1])
    slots = outs[0].shape[0]
    for index, out in enumerate(outs):
        for slot in range(slots):
            out[slot] = product[slot_layer[index * slots + slot]]


def project_first(place, blocks, features, weights):
    layers, halves, tokens, lanes = features[0].shape
    columns = weights[0].shape[2]
    depth = len(FIRST) * halves * lanes
    shape = (GROUPS, layers * tokens // GROUPS, columns)
    smem, anywhere = pl.BlockSpec(memory_space=pltpu.SMEM), pl.BlockSpec(memory_space=pltpu.HBM)
    return pl.pallas_call(
        project_first_kernel,
        out_shape=jax.ShapeDtypeStruct(shape, jnp.bfloat16),
        in_specs=[smem] * 2 + [anywhere] * (len(features) + len(weights)),
        out_specs=pl.BlockSpec(memory_space=pltpu.VMEM),
        scratch_shapes=[
            pltpu.VMEM((depth, columns), jnp.bfloat16),
            *[pltpu.VMEM(feature.shape, feature.dtype) for feature in features],
            pltpu.SemaphoreType.DMA((len(features),)),
            pltpu.SemaphoreType.DMA((len(FIRST), WEIGHTS)),
        ],
        compiler_params=pltpu.CompilerParams(vmem_limit_bytes=40 * MIB),
        cost_estimate=pl.CostEstimate(
            flops=2 * layers * tokens * depth * columns, bytes_accessed=8 * MIB, transcendentals=0
        ),
        name="project_first",
    )(place, blocks, *features, *weights)


def project_rest(place, blocks, slot_layer, partial, features, weights):
    layers, halves, tokens, lanes = features[2].shape
    columns = weights[0].shape[2]
    depth = len(REST) * halves * lanes
    slots = slot_layer.shape[0] // (len(DISTANCES) * C)
    smem, vmem = pl.BlockSpec(memory_space=pltpu.SMEM), pl.BlockSpec(memory_space=pltpu.VMEM)
    shapes = [(slots, tokens, columns)] * (C * len(DISTANCES))
    return pl.pallas_call(
        project_rest_kernel,
        out_shape=[jax.ShapeDtypeStruct(shape, jnp.bfloat16) for shape in shapes],
        in_specs=[smem] * 3 + [pl.BlockSpec(memory_space=pltpu.HBM)] * (1 + len(features) + len(weights)),
        out_specs=[vmem] * len(shapes),
        scratch_shapes=[
            pltpu.VMEM((depth, columns), jnp.bfloat16),
            pltpu.VMEM(partial.shape, partial.dtype),
            pltpu.VMEM((layers, tokens, columns), jnp.bfloat16),
            *[pltpu.VMEM(feature.shape, feature.dtype) for feature in features],
            pltpu.SemaphoreType.DMA((len(features),)),
            pltpu.SemaphoreType.DMA((len(REST), WEIGHTS)),
            pltpu.SemaphoreType.DMA((GROUPS,)),
        ],
        compiler_params=pltpu.CompilerParams(vmem_limit_bytes=62 * MIB),
        cost_estimate=pl.CostEstimate(
            flops=2 * layers * tokens * depth * columns, bytes_accessed=11 * MIB, transcendentals=0
        ),
        name="project_rest",
    )(place, blocks, slot_layer, partial, *features, *weights)


def reduce_z(chunks):
    up = [(i, (i + 1) % Z) for i in range(Z)]
    down = [(i, (i - 1) % Z) for i in range(Z)]
    given = dict(zip(DISTANCES, chunks[0::2]))
    kept = dict(zip(DISTANCES, chunks[1::2]))

    def add(*terms):
        return sum(term.astype(jnp.float32) for term in terms).astype(terms[0].dtype)

    given_up = lax.ppermute(given[4], "z", up)
    kept_down = lax.ppermute(kept[4], "z", down)
    given_down = lax.ppermute(given[-3], "z", down)
    kept_up = lax.ppermute(kept[3], "z", up)
    for distance in (3, 2, 1):
        given_up = lax.ppermute(add(given[distance], given_up), "z", up)
        if distance < 3:
            given_down = lax.ppermute(add(given[-distance], given_down), "z", down)
        kept_down = lax.ppermute(add(kept[-distance], kept_down), "z", down)
        if distance < 3:
            kept_up = lax.ppermute(add(kept[distance], kept_up), "z", up)
    return add(given[0], given_up, given_down), add(kept[0], kept_up, kept_down)


def finish_kernel(state, hidden, layer_grad, near, teacher, across, teacher_across, out):
    core, count = state[0], state[1]
    slots, quarter, _ = near.shape
    quarters = ((C + core, near), (C + 1 - core, across), (core, teacher), (1 - core, teacher_across))
    for index, ref in quarters:
        rows = pl.ds(pl.multiple_of(index * quarter, quarter), quarter)
        for slot in range(slots):
            value = hidden[slot, rows, :].astype(jnp.float32) - ref[slot].astype(jnp.float32)
            value = jnp.where(slot < count, value, 0.0)
            if slot == 0:
                value = value + layer_grad[rows, :]
            out[slot, rows, :] = value.astype(out.dtype)


def finish(c, own_count, hidden, layer_grad, pieces):
    vmem = pl.BlockSpec(memory_space=pltpu.VMEM)
    return pl.pallas_call(
        finish_kernel,
        out_shape=jax.ShapeDtypeStruct(hidden.shape, hidden.dtype),
        in_specs=[pl.BlockSpec(memory_space=pltpu.SMEM)] + [vmem] * 6,
        out_specs=vmem,
        cost_estimate=pl.CostEstimate(flops=2 * hidden.size, bytes_accessed=8 * hidden.size, transcendentals=0),
        name="finish",
    )(jnp.stack([c, own_count]).astype(jnp.int32), hidden, layer_grad, *pieces)


def gather_tensor(own, low, high, far):
    up = [(i, (i + 1) % X) for i in range(X)]
    down = [(i, (i - 1) % X) for i in range(X)]
    swap = [(0, 1), (1, 0)]
    f3a = lax.ppermute(low, "x", up)
    f1b = lax.ppermute(high, "x", down)
    g0 = lax.ppermute(own, "yl", swap)
    low, high, *far = lax.optimization_barrier((low, high, *far))
    f3b = lax.ppermute(high, "x", up)
    f1a = lax.ppermute(low, "x", down)
    f2a = lax.ppermute(f3a, "x", up)
    f2b = lax.ppermute(f1b, "x", down)
    g3 = lax.ppermute(g0, "x", up)
    g1 = lax.ppermute(g0, "x", down)
    g2a = lax.ppermute(f2a, "yl", swap)
    g2b = lax.ppermute(f2b, "yl", swap)
    *far, _ = lax.optimization_barrier((*far, f3a))
    return (own, f1a, f1b, f3a, f3b, g0), (f2a, f2b, g1, g2a, g2b, g3), far


def body(
    teacher_slabs,
    proj_weight,
    child_hidden,
    norm_gain,
    key_weight,
    value_weight,
    key_cotangent,
    value_cotangent,
    layer_map,
    layer_counts,
):
    yh, z, c = lax.axis_index("yh"), lax.axis_index("z"), lax.axis_index("c")
    x, yl = lax.axis_index("x"), lax.axis_index("yl")
    slab_count, tokens, slab_width = teacher_slabs.shape
    layers = layer_map.shape[0]
    columns = proj_weight.shape[2]
    full_width = columns * X * YL
    slot_count = child_hidden.shape[0]
    quarter = tokens // QUARTERS

    swap = [(0, 1), (1, 0)]
    side = ("yh", "yl")
    ring = YH * YL
    up = [(i, (i + 1) % ring) for i in range(ring)]
    down = [(i, (i - 1) % ring) for i in range(ring)]
    half_rows = proj_weight.shape[1] // 2
    w_sib = lax.ppermute(proj_weight, "c", swap)
    place = jnp.stack([2 * yh + c, 2 * yh + 1 - c, 2 * (1 - yh) + c, 2 * (1 - yh) + 1 - c]).astype(jnp.int32)

    is_child = yh == 1
    first_hidden = child_hidden[0].astype(jnp.float32)
    norm_scale = norm_gain[0]
    contract_last = (((1,), (1,)), ((), ()))
    delta_norm = lax.dot_general(
        key_cotangent[0], key_weight[0], contract_last, preferred_element_type=jnp.float32
    )
    delta_norm = delta_norm + lax.dot_general(
        value_cotangent[0], value_weight[0], contract_last, preferred_element_type=jnp.float32
    )
    sums = jnp.stack(
        [
            jnp.sum(first_hidden * first_hidden, axis=1),
            jnp.sum(first_hidden * norm_scale * delta_norm, axis=1),
        ]
    )
    sums = sums + lax.ppermute(sums, "x", [(i, i ^ 1) for i in range(X)])
    sums = sums + lax.ppermute(sums, "x", [(i, i ^ 2) for i in range(X)])
    sums = sums + lax.ppermute(sums, "yl", swap)
    sent = lax.ppermute(arrange(teacher_slabs, 1), side, [(0, 3), (1, 2)])
    arranged = jnp.where(yh == 0, arrange(teacher_slabs, 0), sent)
    arranged, w_sib, sums, weight_rows = lax.optimization_barrier((arranged, w_sib, sums, proj_weight))
    w_mid_a = lax.ppermute(weight_rows[:, :half_rows], side, up)
    w_mid_b = lax.ppermute(weight_rows[:, half_rows:], side, down)
    received = lax.all_to_all(arranged, ("z", "c"), split_axis=0, concat_axis=0, tiled=True)
    received = received.reshape(Z * C * slab_count, YH, quarter, LANES)
    w_far_a, w_far_b = lax.ppermute(w_mid_a, side, up), lax.ppermute(w_mid_b, side, down)
    received, _, _ = lax.optimization_barrier((received, w_mid_a, w_mid_b))

    first_features, rest_features, (w_far_a, w_far_b) = gather_tensor(*pick(layer_map, received), (w_far_a, w_far_b))
    weights = (proj_weight, w_sib, w_far_a, w_far_b, lax.ppermute(w_far_a, "c", swap), lax.ppermute(w_far_b, "c", swap))
    squares, inner_sum = sums[0], sums[1]
    inverse_rms = lax.rsqrt(squares / full_width + EPSILON)[:, None]
    normed = (first_hidden * inverse_rms * norm_scale).astype(jnp.bfloat16)
    contract_rows = (((0,), (0,)), ((), ()))
    key_grad = lax.dot_general(
        normed, key_cotangent[0], contract_rows, preferred_element_type=jnp.float32
    ).astype(jnp.bfloat16)
    value_grad = lax.dot_general(
        normed, value_cotangent[0], contract_rows, preferred_element_type=jnp.float32
    ).astype(jnp.bfloat16)
    gain_grad = jnp.sum(first_hidden * inverse_rms * delta_norm, axis=0)
    layer_grad = (
        inverse_rms * norm_scale * delta_norm
        - first_hidden * inverse_rms**3 * inner_sum[:, None] / full_width
    )
    layer_grad = jnp.where(is_child, layer_grad, 0.0)
    first_blocks, rest_blocks = (
        jnp.stack([(x + step) % X * YL + (yl + yh + other) % YL for step, other in places]).astype(jnp.int32)
        for places in (FIRST, REST)
    )
    prefix_end = jnp.cumsum(layer_counts)
    prefix_start = prefix_end - layer_counts
    slot_layer = jnp.clip(prefix_start[:, None] + jnp.arange(slot_count)[None, :], 0, layers - 1)
    slot_layer = slot_layer.reshape(Z, C, slot_count)[(z + jnp.array(DISTANCES)) % Z]
    slot_layer = jnp.where(c == 0, slot_layer[:, ::-1], slot_layer).reshape(-1).astype(jnp.int32)
    partial = project_first(place, first_blocks, first_features, weights)
    chunks = project_rest(place, rest_blocks, slot_layer, partial, rest_features, weights)
    given, kept = reduce_z(chunks)
    across = lax.ppermute(given, "c", swap)
    teacher = lax.ppermute(kept, "yh", [(0, 1)])
    teacher_across = lax.ppermute(given, ("yh", "c"), [(0, 3), (1, 2)])
    own_count = jnp.where(is_child, layer_counts[2 * z + c], 0)
    hidden_grad = finish(c, own_count, child_hidden, layer_grad, (kept, teacher, across, teacher_across))
    key_grad = jnp.where(is_child, key_grad, jnp.zeros_like(key_grad))
    value_grad = jnp.where(is_child, value_grad, jnp.zeros_like(value_grad))
    gain_grad = jnp.where(is_child, gain_grad, 0.0)
    return (hidden_grad, key_grad[None], value_grad[None], gain_grad[None])


def solution(mesh):
    fine = Mesh(mesh.devices.reshape(YH, Z, C, X, YL), (*SEGMENT, *TENSOR))
    placed = (
        P(SEGMENT, None, TENSOR),
        P(None, SEGMENT, TENSOR),
        P(SEGMENT, None, TENSOR),
        P(SEGMENT, TENSOR),
        P(SEGMENT, TENSOR, None),
        P(SEGMENT, TENSOR, None),
        P(SEGMENT, None, None),
        P(SEGMENT, None, None),
        P(),
        P(),
    )
    return jax.shard_map(
        body,
        mesh=fine,
        in_specs=placed,
        out_specs=(
            P(SEGMENT, None, TENSOR),
            P(SEGMENT, TENSOR, None),
            P(SEGMENT, TENSOR, None),
            P(SEGMENT, TENSOR),
        ),
        check_vma=False,
    )
```

```python
import jax
import jax.numpy as jnp
from jax import lax
from jax.experimental import pallas as pl
from jax.experimental.pallas import tpu as pltpu
from jax.sharding import Mesh, PartitionSpec as P

EPSILON = 1e-05
MIB = 1 << 20

SEGMENT = ("yh", "z", "c")
TENSOR = ("x", "yl")
YH, Z, C, X, YL = 2, 8, 2, 4, 2
QUARTERS = YH * C
LANES = 128


def arrange_kernel(slabs, out):
    slab_count, width, _ = slabs.shape
    tokens = width // C
    for c in range(C):
        for z in range(Z):
            for slab in range(slab_count):
                for h in range(YH):
                    lane = (h * Z + z) * LANES
                    row = (slab * YH + h) * tokens
                    out[z * C + c, row : row + tokens, :] = slabs[
                        slab, c * tokens : (c + 1) * tokens, lane : lane + LANES
                    ]


def arrange(teacher_slabs, section):
    slab_count, tokens, width = teacher_slabs.shape
    rows = slab_count * YH * (tokens // QUARTERS)
    shape = jax.ShapeDtypeStruct((Z * C, rows, LANES), teacher_slabs.dtype)
    return pl.pallas_call(
        arrange_kernel,
        grid=(1,),
        out_shape=shape,
        in_specs=[pl.BlockSpec((slab_count, tokens // YH, width), lambda i: (0, section, 0))],
        out_specs=pl.BlockSpec(shape.shape, lambda i: (0, 0, 0)),
        cost_estimate=pl.CostEstimate(flops=0, bytes_accessed=1600000, transcendentals=0),
        name="arrange",
    )(teacher_slabs)


def pick_kernel(layer_map, received, picked, low, high):
    half = low.shape[0]

    def step(layer, carry):
        value = received[layer_map[layer]]
        picked[layer] = value
        low[layer] = value
        value = received[layer_map[half + layer]]
        picked[half + layer] = value
        high[layer] = value
        return carry

    lax.fori_loop(0, half, step, 0)


def pick(layer_map, received):
    layers = layer_map.shape[0]
    shapes = [(count, *received.shape[1:]) for count in (layers, layers // 2, layers // 2)]
    return pl.pallas_call(
        pick_kernel,
        out_shape=[jax.ShapeDtypeStruct(shape, received.dtype) for shape in shapes],
        in_specs=[
            pl.BlockSpec(memory_space=pltpu.SMEM),
            pl.BlockSpec(memory_space=pltpu.VMEM),
        ],
        out_specs=[pl.BlockSpec(memory_space=pltpu.VMEM)] * len(shapes),
        cost_estimate=pl.CostEstimate(flops=0, bytes_accessed=1300000, transcendentals=0),
        name="pick_layers",
    )(layer_map, received)


DISTANCES = (4, 3, -3, 2, -2, 1, -1, 0)
FIRST = ((0, 0), (1, 0), (3, 0), (0, 1), (2, 0))
REST = ((1, 1), (2, 1), (3, 1))
GROUPS = 4
WEIGHTS = 6


def load_weight(place, blocks, weights, weight, sem):
    piece = weights[0].shape[1]
    half = piece // 2
    copies = []
    for index in range(sem.shape[0]):
        for source, ref in enumerate(weights):
            part = source if source < 2 else 2 + (source - 2) // 2
            shift = half if source in (3, 5) else 0
            row = pl.multiple_of(index * QUARTERS * piece + place[part] * piece + shift, half)
            target = weight.at[pl.ds(row, ref.shape[1])]
            copies.append(pltpu.make_async_copy(ref.at[blocks[index]], target, sem.at[index, source]))
    for copy in copies:
        copy.start()
    return copies


def load_features(features, held, sem):
    copies = [
        pltpu.make_async_copy(ref, slot, sem.at[index]) for index, (ref, slot) in enumerate(zip(features, held))
    ]
    for copy in copies:
        copy.start()
    return copies


def left_rows(refs, firsts, group):
    _, halves, tokens, lanes = refs[0].shape
    return jnp.concatenate(
        [
            ref[pl.ds(first, group), h].reshape(group * tokens, lanes)
            for ref, first in zip(refs, firsts)
            for h in range(halves)
        ],
        axis=1,
    )


def project_first_kernel(place, blocks, *refs):
    count = len(FIRST) + 3
    features, refs = refs[:count], refs[count:]
    weights, (out, weight, *held, feature_sem, weight_sem) = refs[:WEIGHTS], refs[WEIGHTS:]
    copies = load_weight(place, blocks, weights, weight, weight_sem) + load_features(features, held, feature_sem)
    for copy in copies:
        copy.wait()
    own, up_a, up_b, down_a, down_b, row, two_a, two_b = held
    group = own.shape[0] // GROUPS
    for number in range(GROUPS):
        first = number * group
        side = number // (GROUPS // 2)
        offset = (number - side * (GROUPS // 2)) * group
        refs = (own, (up_a, up_b)[side], (down_a, down_b)[side], row, (two_a, two_b)[side])
        left = left_rows(refs, (first, offset, offset, first, offset), group)
        out[number] = jnp.dot(left, weight[...], preferred_element_type=jnp.float32).astype(out.dtype)


def project_rest_kernel(place, blocks, slot_layer, partial, *refs):
    count = len(REST) + 1
    features, refs = refs[:count], refs[count:]
    weights, refs = refs[:WEIGHTS], refs[WEIGHTS:]
    outs, refs = refs[: C * len(DISTANCES)], refs[C * len(DISTANCES) :]
    weight, before, product, *held, feature_sem, weight_sem, before_sem = refs
    copies = load_weight(place, blocks, weights, weight, weight_sem) + load_features(features, held, feature_sem)
    befores = [
        pltpu.make_async_copy(partial.at[number], before.at[number], before_sem.at[number]) for number in range(GROUPS)
    ]
    for copy in befores:
        copy.start()
    for copy in copies:
        copy.wait()
    layers, halves, tokens, lanes = features[0].shape
    group = layers // GROUPS
    row_1, row_2a, row_2b, row_3 = held
    for number in range(GROUPS):
        first = number * group
        side = number // (GROUPS // 2)
        offset = (number - side * (GROUPS // 2)) * group
        refs = (row_1, (row_2a, row_2b)[side], row_3)
        left = left_rows(refs, (first, offset, first), group)
        value = jnp.dot(left, weight[...], preferred_element_type=jnp.float32)
        befores[number].wait()
        value = (value + before[number].astype(jnp.float32)).astype(product.dtype)
        product[pl.ds(first, group)] = value.reshape(group, tokens, value.shape[1])
    slots = outs[0].shape[0]
    for index, out in enumerate(outs):
        for slot in range(slots):
            out[slot] = product[slot_layer[index * slots + slot]]


def project_first(place, blocks, features, weights):
    layers, halves, tokens, lanes = features[0].shape
    columns = weights[0].shape[2]
    depth = len(FIRST) * halves * lanes
    shape = (GROUPS, layers * tokens // GROUPS, columns)
    smem, anywhere = pl.BlockSpec(memory_space=pltpu.SMEM), pl.BlockSpec(memory_space=pltpu.HBM)
    return pl.pallas_call(
        project_first_kernel,
        out_shape=jax.ShapeDtypeStruct(shape, jnp.bfloat16),
        in_specs=[smem] * 2 + [anywhere] * (len(features) + len(weights)),
        out_specs=pl.BlockSpec(memory_space=pltpu.VMEM),
        scratch_shapes=[
            pltpu.VMEM((depth, columns), jnp.bfloat16),
            *[pltpu.VMEM(feature.shape, feature.dtype) for feature in features],
            pltpu.SemaphoreType.DMA((len(features),)),
            pltpu.SemaphoreType.DMA((len(FIRST), WEIGHTS)),
        ],
        compiler_params=pltpu.CompilerParams(vmem_limit_bytes=40 * MIB),
        cost_estimate=pl.CostEstimate(
            flops=2 * layers * tokens * depth * columns, bytes_accessed=8 * MIB, transcendentals=0
        ),
        name="project_first",
    )(place, blocks, *features, *weights)


def project_rest(place, blocks, slot_layer, partial, features, weights):
    layers, halves, tokens, lanes = features[0].shape
    columns = weights[0].shape[2]
    depth = len(REST) * halves * lanes
    slots = slot_layer.shape[0] // (len(DISTANCES) * C)
    smem, vmem = pl.BlockSpec(memory_space=pltpu.SMEM), pl.BlockSpec(memory_space=pltpu.VMEM)
    shapes = [(slots, tokens, columns)] * (C * len(DISTANCES))
    return pl.pallas_call(
        project_rest_kernel,
        out_shape=[jax.ShapeDtypeStruct(shape, jnp.bfloat16) for shape in shapes],
        in_specs=[smem] * 3 + [pl.BlockSpec(memory_space=pltpu.HBM)] * (1 + len(features) + len(weights)),
        out_specs=[vmem] * len(shapes),
        scratch_shapes=[
            pltpu.VMEM((depth, columns), jnp.bfloat16),
            pltpu.VMEM(partial.shape, partial.dtype),
            pltpu.VMEM((layers, tokens, columns), jnp.bfloat16),
            *[pltpu.VMEM(feature.shape, feature.dtype) for feature in features],
            pltpu.SemaphoreType.DMA((len(features),)),
            pltpu.SemaphoreType.DMA((len(REST), WEIGHTS)),
            pltpu.SemaphoreType.DMA((GROUPS,)),
        ],
        compiler_params=pltpu.CompilerParams(vmem_limit_bytes=62 * MIB),
        cost_estimate=pl.CostEstimate(
            flops=2 * layers * tokens * depth * columns, bytes_accessed=11 * MIB, transcendentals=0
        ),
        name="project_rest",
    )(place, blocks, slot_layer, partial, *features, *weights)


def reduce_z(chunks):
    up = [(i, (i + 1) % Z) for i in range(Z)]
    down = [(i, (i - 1) % Z) for i in range(Z)]
    given = dict(zip(DISTANCES, chunks[0::2]))
    kept = dict(zip(DISTANCES, chunks[1::2]))

    def add(*terms):
        return sum(term.astype(jnp.float32) for term in terms).astype(terms[0].dtype)

    given_up = lax.ppermute(given[4], "z", up)
    kept_down = lax.ppermute(kept[4], "z", down)
    given_down = lax.ppermute(given[-3], "z", down)
    kept_up = lax.ppermute(kept[3], "z", up)
    for distance in (3, 2, 1):
        given_up = lax.ppermute(add(given[distance], given_up), "z", up)
        if distance < 3:
            given_down = lax.ppermute(add(given[-distance], given_down), "z", down)
        kept_down = lax.ppermute(add(kept[-distance], kept_down), "z", down)
        if distance < 3:
            kept_up = lax.ppermute(add(kept[distance], kept_up), "z", up)
    return add(given[0], given_up, given_down), add(kept[0], kept_up, kept_down)


def finish_kernel(state, hidden, layer_grad, near, teacher, across, teacher_across, out):
    core, count = state[0], state[1]
    slots, quarter, _ = near.shape
    quarters = ((C + core, near), (C + 1 - core, across), (core, teacher), (1 - core, teacher_across))
    for index, ref in quarters:
        rows = pl.ds(pl.multiple_of(index * quarter, quarter), quarter)
        for slot in range(slots):
            value = hidden[slot, rows, :].astype(jnp.float32) - ref[slot].astype(jnp.float32)
            value = jnp.where(slot < count, value, 0.0)
            if slot == 0:
                value = value + layer_grad[rows, :]
            out[slot, rows, :] = value.astype(out.dtype)


def finish(c, own_count, hidden, layer_grad, pieces):
    vmem = pl.BlockSpec(memory_space=pltpu.VMEM)
    return pl.pallas_call(
        finish_kernel,
        out_shape=jax.ShapeDtypeStruct(hidden.shape, hidden.dtype),
        in_specs=[pl.BlockSpec(memory_space=pltpu.SMEM)] + [vmem] * 6,
        out_specs=vmem,
        cost_estimate=pl.CostEstimate(flops=2 * hidden.size, bytes_accessed=8 * hidden.size, transcendentals=0),
        name="finish",
    )(jnp.stack([c, own_count]).astype(jnp.int32), hidden, layer_grad, *pieces)


def gather_tensor(own, low, high):
    up = [(i, (i + 1) % X) for i in range(X)]
    down = [(i, (i - 1) % X) for i in range(X)]
    swap = [(0, 1), (1, 0)]
    f3a = lax.ppermute(low, "x", up)
    f1b = lax.ppermute(high, "x", down)
    g0 = lax.ppermute(own, "yl", swap)
    f3b = lax.ppermute(high, "x", up)
    f1a = lax.ppermute(low, "x", down)
    f2a = lax.ppermute(f3a, "x", up)
    f2b = lax.ppermute(f1b, "x", down)
    g3 = lax.ppermute(g0, "x", up)
    g1 = lax.ppermute(g0, "x", down)
    g2a = lax.ppermute(f2a, "yl", swap)
    g2b = lax.ppermute(f2b, "yl", swap)
    return (own, f1a, f1b, f3a, f3b, g0, f2a, f2b), (g1, g2a, g2b, g3)


def body(
    teacher_slabs,
    proj_weight,
    child_hidden,
    norm_gain,
    key_weight,
    value_weight,
    key_cotangent,
    value_cotangent,
    layer_map,
    layer_counts,
):
    yh, z, c = lax.axis_index("yh"), lax.axis_index("z"), lax.axis_index("c")
    x, yl = lax.axis_index("x"), lax.axis_index("yl")
    slab_count, tokens, slab_width = teacher_slabs.shape
    layers = layer_map.shape[0]
    columns = proj_weight.shape[2]
    full_width = columns * X * YL
    slot_count = child_hidden.shape[0]
    quarter = tokens // QUARTERS

    swap = [(0, 1), (1, 0)]
    side = ("yh", "yl")
    ring = YH * YL
    up = [(i, (i + 1) % ring) for i in range(ring)]
    down = [(i, (i - 1) % ring) for i in range(ring)]
    half_rows = proj_weight.shape[1] // 2
    w_sib = lax.ppermute(proj_weight, "c", swap)
    place = jnp.stack([2 * yh + c, 2 * yh + 1 - c, 2 * (1 - yh) + c, 2 * (1 - yh) + 1 - c]).astype(jnp.int32)

    is_child = yh == 1
    first_hidden = child_hidden[0].astype(jnp.float32)
    norm_scale = norm_gain[0]
    contract_last = (((1,), (1,)), ((), ()))
    delta_norm = lax.dot_general(
        key_cotangent[0], key_weight[0], contract_last, preferred_element_type=jnp.float32
    )
    delta_norm = delta_norm + lax.dot_general(
        value_cotangent[0], value_weight[0], contract_last, preferred_element_type=jnp.float32
    )
    sums = jnp.stack(
        [
            jnp.sum(first_hidden * first_hidden, axis=1),
            jnp.sum(first_hidden * norm_scale * delta_norm, axis=1),
        ]
    )
    sums = sums + lax.ppermute(sums, "x", [(i, i ^ 1) for i in range(X)])
    sums = sums + lax.ppermute(sums, "x", [(i, i ^ 2) for i in range(X)])
    sums = sums + lax.ppermute(sums, "yl", swap)
    sent = lax.ppermute(arrange(teacher_slabs, 1), side, [(0, 3), (1, 2)])
    arranged = jnp.where(yh == 0, arrange(teacher_slabs, 0), sent)
    arranged, w_sib, sums, weight_rows = lax.optimization_barrier((arranged, w_sib, sums, proj_weight))
    w_far_a = lax.ppermute(lax.ppermute(weight_rows[:, :half_rows], side, up), side, up)
    w_far_b = lax.ppermute(lax.ppermute(weight_rows[:, half_rows:], side, down), side, down)
    received = lax.all_to_all(arranged, ("z", "c"), split_axis=0, concat_axis=0, tiled=True)
    received = received.reshape(Z * C * slab_count, YH, quarter, LANES)

    first_features, rest_features = gather_tensor(*pick(layer_map, received))
    w_far_a, w_far_b, _ = lax.optimization_barrier((w_far_a, w_far_b, first_features[3]))
    weights = (proj_weight, w_sib, w_far_a, w_far_b, lax.ppermute(w_far_a, "c", swap), lax.ppermute(w_far_b, "c", swap))
    squares, inner_sum = sums[0], sums[1]
    inverse_rms = lax.rsqrt(squares / full_width + EPSILON)[:, None]
    normed = (first_hidden * inverse_rms * norm_scale).astype(jnp.bfloat16)
    contract_rows = (((0,), (0,)), ((), ()))
    key_grad = lax.dot_general(
        normed, key_cotangent[0], contract_rows, preferred_element_type=jnp.float32
    ).astype(jnp.bfloat16)
    value_grad = lax.dot_general(
        normed, value_cotangent[0], contract_rows, preferred_element_type=jnp.float32
    ).astype(jnp.bfloat16)
    gain_grad = jnp.sum(first_hidden * inverse_rms * delta_norm, axis=0)
    layer_grad = (
        inverse_rms * norm_scale * delta_norm
        - first_hidden * inverse_rms**3 * inner_sum[:, None] / full_width
    )
    layer_grad = jnp.where(is_child, layer_grad, 0.0)
    first_blocks, rest_blocks = (
        jnp.stack([(x + step) % X * YL + (yl + yh + other) % YL for step, other in places]).astype(jnp.int32)
        for places in (FIRST, REST)
    )
    prefix_end = jnp.cumsum(layer_counts)
    prefix_start = prefix_end - layer_counts
    slot_layer = jnp.clip(prefix_start[:, None] + jnp.arange(slot_count)[None, :], 0, layers - 1)
    slot_layer = slot_layer.reshape(Z, C, slot_count)[(z + jnp.array(DISTANCES)) % Z]
    slot_layer = jnp.where(c == 0, slot_layer[:, ::-1], slot_layer).reshape(-1).astype(jnp.int32)
    partial = project_first(place, first_blocks, first_features, weights)
    chunks = project_rest(place, rest_blocks, slot_layer, partial, rest_features, weights)
    given, kept = reduce_z(chunks)
    across = lax.ppermute(given, "c", swap)
    teacher = lax.ppermute(kept, "yh", [(0, 1)])
    teacher_across = lax.ppermute(given, ("yh", "c"), [(0, 3), (1, 2)])
    own_count = jnp.where(is_child, layer_counts[2 * z + c], 0)
    hidden_grad = finish(c, own_count, child_hidden, layer_grad, (kept, teacher, across, teacher_across))
    key_grad = jnp.where(is_child, key_grad, jnp.zeros_like(key_grad))
    value_grad = jnp.where(is_child, value_grad, jnp.zeros_like(value_grad))
    gain_grad = jnp.where(is_child, gain_grad, 0.0)
    return (hidden_grad, key_grad[None], value_grad[None], gain_grad[None])


def solution(mesh):
    fine = Mesh(mesh.devices.reshape(YH, Z, C, X, YL), (*SEGMENT, *TENSOR))
    placed = (
        P(SEGMENT, None, TENSOR),
        P(None, SEGMENT, TENSOR),
        P(SEGMENT, None, TENSOR),
        P(SEGMENT, TENSOR),
        P(SEGMENT, TENSOR, None),
        P(SEGMENT, TENSOR, None),
        P(SEGMENT, None, None),
        P(SEGMENT, None, None),
        P(),
        P(),
    )
    return jax.shard_map(
        body,
        mesh=fine,
        in_specs=placed,
        out_specs=(
            P(SEGMENT, None, TENSOR),
            P(SEGMENT, TENSOR, None),
            P(SEGMENT, TENSOR, None),
            P(SEGMENT, TENSOR),
        ),
        check_vma=False,
    )
```
